32 devices in a mesh: band: 4 (over y, x), pix: 8 (over z, core).
Axes of the slice: x: 2, y: 2, z: 4, core: 2. Of those that a mesh axis runs over, the one named last changes fastest.
Arguments:
- radiance: float32 [256, 1920], P('pix', 'band'), may hold values from -6 to 6
- stem_weight: float32 [32, 1024], replicated, may hold values from -1 to 1
- band_embed: float32 [120, 1024], replicated, may hold values from -4 to 4
- norm_spectral: float32 [1024], replicated, may hold values from 0.1 to 1.9
- spec_qkv: bfloat16 [1024, 3072], replicated, as said below
- spec_out: bfloat16 [1024, 1024], replicated, may hold values from -0.1875 to 0.1875
- norm_spatial: float32 [1024], replicated, may hold values from 0.1 to 1.9
- spat_qkv: bfloat16 [1024, 3072], replicated, as said below
- spat_out: bfloat16 [1024, 1024], replicated, may hold values from -0.1875 to 0.1875
- norm_mlp: float32 [1024], replicated, may hold values from 0.1 to 1.9
- up_weight: bfloat16 [4096, 1024], P('pix'), may hold values from -0.1875 to 0.1875
- up_bias: bfloat16 [4096], P('pix'), may hold values from -3 to 3
- down_weight: bfloat16 [4096, 1024], P('pix'), may hold values from -0.09375 to 0.09375
Outputs:
- encoded: bfloat16 [256, 120, 1024], P(('pix', 'band'))
The draws below stay inside these ranges and needn't reach their ends.
Inputs may be any that keep to these rules, and one draw needn't show every extreme that they name: `spec_qkv`: columns ordered by head, then query, key, value, then head entries. `spat_qkv`: columns ordered by head, then query, key, value, then head entries.
All inputs are finite; a program needn't handle non-finite values.
Results may differ from the reference program's by a relative error of at most 0.009.
Values may be sent and summed in bfloat16 or wider, within the bound.
No kernel may reach another device: no remote copies, remote signals or barrier semaphores. Data moves between devices by JAX's collectives and lax.ppermute only.
A program may use at most 128 MiB of HBM per device.

```python
import jax
import jax.numpy as jnp
from jax import lax

D = 1024
HEADS = 16
FF = 4096
BANDS = 120
CH_TOK = 16
CHANNELS = 1920
PIXELS = 256


def projection_draw(key):
    first = jax.random.fold_in(key, 0)
    base = jnp.clip(jax.random.normal(first, (D, HEADS, 3, D // HEADS), jnp.float32), -4.0, 4.0) * D ** (-0.5)
    return base.reshape(D, 3 * D).astype(jnp.bfloat16)


def draw_spec_qkv(key, part):
    return projection_draw(jax.random.fold_in(key, 11))


def draw_spat_qkv(key, part):
    return projection_draw(jax.random.fold_in(key, 12))


def block_scale(stream_key, shape, shards, low, top_value):
    factor_of = 1.0
    for axis_at, parts in shards:
        heights = jax.random.uniform(jax.random.fold_in(jax.random.fold_in(stream_key, 6), axis_at), (parts,), jnp.float32, low / len(shards), top_value / len(shards))
        factor_of = factor_of * jnp.repeat(jnp.exp(heights), shape[axis_at] // parts).reshape((-1,) + (1,) * (len(shape) - 1 - axis_at))
    return factor_of


def normal_values(key, dims, scale, most, shards=(), kind=jnp.bfloat16):
    loudness = block_scale(key, dims, shards, -0.22, 0.18) if shards else 1.0
    drawn = jax.random.normal(key, dims, jnp.float32) * scale * loudness
    return jnp.minimum(jnp.maximum(drawn, -most), most).astype(kind)


def setup_inputs(seed: int = 0) -> dict:
    seeds = jax.random.split(jax.random.key(seed), 14)
    radiance = normal_values(seeds[0], (PIXELS, CHANNELS), 1.0, 6.0, ((0, 8), (1, 4)), jnp.float32)
    stem_weight = normal_values(seeds[1], (2 * CH_TOK, D), (2 * CH_TOK) ** -0.5, 1.0, (), jnp.float32)
    band_embed = normal_values(seeds[2], (BANDS, D), 0.5, 4.0, (), jnp.float32)
    norm_spectral = jnp.clip(1.0 + 0.18 * jax.random.normal(seeds[3], (D,), jnp.float32), 0.1, 1.9)
    spec_qkv = draw_spec_qkv(jax.random.fold_in(seeds[13], 71), 0)
    spec_out = normal_values(seeds[5], (D, D), D ** -0.5, 0.1875)
    norm_spatial = jnp.clip(1.0 + 0.18 * jax.random.normal(seeds[6], (D,), jnp.float32), 0.1, 1.9)
    spat_qkv = draw_spat_qkv(jax.random.fold_in(seeds[13], 71), 0)
    spat_out = normal_values(seeds[8], (D, D), D ** -0.5, 0.1875)
    norm_mlp = jnp.clip(1.0 + 0.18 * jax.random.normal(seeds[9], (D,), jnp.float32), 0.1, 1.9)
    up_weight = normal_values(seeds[10], (FF, D), D ** -0.5, 0.1875, ((0, 8),))
    up_bias = normal_values(seeds[11], (FF,), 0.5, 3.0, ((0, 8),))
    down_weight = normal_values(seeds[12], (FF, D), FF ** -0.5, 0.09375, ((0, 8),))
    return dict(radiance=radiance, stem_weight=stem_weight, band_embed=band_embed, norm_spectral=norm_spectral, spec_qkv=spec_qkv, spec_out=spec_out, norm_spatial=norm_spatial, spat_qkv=spat_qkv, spat_out=spat_out, norm_mlp=norm_mlp, up_weight=up_weight, up_bias=up_bias, down_weight=down_weight)


def layer_norm(values, scaling):
    values = values.astype(jnp.float32)
    average = lax.optimization_barrier(jnp.mean(values, axis=-1, keepdims=True))
    centred = values - average
    variance = lax.optimization_barrier(jnp.mean(centred * centred, axis=-1, keepdims=True))
    return centred * lax.rsqrt(variance + 1e-05) * scaling

def attend(queries, key_rows, value_rows, form_scores, form_mix):
    scale = queries.shape[-1] ** (-0.5)
    scores = jnp.einsum(form_scores, queries.astype(jnp.float32), key_rows.astype(jnp.float32)) * scale
    scores = scores - lax.optimization_barrier(jnp.max(scores, axis=-1, keepdims=True))
    weights = jnp.exp(scores)
    weights = weights / lax.optimization_barrier(jnp.sum(weights, axis=-1, keepdims=True))
    probabilities = weights.astype(jnp.bfloat16)
    mixed = jnp.einsum(form_mix, probabilities.astype(jnp.float32), value_rows.astype(jnp.float32))
    return mixed.astype(jnp.bfloat16)

def embed_windows(padded, stem_weight, embedding):
    row_count, width = padded.shape
    band_count = width // CH_TOK - 1
    blocks = padded.reshape(row_count, band_count + 1, CH_TOK)
    windows = jnp.concatenate([blocks[:, :-1], blocks[:, 1:]], axis=2).reshape(row_count * band_count, 2 * CH_TOK)
    result = jnp.dot(windows, stem_weight, precision=lax.Precision.HIGHEST, preferred_element_type=jnp.float32)
    result = result.reshape(row_count, band_count, -1) + embedding[None]
    return result.astype(jnp.bfloat16)

def reference(radiance, stem_weight, band_embed, norm_spectral, spec_qkv, spec_out, norm_spatial, spat_qkv, spat_out, norm_mlp, up_weight, up_bias, down_weight):
    half_reach = CH_TOK // 2
    padded = jnp.pad(radiance, ((0, 0), (half_reach, half_reach)))
    tokens = embed_windows(padded, stem_weight, band_embed)
    head_dim = D // HEADS

    def spectral(block):
        pixel_count = block.shape[0]
        normed = layer_norm(block, norm_spectral).astype(jnp.bfloat16).reshape(-1, D)
        projected = jnp.dot(normed, spec_qkv, preferred_element_type=jnp.float32).astype(jnp.bfloat16)
        projected = projected.reshape(pixel_count, BANDS, HEADS, 3, head_dim)
        mixed_heads = attend(projected[:, :, :, 0], projected[:, :, :, 1], projected[:, :, :, 2], 'pqhd,pkhd->phqk', 'phqk,pkhd->pqhd')
        update = jnp.dot(mixed_heads.reshape(-1, D), spec_out, preferred_element_type=jnp.float32)
        return block.astype(jnp.float32) + update.reshape(pixel_count, BANDS, D)
    after_spectral = lax.map(spectral, tokens.reshape(PIXELS // 8, 8, BANDS, D)).reshape(PIXELS, BANDS, D)

    def project(block):
        normed = layer_norm(block, norm_spatial).astype(jnp.bfloat16).reshape(-1, D)
        projected = jnp.dot(normed, spat_qkv, preferred_element_type=jnp.float32).astype(jnp.bfloat16)
        return projected.reshape(block.shape[0], BANDS, HEADS, 3 * head_dim)
    spatial_proj = lax.map(project, after_spectral.reshape(PIXELS // 8, 8, BANDS, D)).reshape(PIXELS, BANDS, HEADS, 3 * head_dim)
    per_band = jnp.transpose(spatial_proj, (1, 2, 0, 3))

    def spatial(rows):
        return attend(rows[:, :, :head_dim], rows[:, :, head_dim:2 * head_dim], rows[:, :, 2 * head_dim:], 'iqd,ikd->iqk', 'iqk,ikd->iqd')
    spatial_mix = lax.map(spatial, per_band)
    spatial_mix = jnp.transpose(spatial_mix, (2, 0, 1, 3)).reshape(PIXELS, BANDS, D)

    def finish(pair):
        block, mixed_heads = pair
        pixel_count = block.shape[0]
        update = jnp.dot(mixed_heads.reshape(-1, D), spat_out, preferred_element_type=jnp.float32)
        after_spatial = block.reshape(-1, D) + update
        mlp_in = layer_norm(after_spatial, norm_mlp).astype(jnp.bfloat16)
        pre_act = jnp.dot(mlp_in, up_weight.T, preferred_element_type=jnp.float32) + up_bias.astype(jnp.float32)
        hidden = jax.nn.gelu(pre_act, approximate=True).astype(jnp.bfloat16)
        output = after_spatial + jnp.dot(hidden, down_weight, preferred_element_type=jnp.float32)
        return output.astype(jnp.bfloat16).reshape(pixel_count, BANDS, D)
    encoded = lax.map(finish, (after_spectral.reshape(PIXELS // 8, 8, BANDS, D), spatial_mix.reshape(PIXELS // 8, 8, BANDS, D)))
    return encoded.reshape(PIXELS, BANDS, D)
```

```python
import functools

import jax
import jax.numpy as jnp
from jax import lax
from jax.experimental import pallas as pl
from jax.experimental.pallas import tpu as pltpu
from jax.sharding import PartitionSpec as P

HEADS = 16
CH_TOK = 16
WIN = 2 * CH_TOK
LANES = 128
GROUP = LANES // WIN
SPAN = LANES // CH_TOK
F32 = jnp.float32
BF16 = jnp.bfloat16
HIGH = lax.Precision.HIGHEST


def mm(a, b):
    return jnp.dot(a, b, preferred_element_type=F32)


def mm_t(a, b):
    return lax.dot_general(a, b, (((1,), (1,)), ((), ())), preferred_element_type=F32)


def split2(x):
    hi = x.astype(BF16)
    return hi, (x - hi.astype(F32)).astype(BF16)


def spectral_kernel(
    px,
    nb,
    bands,
    base_ref,
    rad_ref,
    sel4_ref,
    sel1_ref,
    gram_ref,
    cross_ref,
    place_ref,
    const_ref,
    mse_ref,
    mee_ref,
    msw_ref,
    mew_ref,
    av_ref,
    stem_ref,
    embed_ref,
    out_w_ref,
    out_ref,
    win,
    ue,
    uw,
    rstd,
):
    base = base_ref[0]
    hg_count = HEADS // GROUP
    tiles = bands // SPAN
    lane = lax.broadcasted_iota(jnp.int32, (px, LANES), 1)
    acc = jnp.zeros((px, LANES), F32)
    for j in range(tiles):
        block = rad_ref[:, j * LANES : (j + 2) * LANES]
        wide = mm(block, sel4_ref[...])
        for i in range(SPAN):
            t = j * SPAN + i
            win[t * px : (t + 1) * px, :] = wide[:, i * LANES : (i + 1) * LANES]
        thin = mm(block, sel1_ref[...])
        thin_b = thin.astype(BF16)
        prod = thin * (
            mm(thin_b, gram_ref[0]) + mm(thin_b, gram_ref[1]) + cross_ref[j : j + 1, :]
        )
        hi, lo = split2(prod)
        summed = mm(hi, place_ref[...]) + mm(lo, place_ref[...])
        acc = jnp.where(lane // SPAN == j, summed, acc)
    for t in range(bands, LANES):
        win[t * px : (t + 1) * px, :] = jnp.zeros((px, LANES), F32)
    scale = lax.rsqrt(acc + const_ref[...] + 1e-5)
    rstd[...] = scale

    own = []
    for i in range(nb):
        rows = pl.ds(pl.multiple_of((base + i) * px, px), px)
        mine = win[rows, :].astype(BF16)
        own.append(mine)
        rq = jnp.sum(jnp.where(lane == base + i, scale, 0.0), axis=1, keepdims=True)
        part = (mm(mine, mse_ref[...]) + mee_ref[i : i + 1, :]) * rq
        for k in range(HEADS):
            r = k * nb + i
            ue[r * px : (r + 1) * px, :] = part[:, k * LANES : (k + 1) * LANES]
        part = (mm(mine, msw_ref[...]) + mew_ref[i : i + 1, :]) * rq
        for hl in range(GROUP):
            for hg in range(hg_count):
                r = (hl * hg_count + hg) * nb + i
                piece = part[:, hg * LANES : (hg + 1) * LANES]
                uw[r * px : (r + 1) * px, :] = jnp.where(lane // WIN == hl, piece, 0.0)

    rows = HEADS * nb
    valid = lax.broadcasted_iota(jnp.int32, (rows, LANES), 1) < bands
    step = 8

    def pixels(g, _):
        ps = [g * step + i for i in range(step)]
        ws = [win[pl.ds(p, LANES, stride=px), :].astype(BF16) for p in ps]
        ls = [uw[pl.ds(p, rows, stride=px), :].astype(BF16) for p in ps]
        rk = rstd[pl.ds(pl.multiple_of(g * step, step), step), :]
        ss = [mm_t(a, w) for a, w in zip(ls, ws)]
        es = []
        for i, p in enumerate(ps):
            rki = rk[i : i + 1, :]
            s = (ss[i] + ue[pl.ds(p, rows, stride=px), :]) * rki
            s = jnp.where(valid, s, -1e30)
            e = jnp.exp(s - jnp.max(s, axis=1, keepdims=True))
            e = e * (1.0 / jnp.sum(e, axis=1, keepdims=True))
            es.append(e * rki)
        zs = [mm(e.astype(BF16), w) for e, w in zip(es, ws)]
        for i, p in enumerate(ps):
            ue[pl.ds(p, rows, stride=px), :] = es[i]
            uw[pl.ds(p, rows, stride=px), :] = zs[i]
        return 0

    lax.fori_loop(0, px // step, pixels, 0)

    wide_lane = lax.broadcasted_iota(jnp.int32, (nb * px, LANES), 1)
    mixes = []
    for hg in range(hg_count):
        parts = []
        z = jnp.zeros((nb * px, LANES), F32)
        for hl in range(GROUP):
            r = (hl * hg_count + hg) * nb * px
            parts.append(ue[r : r + nb * px, :].astype(BF16))
            z = jnp.where(wide_lane // WIN == hl, uw[r : r + nb * px, :], z)
        parts.append(z.astype(BF16))
        mixes.append(mm(jnp.concatenate(parts, axis=1), av_ref[hg]).astype(BF16))
    update = mm(jnp.concatenate(mixes, axis=1), out_w_ref[...])
    for i in range(nb):
        token = (mm(own[i], stem_ref[...]) + embed_ref[i : i + 1, :]).astype(BF16)
        out_ref[i] = token.astype(F32) + update[i * px : (i + 1) * px, :]


def spatial_kernel(x_ref, gain_ref, qkv_ref, w_ref, out_ref, proj, mixed):
    x = x_ref[0]
    pixels, width = x.shape
    mean = jnp.mean(x, axis=1, keepdims=True)
    cent = x - mean
    var = jnp.mean(cent * cent, axis=1, keepdims=True)
    normed = (cent * lax.rsqrt(var + 1e-5) * gain_ref[...]).astype(BF16)
    chunk = 768
    for c in range(0, 3 * width, chunk):
        proj[:, c : c + chunk] = mm(normed, qkv_ref[:, c : c + chunk]).astype(BF16)
    head = width // HEADS
    lane = lax.broadcasted_iota(jnp.int32, (pixels, 2 * head), 1)
    low = lane < head
    for pair in range(HEADS // 2):
        c = pair * 6 * head
        t0 = proj[:, c : c + 2 * head]
        t1 = proj[:, c + 2 * head : c + 4 * head]
        t2 = proj[:, c + 4 * head : c + 6 * head]
        zero = jnp.zeros_like(t0)
        r0 = jnp.concatenate([t0[:, head:], t0[:, :head]], axis=1)
        r2 = jnp.concatenate([t2[:, head:], t2[:, :head]], axis=1)
        outs = []
        for q, k, v in (
            (jnp.where(low, t0, zero), r0, t1),
            (jnp.where(low, zero, t1), r2, t2),
        ):
            s = mm_t(q, k)
            e = jnp.exp((s - jnp.max(s, axis=1, keepdims=True)) * (head**-0.5))
            total = jnp.sum(e, axis=1, keepdims=True)
            outs.append(mm(e.astype(BF16), v) * (1.0 / total))
        mixed[:, pair * 2 * head : (pair + 1) * 2 * head] = jnp.where(
            low, outs[0], outs[1]
        ).astype(BF16)
    out_ref[0] = (x + mm(mixed[...], w_ref[...])).astype(BF16)


def flip_order(parts, index):
    out = jnp.stack(parts)
    bit = 1
    while bit < len(parts):
        shaped = out.reshape((len(parts) // (2 * bit), 2, bit) + out.shape[1:])
        turned = shaped[:, ::-1].reshape(out.shape)
        out = jnp.where((index // bit) % 2 == 1, turned, out)
        bit *= 2
    return out


def swap(x, axis, mask):
    count = lax.axis_size(axis)
    return lax.ppermute(x, axis, [(i, i ^ mask) for i in range(count)])


def gather_radiance(radiance):
    pix, band = lax.axis_index("pix"), lax.axis_index("band")
    r = radiance.astype(BF16)
    half = lax.axis_size("pix") // 2
    zs = flip_order([r] + [swap(r, "pix", 2 * k) for k in range(1, half)], pix // 2)
    bs = flip_order(
        [zs] + [swap(zs, "band", k) for k in range(1, lax.axis_size("band"))], band
    )
    cs = flip_order([bs, swap(bs, "pix", 1)], pix % 2)
    full = cs.transpose(2, 0, 3, 1, 4)
    rows = full.shape[0] * full.shape[1] * full.shape[2]
    return full.reshape(rows, full.shape[3] * full.shape[4])


def layer_norm(values, scaling):
    values = values.astype(F32)
    centred = values - jnp.mean(values, axis=-1, keepdims=True)
    variance = jnp.mean(centred * centred, axis=-1, keepdims=True)
    return centred * lax.rsqrt(variance + 1e-05) * scaling


def spectral_tables(stem_weight, band_embed, gain, qkv, base, nb):
    bands, width = band_embed.shape
    head = width // HEADS
    hg = HEADS // GROUP
    stem_c = stem_weight - jnp.mean(stem_weight, axis=1, keepdims=True)
    emb_c = band_embed - jnp.mean(band_embed, axis=1, keepdims=True)
    feats = (jnp.concatenate([stem_c, emb_c]) * gain).astype(BF16)
    a = mm(feats, qkv).astype(BF16).reshape(WIN + bands, HEADS, 3, head)
    aq, ak, av = a[:, :, 0], a[:, :, 1], a[:, :, 2]
    mine = jnp.concatenate([aq[:WIN], lax.dynamic_slice_in_dim(aq, WIN + base, nb, 0)])
    m = jnp.einsum("ihd,jhd->ihj", mine, ak, preferred_element_type=F32) * head**-0.5
    m = m.reshape(WIN + nb, hg, GROUP, WIN + bands)
    me = jnp.pad(m[..., WIN:], ((0, 0),) * 3 + ((0, LANES - bands),))
    me = me.transpose(0, 2, 1, 3).reshape(WIN + nb, HEADS * LANES)
    mw = m[..., :WIN].reshape(WIN + nb, hg * LANES)

    def stacked(x, n):
        pieces, rest = [], x
        for _ in range(n):
            hi, rest = rest.astype(BF16), rest - rest.astype(BF16).astype(F32)
            pieces.append(hi)
        return jnp.pad(jnp.concatenate(pieces), ((0, LANES - n * WIN), (0, 0)))

    eye = jnp.eye(GROUP, dtype=BF16)
    ave = jnp.pad(av[WIN:], ((0, LANES - bands), (0, 0), (0, 0))).reshape(LANES, hg, GROUP, head)
    ave = jnp.einsum("tgld,lm->gltmd", ave, eye).reshape(hg, GROUP * LANES, GROUP * head)
    avw = av[:WIN].reshape(WIN, hg, GROUP, head)
    avw = jnp.einsum("cgld,lm->glcmd", avw, eye).reshape(hg, LANES, GROUP * head)
    gram = jnp.dot(stem_c, stem_c.T, precision=HIGH) / width
    gram = jnp.kron(jnp.eye(SPAN, dtype=F32), gram)
    cross = 2.0 * jnp.dot(emb_c, stem_c.T, precision=HIGH) / width
    const = jnp.pad(jnp.mean(emb_c * emb_c, axis=1), (0, LANES - bands))[None]
    return dict(
        mse=stacked(me[:WIN], 2),
        mee=me[WIN:],
        msw=stacked(mw[:WIN], 2),
        mew=mw[WIN:],
        av=jnp.concatenate([ave, avw], axis=1),
        stem=stacked(stem_weight, 3),
        embed=lax.dynamic_slice_in_dim(band_embed, base, nb, 0),
        gram=jnp.stack(split2(gram)),
        cross=cross.reshape(bands // SPAN, SPAN * WIN),
        const=const,
    )


def selectors():
    row = jnp.arange(2 * LANES)[:, None]
    col = jnp.arange(SPAN * LANES)[None]
    sel4 = (row == (col // LANES) * CH_TOK + col % WIN).astype(BF16)
    col = jnp.arange(SPAN * WIN)[None]
    sel1 = (row == (col // WIN) * CH_TOK + col % WIN).astype(BF16)
    place = (row // WIN == jnp.arange(LANES)[None] % SPAN).astype(BF16)
    return sel4, sel1, place


def whole_spec(shape):
    return pl.BlockSpec(shape, lambda *_: (0,) * len(shape))


def spectral(full, base, tables, spec_out, nb, bands):
    pixels, channels = full.shape
    width = spec_out.shape[0]
    edge = CH_TOK // 2
    lanes = (bands // SPAN + 1) * LANES
    rad = jnp.pad(full, ((0, 0), (edge, lanes - channels - edge)))
    px = 64
    sel4, sel1, place = selectors()
    t = tables
    consts = [
        sel4, sel1, t["gram"], t["cross"], place, t["const"], t["mse"], t["mee"],
        t["msw"], t["mew"], t["av"], t["stem"], t["embed"], spec_out,
    ]
    return pl.pallas_call(
        functools.partial(spectral_kernel, px, nb, bands),
        grid=(pixels // px,),
        out_shape=jax.ShapeDtypeStruct((nb, pixels, width), F32),
        in_specs=[pl.BlockSpec(memory_space=pltpu.SMEM), pl.BlockSpec((px, lanes), lambda i: (i, 0))]
        + [whole_spec(c.shape) for c in consts],
        out_specs=pl.BlockSpec((nb, px, width), lambda i: (0, i, 0)),
        scratch_shapes=[
            pltpu.VMEM((LANES * px, LANES), F32),
            pltpu.VMEM((HEADS * nb * px, LANES), F32),
            pltpu.VMEM((HEADS * nb * px, LANES), F32),
            pltpu.VMEM((px, LANES), F32),
        ],
        compiler_params=pltpu.CompilerParams(vmem_limit_bytes=56 * 2**20),
        name="spectral",
    )(base[None], rad, *consts)


def spatial(x, gain, qkv, w):
    nb, pixels, width = x.shape
    return pl.pallas_call(
        spatial_kernel,
        grid=(nb,),
        out_shape=jax.ShapeDtypeStruct(x.shape, BF16),
        in_specs=[
            pl.BlockSpec((1, pixels, width), lambda i: (i, 0, 0)),
            whole_spec((1, width)),
            whole_spec(qkv.shape),
            whole_spec(w.shape),
        ],
        out_specs=pl.BlockSpec((1, pixels, width), lambda i: (i, 0, 0)),
        scratch_shapes=[
            pltpu.VMEM((pixels, 3 * width), BF16),
            pltpu.VMEM((pixels, width), BF16),
        ],
        compiler_params=pltpu.CompilerParams(vmem_limit_bytes=56 * 2**20),
        name="spatial",
    )(x, gain[None], qkv, w)


def local(
    radiance,
    stem_weight,
    band_embed,
    norm_spectral,
    spec_qkv,
    spec_out,
    norm_spatial,
    spat_qkv,
    spat_out,
    norm_mlp,
    up_weight,
    up_bias,
    down_weight,
):
    bands, width = band_embed.shape
    bsize, psize = lax.axis_size("band"), lax.axis_size("pix")
    devices = bsize * psize
    nb = -(-bands // devices)
    band = lax.axis_index("band")
    place = lax.axis_index("pix") * bsize + band
    base = jnp.minimum(place * nb, bands - nb).astype(jnp.int32)

    share = up_weight.shape[0] // bsize
    both = jnp.concatenate(
        [
            lax.dynamic_slice_in_dim(up_weight, band * share, share, 0),
            lax.dynamic_slice_in_dim(down_weight, band * share, share, 0),
        ]
    )
    both = lax.all_gather(both, ("pix", "band"), axis=0)
    up = both[:, :share].reshape(-1, width)
    down = both[:, share:].reshape(-1, width)
    bias = lax.all_gather(up_bias, "pix", axis=0, tiled=True)

    full = gather_radiance(radiance)
    tables = spectral_tables(stem_weight, band_embed, norm_spectral, spec_qkv, base, nb)
    after_spectral = spectral(full, base, tables, spec_out, nb, bands)
    after_spatial = spatial(after_spectral, norm_spatial, spat_qkv, spat_out)
    moved = lax.all_to_all(
        after_spatial, ("pix", "band"), split_axis=1, concat_axis=0, tiled=True
    )[:bands]
    pixel_count = moved.shape[1]
    x = moved.reshape(-1, width).astype(F32)
    mlp_in = layer_norm(x, norm_mlp).astype(BF16)
    pre_act = mm_t(mlp_in, up) + bias.astype(F32)
    hidden = jax.nn.gelu(pre_act, approximate=True).astype(BF16)
    encoded = (x + mm(hidden, down)).astype(BF16)
    return encoded.reshape(bands, pixel_count, width).transpose(1, 0, 2)


def solution(mesh):
    placed = (
        P("pix", "band"),
        P(),
        P(),
        P(),
        P(),
        P(),
        P(),
        P(),
        P(),
        P(),
        P("pix", None),
        P("pix"),
        P("pix", None),
    )
    return jax.shard_map(
        local, mesh=mesh, in_specs=placed, out_specs=P(("pix", "band"), None, None), check_vma=False
    )
```

```python
import functools

import jax
import jax.numpy as jnp
from jax import lax
from jax.experimental import pallas as pl
from jax.experimental.pallas import tpu as pltpu
from jax.sharding import PartitionSpec as P

HEADS = 16
CH_TOK = 16
WIN = 2 * CH_TOK
LANES = 128
GROUP = LANES // WIN
SPAN = LANES // CH_TOK
GAP = 8
F32 = jnp.float32
BF16 = jnp.bfloat16
HIGH = lax.Precision.HIGHEST
VMEM_LIMIT = 60 * 2**20


def mm(a, b):
    return jnp.dot(a, b, preferred_element_type=F32)


def mm_t(a, b):
    return lax.dot_general(a, b, (((1,), (1,)), ((), ())), preferred_element_type=F32)


def split2(x):
    hi = x.astype(BF16)
    return hi, (x - hi.astype(F32)).astype(BF16)


def tables_kernel(bands, stem_ref, embed_ref, own_ref, gain_ref, qkv_ref, mse_ref, mee_ref, av_ref, feats):
    @pl.when(pl.program_id(0) == 0)
    def _():
        def centred(x):
            return (x - jnp.mean(x, axis=1, keepdims=True)) * gain_ref[...]

        stem = centred(stem_ref[...])
        own = centred(own_ref[...])
        width = stem.shape[1]
        blank = jnp.zeros((LANES - bands, width), F32)
        tail = jnp.zeros((8, width), F32)
        feats[...] = jnp.concatenate(
            [centred(embed_ref[...]), blank] + [stem] * GROUP + [own, tail]
        ).astype(BF16)

    a = mm(feats[...], qkv_ref[...]).astype(BF16)
    head = a.shape[1] // 6
    keys = 2 * LANES
    scale = head**-0.5
    for i in range(2):
        c = 3 * i * head
        q = a[:, c : c + head]
        k = a[:keys, c + head : c + 2 * head]
        m = mm_t(q[LANES : LANES + WIN], k) * scale
        hi, lo = split2(m)
        mse_ref[:WIN, i * keys : (i + 1) * keys] = hi
        mse_ref[WIN:, i * keys : (i + 1) * keys] = lo
        mee_ref[:, i * keys : (i + 1) * keys] = mm_t(q[keys : keys + 16], k)[:8] * scale
    av_ref[...] = a[:keys, 2 * head :]


def make_tables(stem_weight, band_embed, own, gain, qkv):
    bands, width = band_embed.shape
    own8 = jnp.pad(own, ((0, 8 - own.shape[0]), (0, 0)))
    steps = HEADS // 2
    cols = qkv.shape[1] // steps
    return pl.pallas_call(
        functools.partial(tables_kernel, bands),
        grid=(steps,),
        out_shape=[
            jax.ShapeDtypeStruct((2 * WIN, HEADS * 2 * LANES), BF16),
            jax.ShapeDtypeStruct((8, HEADS * 2 * LANES), F32),
            jax.ShapeDtypeStruct((2 * LANES, steps * cols * 2 // 3), BF16),
        ],
        in_specs=[
            whole_spec(stem_weight.shape),
            whole_spec(band_embed.shape),
            whole_spec(own8.shape),
            whole_spec((1, width)),
            pl.BlockSpec((width, cols), lambda i: (0, i)),
        ],
        out_specs=[
            pl.BlockSpec((2 * WIN, 4 * LANES), lambda i: (0, i)),
            pl.BlockSpec((8, 4 * LANES), lambda i: (0, i)),
            pl.BlockSpec((2 * LANES, cols * 2 // 3), lambda i: (0, i)),
        ],
        scratch_shapes=[pltpu.VMEM((2 * LANES + 16, width), BF16)],
        compiler_params=pltpu.CompilerParams(vmem_limit_bytes=VMEM_LIMIT),
        cost_estimate=pl.CostEstimate(flops=4 * 10**9, bytes_accessed=8 * 2**20, transcendentals=0),
        name="tables",
    )(stem_weight, band_embed, own8, gain[None], qkv)


def spectral_kernel(
    nb,
    bands,
    base_ref,
    rad_ref,
    sel_ref,
    sel1_ref,
    gram_ref,
    cross_ref,
    place_ref,
    const_ref,
    mse_ref,
    mee_ref,
    av_ref,
    stem_ref,
    embed_ref,
    out_w_ref,
    out_ref,
    win,
    ue,
    uw,
    rstd,
):
    base = base_ref[0]
    px = rad_ref.shape[0]
    part_px = px // GROUP
    tiles = bands // SPAN
    wstep, ustep = part_px + GAP, px + GAP
    lane = lax.broadcasted_iota(jnp.int32, (px, LANES), 1)
    row = lax.broadcasted_iota(jnp.int32, (px, LANES), 0)
    blocks = [rad_ref[:, j * LANES : (j + 2) * LANES] for j in range(tiles)]

    packed = jnp.concatenate(
        [
            jnp.concatenate([b[i * part_px : (i + 1) * part_px] for i in range(GROUP)], axis=1)
            for b in blocks
        ]
    )
    for i in range(0, SPAN, 2):
        wide = mm(packed, sel_ref[:, i * LANES : (i + 2) * LANES])
        for j in range(tiles):
            for k in range(2):
                t = j * SPAN + i + k
                win[t * wstep : t * wstep + part_px, :] = wide[
                    j * part_px : (j + 1) * part_px, k * LANES : (k + 1) * LANES
                ]
    for t in range(bands, LANES):
        win[t * wstep : t * wstep + part_px, :] = jnp.zeros((part_px, LANES), F32)

    acc = jnp.zeros((px, LANES), F32)
    thin = mm(jnp.concatenate(blocks), sel1_ref[...])
    thin_b = thin.astype(BF16)
    form = mm(thin_b, gram_ref[0]) + mm(thin_b, gram_ref[1])
    for j in range(tiles):
        rows = slice(j * px, (j + 1) * px)
        hi, lo = split2(thin[rows] * (form[rows] + cross_ref[j : j + 1, :]))
        summed = mm(hi, place_ref[...]) + mm(lo, place_ref[...])
        acc = jnp.where(lane // SPAN == j, summed, acc)
    scale = lax.rsqrt(acc + const_ref[...] + 1e-5)
    rstd[...] = scale

    own = []
    for i in range(nb):
        t = base + i
        tile = t // SPAN
        cols = pl.ds(pl.multiple_of(tile * LANES, LANES), 2 * LANES)
        shift = t % SPAN
        at = lax.broadcasted_iota(jnp.int32, (2 * LANES, LANES), 0)
        to = lax.broadcasted_iota(jnp.int32, (2 * LANES, LANES), 1)
        pick = (at == shift * CH_TOK + to % WIN).astype(F32).astype(BF16)
        mine = mm(rad_ref[:, cols], pick).astype(BF16)
        own.append(mine)
        rq = jnp.sum(jnp.where(lane == t, scale, 0.0), axis=1, keepdims=True)
        for h in range(0, HEADS, 2):
            both = slice(2 * h * LANES, 2 * (h + 2) * LANES)
            part = (mm(mine[:, : 2 * WIN], mse_ref[:, both]) + mee_ref[i : i + 1, both]) * rq
            for k in range(2):
                r = ((h + k) * nb + i) * ustep
                ue[r : r + px, :] = part[:, 2 * k * LANES : (2 * k + 1) * LANES]
                uw[r : r + px, :] = jnp.where(
                    lane // WIN == row // part_px,
                    part[:, (2 * k + 1) * LANES : (2 * k + 2) * LANES],
                    0.0,
                )

    rows = HEADS * nb
    valid = lax.broadcasted_iota(jnp.int32, (rows, LANES), 1) < bands
    step = 2

    def groups(g, _):
        ids = [g * step + k for k in range(step)]
        ws = [win[pl.ds(p, LANES, stride=wstep), :].astype(BF16) for p in ids]
        ls = [
            jnp.concatenate(
                [uw[pl.ds(i * part_px + p, rows, stride=ustep), :] for i in range(GROUP)]
            ).astype(BF16)
            for p in ids
        ]
        ss = [mm_t(a, w) for a, w in zip(ls, ws)]
        es = []
        for k, p in enumerate(ids):
            for i in range(GROUP):
                q = i * part_px + p
                rki = rstd[pl.ds(q, 1), :]
                s = (ss[k][i * rows : (i + 1) * rows] + ue[pl.ds(q, rows, stride=ustep), :]) * rki
                s = jnp.where(valid, s, -1e30)
                e = jnp.exp(s - jnp.max(s, axis=1, keepdims=True))
                e = e * (1.0 / jnp.sum(e, axis=1, keepdims=True)) * rki
                ue[pl.ds(q, rows, stride=ustep), :] = e
                es.append(e)
        for k, p in enumerate(ids):
            z = mm(jnp.concatenate(es[k * GROUP : (k + 1) * GROUP]).astype(BF16), ws[k])
            for i in range(GROUP):
                uw[pl.ds(i * part_px + p, rows, stride=ustep), :] = z[i * rows : (i + 1) * rows]
        return 0

    lax.fori_loop(0, part_px // step, groups, 0)

    keep = lane // WIN == row // part_px
    half = lane < LANES // 2
    for i in range(nb):
        mixes = []
        for h in range(0, HEADS, 2):
            outs = []
            for k in range(2):
                r = ((h + k) * nb + i) * ustep
                both = jnp.concatenate(
                    [ue[r : r + px, :], jnp.where(keep, uw[r : r + px, :], 0.0)], axis=1
                ).astype(BF16)
                outs.append(mm(both, av_ref[:, (h + k) * LANES : (h + k + 1) * LANES]))
            mixes.append(jnp.where(half, outs[0], outs[1]).astype(BF16))
        update = mm(jnp.concatenate(mixes, axis=1), out_w_ref[...])
        token = (mm(own[i], stem_ref[...]) + embed_ref[i : i + 1, :]).astype(BF16)
        out_ref[i] = token.astype(F32) + update


def spatial_band(x, gain_ref, qkv_ref, w_ref, proj, mixed):
    pixels, width = x.shape
    cent = x - jnp.mean(x, axis=1, keepdims=True)
    var = jnp.mean(cent * cent, axis=1, keepdims=True)
    normed = (cent * lax.rsqrt(var + 1e-5) * gain_ref[...]).astype(BF16)
    chunk = 6 * width // HEADS
    for c in range(0, 3 * width, chunk):
        proj[:, c : c + chunk] = mm(normed, qkv_ref[:, c : c + chunk]).astype(BF16)
    head = width // HEADS
    low = lax.broadcasted_iota(jnp.int32, (pixels, 2 * head), 1) < head
    for pair in range(HEADS // 2):
        c = pair * 6 * head
        t0 = proj[:, c : c + 2 * head]
        t1 = proj[:, c + 2 * head : c + 4 * head]
        t2 = proj[:, c + 4 * head : c + 6 * head]
        zero = jnp.zeros_like(t0)
        r0 = jnp.concatenate([t0[:, head:], t0[:, :head]], axis=1)
        r2 = jnp.concatenate([t2[:, head:], t2[:, :head]], axis=1)
        outs = []
        for q, k, v in (
            (jnp.where(low, t0, zero), r0, t1),
            (jnp.where(low, zero, t1), r2, t2),
        ):
            s = mm_t(q, k)
            e = jnp.exp((s - jnp.max(s, axis=1, keepdims=True)) * (head**-0.5))
            total = jnp.sum(e, axis=1, keepdims=True)
            outs.append(mm(e.astype(BF16), v) * (1.0 / total))
        mixed[:, pair * 2 * head : (pair + 1) * 2 * head] = jnp.where(
            low, outs[0], outs[1]
        ).astype(BF16)
    return x + mm(mixed[...], w_ref[...])


def spatial_kernel(x_ref, gain_ref, qkv_ref, w_ref, out_ref, proj, mixed):
    out_ref[0] = spatial_band(x_ref[0], gain_ref, qkv_ref, w_ref, proj, mixed).astype(BF16)


def spatial_send_kernel(devices, x_ref, gain_ref, qkv_ref, w_ref, out_ref, proj, mixed, rows):
    b = pl.program_id(0)
    y = spatial_band(x_ref[0], gain_ref, qkv_ref, w_ref, proj, mixed)
    each = y.shape[0] // devices
    rows[:, pl.ds(pl.multiple_of(b * each, each), each), :] = y.reshape(devices, each, y.shape[1])

    @pl.when(b == pl.num_programs(0) - 1)
    def _():
        out_ref[...] = rows[...].astype(BF16)


def spatial(x, gain, qkv, w, first, count, devices):
    nb, pixels, width = x.shape
    each = pixels // devices
    in_specs = [
        pl.BlockSpec((1, pixels, width), lambda i: (first + i, 0, 0)),
        whole_spec((1, width)),
        whole_spec(qkv.shape),
        whole_spec(w.shape),
    ]
    scratch = [pltpu.VMEM((pixels, 3 * width), BF16), pltpu.VMEM((pixels, width), BF16)]
    params = dict(
        grid=(count,),
        in_specs=in_specs,
        compiler_params=pltpu.CompilerParams(vmem_limit_bytes=VMEM_LIMIT),
        cost_estimate=pl.CostEstimate(
            flops=count * 5 * 10**9, bytes_accessed=10 * 2**20, transcendentals=0
        ),
        name="spatial",
    )
    if direct(pixels, devices, count):
        return pl.pallas_call(
            functools.partial(spatial_send_kernel, devices),
            out_shape=jax.ShapeDtypeStruct((devices, count * each, width), BF16),
            out_specs=whole_spec((devices, count * each, width)),
            scratch_shapes=scratch + [pltpu.VMEM((devices, count * each, width), F32)],
            **params,
        )(x, gain[None], qkv, w)
    return pl.pallas_call(
        spatial_kernel,
        out_shape=jax.ShapeDtypeStruct((count, pixels, width), BF16),
        out_specs=pl.BlockSpec((1, pixels, width), lambda i: (i, 0, 0)),
        scratch_shapes=scratch,
        **params,
    )(x, gain[None], qkv, w)


def direct(pixels, devices, count):
    each = pixels // devices
    return each % 8 == 0 and (each * count) % 16 == 0


def mlp_kernel(x_ref, gain_ref, w_ref, bias_ref, out_ref, normed, acc):
    step = pl.program_id(0)
    src, share2, width = w_ref.shape
    share = share2 // 2

    @pl.when(step == 0)
    def _():
        x = x_ref[...].astype(F32)
        cent = x - jnp.mean(x, axis=1, keepdims=True)
        var = jnp.mean(cent * cent, axis=1, keepdims=True)
        normed[...] = (cent * lax.rsqrt(var + 1e-5) * gain_ref[...]).astype(BF16)
        acc[...] = x

    up = w_ref[:, :share, :].reshape(src * share, width)
    down = w_ref[:, share:, :].reshape(src * share, width)
    v = mm_t(normed[...], up) + bias_ref[0]
    hidden = 0.5 * v * (1.0 + jnp.tanh((2 / jnp.pi) ** 0.5 * (v + 0.044715 * (v * v * v))))
    acc[...] += mm(hidden.astype(BF16), down)

    @pl.when(step == pl.num_programs(0) - 1)
    def _():
        out_ref[...] = acc[...].astype(BF16)


def mlp(x, rows, gain, weights, bias):
    devices, share2, width = weights.shape
    hidden = 512
    per = hidden * 2 // share2
    steps = devices // per
    return pl.pallas_call(
        mlp_kernel,
        grid=(steps,),
        out_shape=jax.ShapeDtypeStruct((rows, width), BF16),
        in_specs=[
            pl.BlockSpec((rows, width), lambda i: (0, 0)),
            whole_spec((1, width)),
            pl.BlockSpec((per, share2, width), lambda i: (i, 0, 0)),
            pl.BlockSpec((1, 1, hidden), lambda i: (i, 0, 0)),
        ],
        out_specs=pl.BlockSpec((rows, width), lambda i: (0, 0)),
        scratch_shapes=[pltpu.VMEM((rows, width), BF16), pltpu.VMEM((rows, width), F32)],
        compiler_params=pltpu.CompilerParams(vmem_limit_bytes=VMEM_LIMIT),
        cost_estimate=pl.CostEstimate(
            flops=4 * rows * width * share2 * devices // 2, bytes_accessed=20 * 2**20, transcendentals=0
        ),
        name="mlp",
    )(x, gain[None], weights, bias.reshape(steps, 1, hidden))


def flip_order(parts, index):
    out = jnp.stack(parts)
    bit = 1
    while bit < len(parts):
        shaped = out.reshape((len(parts) // (2 * bit), 2, bit) + out.shape[1:])
        turned = shaped[:, ::-1].reshape(out.shape)
        out = jnp.where((index // bit) % 2 == 1, turned, out)
        bit *= 2
    return out


def swap(x, axis, mask):
    count = lax.axis_size(axis)
    return lax.ppermute(x, axis, [(i, i ^ mask) for i in range(count)])


def variance_tables(stem_weight, band_embed):
    bands, width = band_embed.shape
    stem_c = stem_weight - jnp.mean(stem_weight, axis=1, keepdims=True)
    emb_c = band_embed - jnp.mean(band_embed, axis=1, keepdims=True)
    gram = jnp.dot(stem_c, stem_c.T, precision=HIGH) / width
    gram = jnp.kron(jnp.eye(SPAN, dtype=F32), gram)
    cross = 2.0 * jnp.dot(emb_c, stem_c.T, precision=HIGH) / width
    const = jnp.pad(jnp.mean(emb_c * emb_c, axis=1), (0, LANES - bands))[None]
    return jnp.stack(split2(gram)), cross.reshape(bands // SPAN, SPAN * WIN), const


def selectors():
    row = jnp.arange(GROUP * 2 * LANES)[:, None]
    col = jnp.arange(SPAN * LANES)[None]
    within = row % (2 * LANES)
    sel = (within == (col // LANES) * CH_TOK + col % WIN) & (
        row // (2 * LANES) == col % LANES // WIN
    )
    row = jnp.arange(2 * LANES)[:, None]
    col = jnp.arange(SPAN * WIN)[None]
    sel1 = row == (col // WIN) * CH_TOK + col % WIN
    place = row // WIN == jnp.arange(LANES)[None] % SPAN
    return sel.astype(BF16), sel1.astype(BF16), place.astype(BF16)


def stem_pieces(x):
    pieces, rest = [], x
    for _ in range(3):
        hi = rest.astype(BF16)
        rest = rest - hi.astype(F32)
        pieces.append(hi)
    return jnp.pad(jnp.concatenate(pieces), ((0, LANES - 3 * WIN), (0, 0)))


def whole_spec(shape):
    return pl.BlockSpec(shape, lambda *_: (0,) * len(shape))


def spectral(full, base, tables, variances, chosen, stem, own, spec_out, nb, bands):
    pixels, channels = full.shape
    width = spec_out.shape[0]
    edge = CH_TOK // 2
    lanes = (bands // SPAN + 1) * LANES
    rad = jnp.pad(full, ((0, 0), (edge, lanes - channels - edge)))
    sel, sel1, place = chosen
    gram, cross, const = variances
    mse, mee, av = tables
    consts = [sel, sel1, gram, cross, place, const, mse, mee, av, stem, own, spec_out]
    part_px = pixels // GROUP
    return pl.pallas_call(
        functools.partial(spectral_kernel, nb, bands),
        out_shape=jax.ShapeDtypeStruct((nb, pixels, width), F32),
        in_specs=[pl.BlockSpec(memory_space=pltpu.SMEM)]
        + [pl.BlockSpec(memory_space=pltpu.VMEM)] * (1 + len(consts)),
        out_specs=pl.BlockSpec(memory_space=pltpu.VMEM),
        scratch_shapes=[
            pltpu.VMEM((LANES * (part_px + GAP), LANES), F32),
            pltpu.VMEM((HEADS * nb * (pixels + GAP), LANES), F32),
            pltpu.VMEM((HEADS * nb * (pixels + GAP), LANES), F32),
            pltpu.VMEM((pixels, LANES), F32),
        ],
        compiler_params=pltpu.CompilerParams(vmem_limit_bytes=VMEM_LIMIT),
        cost_estimate=pl.CostEstimate(
            flops=12 * 10**9, bytes_accessed=12 * 2**20, transcendentals=0
        ),
        name="spectral",
    )(base[None], rad, *consts)


def local(
    radiance,
    stem_weight,
    band_embed,
    norm_spectral,
    spec_qkv,
    spec_out,
    norm_spatial,
    spat_qkv,
    spat_out,
    norm_mlp,
    up_weight,
    up_bias,
    down_weight,
):
    bands, width = band_embed.shape
    bsize, psize = lax.axis_size("band"), lax.axis_size("pix")
    devices = bsize * psize
    nb = -(-bands // devices)
    band, pix = lax.axis_index("band"), lax.axis_index("pix")
    base = jnp.minimum((pix * bsize + band) * nb, bands - nb).astype(jnp.int32)

    share = up_weight.shape[0] // bsize
    both = jnp.concatenate(
        [
            lax.dynamic_slice_in_dim(up_weight, band * share, share, 0),
            lax.dynamic_slice_in_dim(down_weight, band * share, share, 0),
        ]
    )
    weights = lax.all_gather(both, ("pix", "band"), axis=0)

    rows, channels = radiance.shape
    message = jnp.concatenate([radiance.astype(BF16), up_bias.reshape(rows, -1)], axis=1)
    zs = flip_order([message] + [swap(message, "pix", 2 * k) for k in range(1, psize // 2)], pix // 2)
    bs = flip_order([zs] + [swap(zs, "band", k) for k in range(1, bsize)], band)
    cs = flip_order([bs, swap(bs, "pix", 1)], pix % 2)
    cs = cs.transpose(2, 0, 3, 1, 4)
    full = cs[..., :channels].reshape(rows * psize, bsize * channels)
    bias = cs[:, :, :, 0, channels:].astype(F32)

    own = lax.dynamic_slice_in_dim(band_embed, base, nb, 0)
    tables = make_tables(stem_weight, band_embed, own, norm_spectral, spec_qkv)
    after_spectral = spectral(
        full,
        base,
        tables,
        variance_tables(stem_weight, band_embed),
        selectors(),
        stem_pieces(stem_weight),
        own,
        spec_out,
        nb,
        bands,
    )
    pixels = after_spectral.shape[1]
    each = pixels // devices
    count = nb // 2 if nb % 2 == 0 and direct(pixels, devices, nb // 2) else nb
    results = []
    for first in range(0, nb, count):
        part = spatial(after_spectral, norm_spatial, spat_qkv, spat_out, first, count, devices)
        if direct(pixels, devices, count):
            moved = lax.all_to_all(part, ("pix", "band"), split_axis=0, concat_axis=0, tiled=True)
        else:
            moved = lax.all_to_all(part, ("pix", "band"), split_axis=1, concat_axis=0, tiled=True)
        moved = moved.reshape(-1, width)
        valid = bands // nb * count * each
        done = mlp(moved, valid, norm_mlp, weights, bias)
        results.append(done.reshape(bands // nb, count, each, width))
    encoded = jnp.stack(results, axis=1)
    return encoded.reshape(bands, each, width).transpose(1, 0, 2)


def solution(mesh):
    placed = (
        P("pix", "band"),
        P(),
        P(),
        P(),
        P(),
        P(),
        P(),
        P(),
        P(),
        P(),
        P("pix", None),
        P("pix"),
        P("pix", None),
    )
    return jax.shard_map(
        local, mesh=mesh, in_specs=placed, out_specs=P(("pix", "band"), None, None), check_vma=False
    )
```

```python
import functools
import math

import jax
import jax.numpy as jnp
import numpy as np
from jax import lax
from jax.experimental import pallas as pl
from jax.experimental.pallas import tpu as pltpu
from jax.sharding import PartitionSpec as P

HEADS = 16
CH_TOK = 16
WIN = 2 * CH_TOK
LANES = 128
GROUP = LANES // WIN
SPAN = LANES // CH_TOK
GAP = 8
F32 = jnp.float32
BF16 = jnp.bfloat16
HIGH = lax.Precision.HIGHEST
LOG2_E = math.log2(math.e)
VMEM_LIMIT = 60 * 2**20


def mm(a, b):
    return jnp.dot(a, b, preferred_element_type=F32)


def mm_t(a, b):
    return lax.dot_general(a, b, (((1,), (1,)), ((), ())), preferred_element_type=F32)


def split2(x):
    hi = x.astype(BF16)
    return hi, (x - hi.astype(F32)).astype(BF16)


def mm_exact(a, b):
    return lax.dot_general(
        a, b, (((1,), (1,)), ((), ())), precision=HIGH, preferred_element_type=F32
    )


def tables_kernel(
    bands,
    stem_ref,
    embed_ref,
    own_ref,
    gain_ref,
    qkv_ref,
    mse_ref,
    mee_ref,
    av_ref,
    gram_ref,
    cross_ref,
    const_ref,
    pieces_ref,
    feats,
):
    @pl.when(pl.program_id(0) == 0)
    def _():
        def centred(x):
            return x - jnp.mean(x, axis=1, keepdims=True)

        gain = gain_ref[...]
        stem = centred(stem_ref[...])
        width = stem.shape[1]
        blank = jnp.zeros((LANES - bands, width), F32)
        embed = jnp.concatenate([centred(embed_ref[...]), blank])
        stem_g = stem * gain
        tail = jnp.zeros((8, width), F32)
        feats[...] = jnp.concatenate(
            [embed * gain] + [stem_g] * GROUP + [centred(own_ref[...]) * gain, tail]
        ).astype(BF16)

        many = jnp.concatenate([stem] * SPAN)
        shape = (SPAN * WIN, SPAN * WIN)
        same = (
            lax.broadcasted_iota(jnp.int32, shape, 0) // WIN
            == lax.broadcasted_iota(jnp.int32, shape, 1) // WIN
        )
        gram = jnp.where(same, mm_exact(many, many) * (1.0 / width), 0.0)
        gram_ref[0], gram_ref[1] = split2(gram)
        shape = (LANES, SPAN * WIN)
        same = (
            lax.broadcasted_iota(jnp.int32, shape, 0) % SPAN
            == lax.broadcasted_iota(jnp.int32, shape, 1) // WIN
        )
        cross = jnp.where(same, mm_exact(embed, many) * (2.0 / width), 0.0)
        cross_ref[...] = jnp.sum(cross.reshape(LANES // SPAN, SPAN, SPAN * WIN), axis=1)
        const_ref[...] = mm_exact(jnp.ones((8, width), F32), embed * embed) * (1.0 / width)

        rest = stem_ref[...]
        pieces = []
        for _ in range(3):
            hi = rest.astype(BF16).astype(F32)
            pieces.append(hi)
            rest = rest - hi
        pieces_ref[...] = jnp.concatenate(pieces + [jnp.zeros_like(rest)]).astype(BF16)

    a = mm(feats[...], qkv_ref[...]).astype(BF16)
    head = a.shape[1] // 6
    keys = 2 * LANES
    scale = head**-0.5 * LOG2_E
    beyond = lax.broadcasted_iota(jnp.int32, (8, keys), 1)
    beyond = (beyond >= bands) & (beyond < LANES)
    for i in range(2):
        c = 3 * i * head
        q = a[:, c : c + head]
        k = a[:keys, c + head : c + 2 * head]
        m = mm_t(q[LANES : LANES + WIN], k) * scale
        hi, lo = split2(m)
        mse_ref[:WIN, i * keys : (i + 1) * keys] = hi
        mse_ref[WIN:, i * keys : (i + 1) * keys] = lo
        m = mm_t(q[keys : keys + 16], k)[:8] * scale
        mee_ref[:, i * keys : (i + 1) * keys] = jnp.where(beyond, -1e30, m)
    av_ref[...] = a[:keys, 2 * head :]


def make_tables(stem_weight, band_embed, own, gain, qkv):
    bands, width = band_embed.shape
    own8 = jnp.pad(own, ((0, 8 - own.shape[0]), (0, 0)))
    steps = HEADS // 2
    cols = qkv.shape[1] // steps
    square = SPAN * WIN
    fixed = [
        jax.ShapeDtypeStruct((2, square, square), BF16),
        jax.ShapeDtypeStruct((LANES // SPAN, square), F32),
        jax.ShapeDtypeStruct((8, LANES), F32),
        jax.ShapeDtypeStruct((LANES, width), BF16),
    ]
    return pl.pallas_call(
        functools.partial(tables_kernel, bands),
        grid=(steps,),
        out_shape=[
            jax.ShapeDtypeStruct((2 * WIN, HEADS * 2 * LANES), BF16),
            jax.ShapeDtypeStruct((8, HEADS * 2 * LANES), F32),
            jax.ShapeDtypeStruct((2 * LANES, steps * cols * 2 // 3), BF16),
        ]
        + fixed,
        in_specs=[
            whole_spec(stem_weight.shape),
            whole_spec(band_embed.shape),
            whole_spec(own8.shape),
            whole_spec((1, width)),
            pl.BlockSpec((width, cols), lambda i: (0, i)),
        ],
        out_specs=[
            pl.BlockSpec((2 * WIN, 4 * LANES), lambda i: (0, i)),
            pl.BlockSpec((8, 4 * LANES), lambda i: (0, i)),
            pl.BlockSpec((2 * LANES, cols * 2 // 3), lambda i: (0, i)),
        ]
        + [whole_spec(f.shape) for f in fixed],
        scratch_shapes=[pltpu.VMEM((2 * LANES + 16, width), BF16)],
        compiler_params=pltpu.CompilerParams(vmem_limit_bytes=32 * 2**20),
        cost_estimate=pl.CostEstimate(flops=4 * 10**9, bytes_accessed=8 * 2**20, transcendentals=0),
        name="tables",
    )(stem_weight, band_embed, own8, gain[None], qkv)


def spectral_kernel(
    nb,
    bands,
    place_ref,
    near_ref,
    far_ref,
    sel_ref,
    sel1_ref,
    group_ref,
    mse_ref,
    mee_ref,
    av_ref,
    gram_ref,
    cross_ref,
    const_ref,
    stem_ref,
    embed_ref,
    out_w_ref,
    out_ref,
    rad_ref,
    win,
    ue,
    uw,
    rstd,
):
    base, band, depth, core = (place_ref[k] for k in range(4))
    bsize, zsize, some, _ = near_ref.shape
    px, lanes = rad_ref.shape
    channels = bands * CH_TOK // bsize
    edge = CH_TOK // 2
    for k, ref in enumerate((near_ref, far_ref)):
        for kz in range(zsize):
            at = ((depth ^ kz) * 2 + (core ^ k)) * some
            pieces = [ref[b ^ band, kz, :, :channels].astype(F32) for b in range(bsize)]
            pieces = [jnp.zeros((some, edge), F32)] + pieces
            pieces.append(jnp.zeros((some, lanes - bands * CH_TOK - edge), F32))
            rad_ref[pl.ds(pl.multiple_of(at, some), some), :] = jnp.concatenate(
                pieces, axis=1
            ).astype(BF16)

    part_px = px // GROUP
    tiles = bands // SPAN
    wstep, ustep = part_px + GAP, px + GAP
    lane = lax.broadcasted_iota(jnp.int32, (px, LANES), 1)
    row = lax.broadcasted_iota(jnp.int32, (px, LANES), 0)
    blocks = [rad_ref[:, j * LANES : (j + 2) * LANES] for j in range(tiles)]

    packed = jnp.concatenate(
        [
            jnp.concatenate([b[i * part_px : (i + 1) * part_px] for i in range(GROUP)], axis=1)
            for b in blocks
        ]
    )
    for i in range(0, SPAN, 2):
        wide = mm(packed, sel_ref[:, i * LANES : (i + 2) * LANES])
        for j in range(tiles):
            for k in range(2):
                t = j * SPAN + i + k
                win[t * wstep : t * wstep + part_px, :] = wide[
                    j * part_px : (j + 1) * part_px, k * LANES : (k + 1) * LANES
                ]
    for t in range(bands, LANES):
        win[t * wstep : t * wstep + part_px, :] = jnp.zeros((part_px, LANES), F32)

    acc = jnp.zeros((px, LANES), F32)
    thin = mm(jnp.concatenate(blocks), sel1_ref[...])
    thin_b = thin.astype(BF16)
    form = mm(thin_b, gram_ref[0]) + mm(thin_b, gram_ref[1])
    for j in range(tiles):
        rows = slice(j * px, (j + 1) * px)
        hi, lo = split2(thin[rows] * (form[rows] + cross_ref[j : j + 1, :]))
        summed = mm(hi, group_ref[...]) + mm(lo, group_ref[...])
        acc = jnp.where(lane // SPAN == j, summed, acc)
    scale = lax.rsqrt(acc + const_ref[:1, :] + 1e-5)
    rstd[...] = scale

    own = []
    for i in range(nb):
        t = base + i
        tile = t // SPAN
        cols = pl.ds(pl.multiple_of(tile * LANES, LANES), 2 * LANES)
        shift = t % SPAN
        at = lax.broadcasted_iota(jnp.int32, (2 * LANES, LANES), 0)
        to = lax.broadcasted_iota(jnp.int32, (2 * LANES, LANES), 1)
        pick = (at == shift * CH_TOK + to % WIN).astype(F32).astype(BF16)
        mine = mm(rad_ref[:, cols], pick).astype(BF16)
        own.append(mine)
        rq = jnp.sum(jnp.where(lane == t, scale, 0.0), axis=1, keepdims=True)
        for h in range(0, HEADS, 2):
            both = slice(2 * h * LANES, 2 * (h + 2) * LANES)
            part = (mm(mine[:, : 2 * WIN], mse_ref[:, both]) + mee_ref[i : i + 1, both]) * rq
            for k in range(2):
                r = ((h + k) * nb + i) * ustep
                ue[r : r + px, :] = part[:, 2 * k * LANES : (2 * k + 1) * LANES]
                uw[r : r + px, :] = jnp.where(
                    lane // WIN == row // part_px,
                    part[:, (2 * k + 1) * LANES : (2 * k + 2) * LANES],
                    0.0,
                )

    rows = HEADS * nb
    step = 4

    def groups(g, _):
        ids = [g * step + k for k in range(step)]
        ws = [win[pl.ds(p, LANES, stride=wstep), :].astype(BF16) for p in ids]
        ls = [
            jnp.concatenate(
                [uw[pl.ds(i * part_px + p, rows, stride=ustep), :] for i in range(GROUP)]
            ).astype(BF16)
            for p in ids
        ]
        ss = [mm_t(a, w) for a, w in zip(ls, ws)]
        es = []
        for k, p in enumerate(ids):
            for i in range(GROUP):
                q = i * part_px + p
                rki = rstd[pl.ds(q, 1), :]
                s = (ss[k][i * rows : (i + 1) * rows] + ue[pl.ds(q, rows, stride=ustep), :]) * rki
                e = jnp.exp2(s - jnp.max(s, axis=1, keepdims=True))
                e = e * (1.0 / jnp.sum(e, axis=1, keepdims=True)) * rki
                ue[pl.ds(q, rows, stride=ustep), :] = e
                es.append(e)
        for k, p in enumerate(ids):
            z = mm(jnp.concatenate(es[k * GROUP : (k + 1) * GROUP]).astype(BF16), ws[k])
            for i in range(GROUP):
                uw[pl.ds(i * part_px + p, rows, stride=ustep), :] = z[i * rows : (i + 1) * rows]
        return 0

    lax.fori_loop(0, part_px // step, groups, 0)

    keep = lane // WIN == row // part_px
    half = lane < LANES // 2
    for i in range(nb):
        mixes = []
        for h in range(0, HEADS, 2):
            outs = []
            for k in range(2):
                r = ((h + k) * nb + i) * ustep
                both = jnp.concatenate(
                    [ue[r : r + px, :], jnp.where(keep, uw[r : r + px, :], 0.0)], axis=1
                ).astype(BF16)
                outs.append(mm(both, av_ref[:, (h + k) * LANES : (h + k + 1) * LANES]))
            mixes.append(jnp.where(half, outs[0], outs[1]).astype(BF16))
        update = mm(jnp.concatenate(mixes, axis=1), out_w_ref[...])
        token = (mm(own[i], stem_ref[...]) + embed_ref[i : i + 1, :]).astype(BF16)
        out_ref[i] = token.astype(F32) + update


def spatial_band(x, gain_ref, qkv_ref, w_ref, proj, mixed):
    pixels, width = x.shape
    cent = x - jnp.mean(x, axis=1, keepdims=True)
    var = jnp.mean(cent * cent, axis=1, keepdims=True)
    normed = (cent * lax.rsqrt(var + 1e-5) * gain_ref[...]).astype(BF16)
    chunk = 6 * width // HEADS
    for c in range(0, 3 * width, chunk):
        proj[:, c : c + chunk] = mm(normed, qkv_ref[:, c : c + chunk]).astype(BF16)
    head = width // HEADS
    low = lax.broadcasted_iota(jnp.int32, (pixels, 2 * head), 1) < head
    for pair in range(HEADS // 2):
        c = pair * 6 * head
        t0 = proj[:, c : c + 2 * head]
        t1 = proj[:, c + 2 * head : c + 4 * head]
        t2 = proj[:, c + 4 * head : c + 6 * head]
        zero = jnp.zeros_like(t0)
        r0 = jnp.concatenate([t0[:, head:], t0[:, :head]], axis=1)
        r2 = jnp.concatenate([t2[:, head:], t2[:, :head]], axis=1)
        outs = []
        for q, k, v in (
            (jnp.where(low, t0, zero), r0, t1),
            (jnp.where(low, zero, t1), r2, t2),
        ):
            s = mm_t(q, k)
            e = jnp.exp((s - jnp.max(s, axis=1, keepdims=True)) * (head**-0.5))
            total = jnp.sum(e, axis=1, keepdims=True)
            outs.append(mm(e.astype(BF16), v) * (1.0 / total))
        mixed[:, pair * 2 * head : (pair + 1) * 2 * head] = jnp.where(
            low, outs[0], outs[1]
        ).astype(BF16)
    return x + mm(mixed[...], w_ref[...])


def spatial_kernel(x_ref, gain_ref, qkv_ref, w_ref, out_ref, proj, mixed):
    out_ref[0] = spatial_band(x_ref[0], gain_ref, qkv_ref, w_ref, proj, mixed).astype(BF16)


def spatial_send_kernel(devices, x_ref, gain_ref, qkv_ref, w_ref, out_ref, proj, mixed, rows):
    b = pl.program_id(0)
    y = spatial_band(x_ref[0], gain_ref, qkv_ref, w_ref, proj, mixed)
    each = y.shape[0] // devices
    rows[:, pl.ds(pl.multiple_of(b * each, each), each), :] = y.reshape(devices, each, y.shape[1])

    @pl.when(b == pl.num_programs(0) - 1)
    def _():
        out_ref[...] = rows[...].astype(BF16)


def spatial(x, gain, qkv, w, first, count, devices):
    nb, pixels, width = x.shape
    each = pixels // devices
    in_specs = [
        pl.BlockSpec((1, pixels, width), lambda i: (first + i, 0, 0)),
        whole_spec((1, width)),
        whole_spec(qkv.shape),
        whole_spec(w.shape),
    ]
    scratch = [pltpu.VMEM((pixels, 3 * width), BF16), pltpu.VMEM((pixels, width), BF16)]
    params = dict(
        grid=(count,),
        in_specs=in_specs,
        compiler_params=pltpu.CompilerParams(vmem_limit_bytes=VMEM_LIMIT),
        cost_estimate=pl.CostEstimate(
            flops=count * 5 * 10**9, bytes_accessed=10 * 2**20, transcendentals=0
        ),
        name="spatial",
    )
    if direct(pixels, devices, count):
        return pl.pallas_call(
            functools.partial(spatial_send_kernel, devices),
            out_shape=jax.ShapeDtypeStruct((devices, count * each, width), BF16),
            out_specs=whole_spec((devices, count * each, width)),
            scratch_shapes=scratch + [pltpu.VMEM((devices, count * each, width), F32)],
            **params,
        )(x, gain[None], qkv, w)
    return pl.pallas_call(
        spatial_kernel,
        out_shape=jax.ShapeDtypeStruct((count, pixels, width), BF16),
        out_specs=pl.BlockSpec((1, pixels, width), lambda i: (i, 0, 0)),
        scratch_shapes=scratch,
        **params,
    )(x, gain[None], qkv, w)


def direct(pixels, devices, count):
    each = pixels // devices
    return each % 8 == 0 and (each * count) % 16 == 0


def gelu(v):
    half = 0.5 * v
    inner = v * ((2 / math.pi) ** 0.5 + (2 / math.pi) ** 0.5 * 0.044715 * (v * v))
    return half + half * jnp.tanh(inner)


def mlp_kernel(run, earlier, x_ref, gain_ref, w_ref, bias_ref, *refs):
    earlier_refs, out_ref, normed, acc = refs[:earlier], refs[earlier], *refs[earlier + 1 : earlier + 3]
    step = pl.program_id(0)
    src, share2, width = w_ref.shape
    share = share2 // 2
    rows = x_ref.shape[0]

    @pl.when(step == 0)
    def _():
        x = x_ref[...].astype(F32)
        cent = x - jnp.mean(x, axis=1, keepdims=True)
        var = jnp.mean(cent * cent, axis=1, keepdims=True)
        normed[...] = (cent * lax.rsqrt(var + 1e-5) * gain_ref[...]).astype(BF16)
        acc[...] = x

    cut = src // 2
    ups = [w_ref[i * cut : (i + 1) * cut, :share, :].reshape(cut * share, width) for i in range(2)]
    downs = [w_ref[i * cut : (i + 1) * cut, share:, :].reshape(cut * share, width) for i in range(2)]
    size = cut * share
    pre = [mm_t(normed[...], u) for u in ups]
    hidden = [gelu(v + bias_ref[0, :, i * size : (i + 1) * size]).astype(BF16) for i, v in enumerate(pre)]
    acc[...] += mm(hidden[0], downs[0]) + mm(hidden[1], downs[1])

    @pl.when(step == pl.num_programs(0) - 1)
    def _():
        if len(out_ref.shape) == 2:
            out_ref[...] = acc[...].astype(BF16)
            return
        lay = refs[-1]
        each, bands, _ = out_ref.shape
        total = bands * each
        parts = earlier + 1
        if parts == 1:
            for c in range(width // LANES):
                lay[c * total : (c + 1) * total, :] = acc[:, c * LANES : (c + 1) * LANES]
        else:
            for p in range(parts):
                part = earlier_refs[p][...].astype(F32) if p < earlier else acc[...]
                for c in range(width // LANES):
                    for i in range(rows // run):
                        to = c * total + (i * parts + p) * run
                        lay[to : to + run, :] = part[
                            i * run : (i + 1) * run, c * LANES : (c + 1) * LANES
                        ]
        for c in range(width // LANES):
            for px in range(each):
                out_ref[px, :, c * LANES : (c + 1) * LANES] = lay[
                    pl.ds(c * total + px, bands, stride=each), :
                ].astype(BF16)


def mlp(x, rows, gain, weights, bias, earlier, run, result):
    devices, share2, width = weights.shape
    hidden = 512
    per = hidden * 2 // share2
    steps = devices // per
    scratch = [pltpu.VMEM((rows, width), BF16), pltpu.VMEM((rows, width), F32)]
    if result is None:
        shape = (rows, width)
    else:
        shape = result
        scratch.append(pltpu.VMEM((math.prod(result) // LANES, LANES), F32))
    return pl.pallas_call(
        functools.partial(mlp_kernel, run, len(earlier)),
        grid=(steps,),
        out_shape=jax.ShapeDtypeStruct(shape, BF16),
        in_specs=[
            pl.BlockSpec((rows, width), lambda i: (0, 0)),
            whole_spec((1, width)),
            pl.BlockSpec((per, share2, width), lambda i: (i, 0, 0)),
            pl.BlockSpec((1, 1, hidden), lambda i: (i, 0, 0)),
        ]
        + [whole_spec(e.shape) for e in earlier],
        out_specs=whole_spec(shape),
        scratch_shapes=scratch,
        compiler_params=pltpu.CompilerParams(vmem_limit_bytes=48 * 2**20),
        cost_estimate=pl.CostEstimate(
            flops=4 * rows * width * share2 * devices // 2, bytes_accessed=20 * 2**20, transcendentals=0
        ),
        name="mlp",
    )(x, gain[None], weights, bias.reshape(steps, 1, hidden), *earlier)


def flip_order(parts, index):
    out = jnp.stack(parts)
    bit = 1
    while bit < len(parts):
        shaped = out.reshape((len(parts) // (2 * bit), 2, bit) + out.shape[1:])
        turned = shaped[:, ::-1].reshape(out.shape)
        out = jnp.where((index // bit) % 2 == 1, turned, out)
        bit *= 2
    return out


def swap(x, axis, mask):
    count = lax.axis_size(axis)
    return lax.ppermute(x, axis, [(i, i ^ mask) for i in range(count)])


def selectors():
    row = np.arange(GROUP * 2 * LANES)[:, None]
    col = np.arange(SPAN * LANES)[None]
    within = row % (2 * LANES)
    sel = (within == (col // LANES) * CH_TOK + col % WIN) & (
        row // (2 * LANES) == col % LANES // WIN
    )
    row = np.arange(2 * LANES)[:, None]
    col = np.arange(SPAN * WIN)[None]
    sel1 = row == (col // WIN) * CH_TOK + col % WIN
    group = row // WIN == np.arange(LANES)[None] % SPAN
    return sel.astype(BF16), sel1.astype(BF16), group.astype(BF16)


def whole_spec(shape):
    return pl.BlockSpec(shape, lambda *_: (0,) * len(shape))


def spectral(place, near, far, tables, own, spec_out, nb, bands):
    bsize, zsize, some, _ = near.shape
    pixels = 2 * zsize * some
    width = spec_out.shape[0]
    lanes = (bands // SPAN + 1) * LANES
    args = [near, far, *selectors(), *tables, own, spec_out]
    part_px = pixels // GROUP
    return pl.pallas_call(
        functools.partial(spectral_kernel, nb, bands),
        out_shape=jax.ShapeDtypeStruct((nb, pixels, width), F32),
        in_specs=[pl.BlockSpec(memory_space=pltpu.SMEM)]
        + [pl.BlockSpec(memory_space=pltpu.VMEM)] * len(args),
        out_specs=pl.BlockSpec(memory_space=pltpu.VMEM),
        scratch_shapes=[
            pltpu.VMEM((pixels, lanes), BF16),
            pltpu.VMEM((LANES * (part_px + GAP), LANES), F32),
            pltpu.VMEM((HEADS * nb * (pixels + GAP), LANES), F32),
            pltpu.VMEM((HEADS * nb * (pixels + GAP), LANES), F32),
            pltpu.VMEM((pixels, LANES), F32),
        ],
        compiler_params=pltpu.CompilerParams(vmem_limit_bytes=48 * 2**20),
        cost_estimate=pl.CostEstimate(
            flops=12 * 10**9, bytes_accessed=12 * 2**20, transcendentals=0
        ),
        name="spectral",
    )(place, *args)


def local(
    radiance,
    stem_weight,
    band_embed,
    norm_spectral,
    spec_qkv,
    spec_out,
    norm_spatial,
    spat_qkv,
    spat_out,
    norm_mlp,
    up_weight,
    up_bias,
    down_weight,
):
    bands, width = band_embed.shape
    bsize, psize = lax.axis_size("band"), lax.axis_size("pix")
    devices = bsize * psize
    nb = -(-bands // devices)
    band, pix = lax.axis_index("band"), lax.axis_index("pix")
    base = jnp.minimum((pix * bsize + band) * nb, bands - nb).astype(jnp.int32)

    share = up_weight.shape[0] // bsize
    both = jnp.concatenate(
        [
            lax.dynamic_slice_in_dim(up_weight, band * share, share, 0),
            lax.dynamic_slice_in_dim(down_weight, band * share, share, 0),
        ]
    )
    weights = lax.all_gather(both, ("pix", "band"), axis=0)

    rows, channels = radiance.shape
    message = jnp.concatenate([radiance.astype(BF16), up_bias.reshape(rows, -1)], axis=1)
    zs = jnp.stack([message] + [swap(message, "pix", 2 * k) for k in range(1, psize // 2)])
    zs, stem_weight = lax.optimization_barrier((zs, stem_weight))
    near = jnp.stack([zs] + [swap(zs, "band", k) for k in range(1, bsize)])
    far = swap(near, "pix", 1)
    bias = jnp.stack([near[0, :, :, channels:], far[0, :, :, channels:]])
    bias = flip_order(list(flip_order(list(bias.swapaxes(0, 1)), pix // 2).swapaxes(0, 1)), pix % 2)
    bias = bias.swapaxes(0, 1).astype(F32)

    own = lax.dynamic_slice_in_dim(band_embed, base, nb, 0)
    tables = make_tables(stem_weight, band_embed, own, norm_spectral, spec_qkv)
    place = jnp.stack([base, band, pix // 2, pix % 2]).astype(jnp.int32)
    after_spectral = spectral(place, near, far, tables, own, spec_out, nb, bands)
    pixels = after_spectral.shape[1]
    each = pixels // devices
    count = nb // 2 if nb % 2 == 0 and direct(pixels, devices, nb // 2) else nb
    results = []
    for first in range(0, nb, count):
        part = spatial(after_spectral, norm_spatial, spat_qkv, spat_out, first, count, devices)
        if direct(pixels, devices, count):
            moved = lax.all_to_all(part, ("pix", "band"), split_axis=0, concat_axis=0, tiled=True)
        else:
            moved = lax.all_to_all(part, ("pix", "band"), split_axis=1, concat_axis=0, tiled=True)
        moved = moved.reshape(-1, width)
        run = count * each
        last = first + count == nb
        results.append(
            mlp(
                moved,
                bands // nb * run,
                norm_mlp,
                weights,
                bias,
                results if last else [],
                run,
                (each, bands, width) if last else None,
            )
        )
    return results[-1]


def solution(mesh):
    placed = (
        P("pix", "band"),
        P(),
        P(),
        P(),
        P(),
        P(),
        P(),
        P(),
        P(),
        P(),
        P("pix", None),
        P("pix"),
        P("pix", None),
    )
    return jax.shard_map(
        local, mesh=mesh, in_specs=placed, out_specs=P(("pix", "band"), None, None), check_vma=False
    )
```

```python
import functools
import math

import jax
import jax.numpy as jnp
import numpy as np
from jax import lax
from jax.experimental import pallas as pl
from jax.experimental.pallas import tpu as pltpu
from jax.sharding import PartitionSpec as P

HEADS = 16
CH_TOK = 16
WIN = 2 * CH_TOK
LANES = 128
GROUP = LANES // WIN
SPAN = LANES // CH_TOK
GAP = 8
F32 = jnp.float32
BF16 = jnp.bfloat16
HIGH = lax.Precision.HIGHEST
LOG2_E = math.log2(math.e)
VMEM_LIMIT = 60 * 2**20


def mm(a, b):
    return jnp.dot(a, b, preferred_element_type=F32)


def mm_t(a, b):
    return lax.dot_general(a, b, (((1,), (1,)), ((), ())), preferred_element_type=F32)


def split2(x):
    hi = x.astype(BF16)
    return hi, (x - hi.astype(F32)).astype(BF16)


def mm_exact(a, b):
    return lax.dot_general(
        a, b, (((1,), (1,)), ((), ())), precision=HIGH, preferred_element_type=F32
    )


def tables_kernel(
    bands,
    stem_ref,
    embed_ref,
    own_ref,
    gain_ref,
    qkv_ref,
    mse_ref,
    mee_ref,
    av_ref,
    gram_ref,
    cross_ref,
    const_ref,
    pieces_ref,
    feats,
):
    @pl.when(pl.program_id(0) == 0)
    def _():
        def centred(x):
            return x - jnp.mean(x, axis=1, keepdims=True)

        gain = gain_ref[...]
        stem = centred(stem_ref[...])
        width = stem.shape[1]
        blank = jnp.zeros((LANES - bands, width), F32)
        embed = jnp.concatenate([centred(embed_ref[...]), blank])
        stem_g = stem * gain
        tail = jnp.zeros((8, width), F32)
        feats[...] = jnp.concatenate(
            [embed * gain] + [stem_g] * GROUP + [centred(own_ref[...]) * gain, tail]
        ).astype(BF16)

        many = jnp.concatenate([stem] * SPAN)
        shape = (SPAN * WIN, SPAN * WIN)
        same = (
            lax.broadcasted_iota(jnp.int32, shape, 0) // WIN
            == lax.broadcasted_iota(jnp.int32, shape, 1) // WIN
        )
        gram = jnp.where(same, mm_exact(many, many) * (1.0 / width), 0.0)
        gram_ref[0], gram_ref[1] = split2(gram)
        shape = (LANES, SPAN * WIN)
        same = (
            lax.broadcasted_iota(jnp.int32, shape, 0) % SPAN
            == lax.broadcasted_iota(jnp.int32, shape, 1) // WIN
        )
        cross = jnp.where(same, mm_exact(embed, many) * (2.0 / width), 0.0)
        cross_ref[...] = jnp.sum(cross.reshape(LANES // SPAN, SPAN, SPAN * WIN), axis=1)
        const_ref[...] = mm_exact(jnp.ones((8, width), F32), embed * embed) * (1.0 / width)

        rest = stem_ref[...]
        pieces = []
        for _ in range(3):
            hi = rest.astype(BF16).astype(F32)
            pieces.append(hi)
            rest = rest - hi
        pieces_ref[...] = jnp.concatenate(pieces + [jnp.zeros_like(rest)]).astype(BF16)

    a = mm(feats[...], qkv_ref[...]).astype(BF16)
    head = a.shape[1] // 6
    keys = 2 * LANES
    scale = head**-0.5 * LOG2_E
    beyond = lax.broadcasted_iota(jnp.int32, (8, keys), 1)
    beyond = (beyond >= bands) & (beyond < LANES)
    for i in range(2):
        c = 3 * i * head
        q = a[:, c : c + head]
        k = a[:keys, c + head : c + 2 * head]
        m = mm_t(q[LANES : LANES + WIN], k) * scale
        hi, lo = split2(m)
        mse_ref[:WIN, i * keys : (i + 1) * keys] = hi
        mse_ref[WIN:, i * keys : (i + 1) * keys] = lo
        m = mm_t(q[keys : keys + 16], k)[:8] * scale
        mee_ref[:, i * keys : (i + 1) * keys] = jnp.where(beyond, -1e30, m)
    av_ref[...] = a[:keys, 2 * head :]


def make_tables(stem_weight, band_embed, own, gain, qkv):
    bands, width = band_embed.shape
    own8 = jnp.pad(own, ((0, 8 - own.shape[0]), (0, 0)))
    steps = HEADS // 2
    cols = qkv.shape[1] // steps
    square = SPAN * WIN
    fixed = [
        jax.ShapeDtypeStruct((2, square, square), BF16),
        jax.ShapeDtypeStruct((LANES // SPAN, square), F32),
        jax.ShapeDtypeStruct((8, LANES), F32),
        jax.ShapeDtypeStruct((LANES, width), BF16),
    ]
    return pl.pallas_call(
        functools.partial(tables_kernel, bands),
        grid=(steps,),
        out_shape=[
            jax.ShapeDtypeStruct((2 * WIN, HEADS * 2 * LANES), BF16),
            jax.ShapeDtypeStruct((8, HEADS * 2 * LANES), F32),
            jax.ShapeDtypeStruct((2 * LANES, steps * cols * 2 // 3), BF16),
        ]
        + fixed,
        in_specs=[
            whole_spec(stem_weight.shape),
            whole_spec(band_embed.shape),
            whole_spec(own8.shape),
            whole_spec((1, width)),
            pl.BlockSpec((width, cols), lambda i: (0, i)),
        ],
        out_specs=[
            pl.BlockSpec((2 * WIN, 4 * LANES), lambda i: (0, i)),
            pl.BlockSpec((8, 4 * LANES), lambda i: (0, i)),
            pl.BlockSpec((2 * LANES, cols * 2 // 3), lambda i: (0, i)),
        ]
        + [whole_spec(f.shape) for f in fixed],
        scratch_shapes=[pltpu.VMEM((2 * LANES + 16, width), BF16)],
        compiler_params=pltpu.CompilerParams(vmem_limit_bytes=32 * 2**20),
        cost_estimate=pl.CostEstimate(flops=4 * 10**9, bytes_accessed=8 * 2**20, transcendentals=0),
        name="tables",
    )(stem_weight, band_embed, own8, gain[None], qkv)


def spectral_kernel(
    nb,
    bands,
    place_ref,
    near_ref,
    far_ref,
    sel_ref,
    sel1_ref,
    group_ref,
    mse_ref,
    mee_ref,
    av_ref,
    gram_ref,
    cross_ref,
    const_ref,
    stem_ref,
    embed_ref,
    out_w_ref,
    out_ref,
    rad_ref,
    win,
    ue,
    uw,
    rstd,
):
    base, band, depth, core = (place_ref[k] for k in range(4))
    bsize, zsize, some, _ = near_ref.shape
    px, lanes = rad_ref.shape
    channels = bands * CH_TOK // bsize
    edge = CH_TOK // 2
    for k, ref in enumerate((near_ref, far_ref)):
        for kz in range(zsize):
            at = ((depth ^ kz) * 2 + (core ^ k)) * some
            pieces = [ref[b ^ band, kz, :, :channels].astype(F32) for b in range(bsize)]
            pieces = [jnp.zeros((some, edge), F32)] + pieces
            pieces.append(jnp.zeros((some, lanes - bands * CH_TOK - edge), F32))
            rad_ref[pl.ds(pl.multiple_of(at, some), some), :] = jnp.concatenate(
                pieces, axis=1
            ).astype(BF16)

    part_px = px // GROUP
    tiles = bands // SPAN
    wstep, ustep = part_px + GAP, px + GAP
    lane = lax.broadcasted_iota(jnp.int32, (px, LANES), 1)
    row = lax.broadcasted_iota(jnp.int32, (px, LANES), 0)
    blocks = [rad_ref[:, j * LANES : (j + 2) * LANES] for j in range(tiles)]

    packed = jnp.concatenate(
        [
            jnp.concatenate([b[i * part_px : (i + 1) * part_px] for i in range(GROUP)], axis=1)
            for b in blocks
        ]
    )
    for i in range(0, SPAN, 2):
        wide = mm(packed, sel_ref[:, i * LANES : (i + 2) * LANES])
        for j in range(tiles):
            for k in range(2):
                t = j * SPAN + i + k
                win[t * wstep : t * wstep + part_px, :] = wide[
                    j * part_px : (j + 1) * part_px, k * LANES : (k + 1) * LANES
                ]
    for t in range(bands, LANES):
        win[t * wstep : t * wstep + part_px, :] = jnp.zeros((part_px, LANES), F32)

    acc = jnp.zeros((px, LANES), F32)
    thin = mm(jnp.concatenate(blocks), sel1_ref[...])
    thin_b = thin.astype(BF16)
    form = mm(thin_b, gram_ref[0]) + mm(thin_b, gram_ref[1])
    for j in range(tiles):
        rows = slice(j * px, (j + 1) * px)
        hi, lo = split2(thin[rows] * (form[rows] + cross_ref[j : j + 1, :]))
        summed = mm(hi, group_ref[...]) + mm(lo, group_ref[...])
        acc = jnp.where(lane // SPAN == j, summed, acc)
    scale = lax.rsqrt(acc + const_ref[:1, :] + 1e-5)
    rstd[...] = scale

    own = []
    for i in range(nb):
        t = base + i
        tile = t // SPAN
        cols = pl.ds(pl.multiple_of(tile * LANES, LANES), 2 * LANES)
        shift = t % SPAN
        at = lax.broadcasted_iota(jnp.int32, (2 * LANES, LANES), 0)
        to = lax.broadcasted_iota(jnp.int32, (2 * LANES, LANES), 1)
        pick = (at == shift * CH_TOK + to % WIN).astype(F32).astype(BF16)
        mine = mm(rad_ref[:, cols], pick).astype(BF16)
        own.append(mine)
        rq = jnp.sum(jnp.where(lane == t, scale, 0.0), axis=1, keepdims=True)
        for h in range(0, HEADS, 2):
            both = slice(2 * h * LANES, 2 * (h + 2) * LANES)
            part = (mm(mine[:, : 2 * WIN], mse_ref[:, both]) + mee_ref[i : i + 1, both]) * rq
            for k in range(2):
                r = ((h + k) * nb + i) * ustep
                ue[r : r + px, :] = part[:, 2 * k * LANES : (2 * k + 1) * LANES]
                uw[r : r + px, :] = jnp.where(
                    lane // WIN == row // part_px,
                    part[:, (2 * k + 1) * LANES : (2 * k + 2) * LANES],
                    0.0,
                )

    rows = HEADS * nb
    step = 4

    def groups(g, _):
        ids = [g * step + k for k in range(step)]
        ws = [win[pl.ds(p, LANES, stride=wstep), :].astype(BF16) for p in ids]
        ls = [
            jnp.concatenate(
                [uw[pl.ds(i * part_px + p, rows, stride=ustep), :] for i in range(GROUP)]
            ).astype(BF16)
            for p in ids
        ]
        ss = [mm_t(a, w) for a, w in zip(ls, ws)]
        es = []
        for k, p in enumerate(ids):
            for i in range(GROUP):
                q = i * part_px + p
                rki = rstd[pl.ds(q, 1), :]
                s = (ss[k][i * rows : (i + 1) * rows] + ue[pl.ds(q, rows, stride=ustep), :]) * rki
                e = jnp.exp2(s - jnp.max(s, axis=1, keepdims=True))
                e = e * (1.0 / jnp.sum(e, axis=1, keepdims=True)) * rki
                ue[pl.ds(q, rows, stride=ustep), :] = e
                es.append(e)
        for k, p in enumerate(ids):
            z = mm(jnp.concatenate(es[k * GROUP : (k + 1) * GROUP]).astype(BF16), ws[k])
            for i in range(GROUP):
                uw[pl.ds(i * part_px + p, rows, stride=ustep), :] = z[i * rows : (i + 1) * rows]
        return 0

    lax.fori_loop(0, part_px // step, groups, 0)

    keep = lane // WIN == row // part_px
    half = lane < LANES // 2
    for i in range(nb):
        mixes = []
        for h in range(0, HEADS, 2):
            outs = []
            for k in range(2):
                r = ((h + k) * nb + i) * ustep
                both = jnp.concatenate(
                    [ue[r : r + px, :], jnp.where(keep, uw[r : r + px, :], 0.0)], axis=1
                ).astype(BF16)
                outs.append(mm(both, av_ref[:, (h + k) * LANES : (h + k + 1) * LANES]))
            mixes.append(jnp.where(half, outs[0], outs[1]).astype(BF16))
        update = mm(jnp.concatenate(mixes, axis=1), out_w_ref[...])
        token = (mm(own[i], stem_ref[...]) + embed_ref[i : i + 1, :]).astype(BF16)
        out_ref[i] = token.astype(F32) + update


def spatial_band(x, gain_ref, qkv_ref, w_ref, proj, mixed):
    pixels, width = x.shape
    cent = x - jnp.mean(x, axis=1, keepdims=True)
    var = jnp.mean(cent * cent, axis=1, keepdims=True)
    normed = (cent * lax.rsqrt(var + 1e-5) * gain_ref[...]).astype(BF16)
    chunk = 6 * width // HEADS
    for c in range(0, 3 * width, chunk):
        proj[:, c : c + chunk] = mm(normed, qkv_ref[:, c : c + chunk]).astype(BF16)
    head = width // HEADS
    low = lax.broadcasted_iota(jnp.int32, (pixels, 2 * head), 1) < head
    for pair in range(HEADS // 2):
        c = pair * 6 * head
        t0 = proj[:, c : c + 2 * head]
        t1 = proj[:, c + 2 * head : c + 4 * head]
        t2 = proj[:, c + 4 * head : c + 6 * head]
        zero = jnp.zeros_like(t0)
        r0 = jnp.concatenate([t0[:, head:], t0[:, :head]], axis=1)
        r2 = jnp.concatenate([t2[:, head:], t2[:, :head]], axis=1)
        outs = []
        for q, k, v in (
            (jnp.where(low, t0, zero), r0, t1),
            (jnp.where(low, zero, t1), r2, t2),
        ):
            s = mm_t(q, k)
            e = jnp.exp((s - jnp.max(s, axis=1, keepdims=True)) * (head**-0.5))
            total = jnp.sum(e, axis=1, keepdims=True)
            outs.append(mm(e.astype(BF16), v) * (1.0 / total))
        mixed[:, pair * 2 * head : (pair + 1) * 2 * head] = jnp.where(
            low, outs[0], outs[1]
        ).astype(BF16)
    return x + mm(mixed[...], w_ref[...])


def spatial_kernel(x_ref, gain_ref, qkv_ref, w_ref, out_ref, proj, mixed):
    out_ref[0] = spatial_band(x_ref[0], gain_ref, qkv_ref, w_ref, proj, mixed).astype(BF16)


def spatial_send_kernel(devices, x_ref, gain_ref, qkv_ref, w_ref, out_ref, proj, mixed, rows):
    b = pl.program_id(0)
    y = spatial_band(x_ref[0], gain_ref, qkv_ref, w_ref, proj, mixed)
    each = y.shape[0] // devices
    rows[:, pl.ds(pl.multiple_of(b * each, each), each), :] = y.reshape(devices, each, y.shape[1])

    @pl.when(b == pl.num_programs(0) - 1)
    def _():
        out_ref[...] = rows[...].astype(BF16)


def spatial(x, gain, qkv, w, first, count, devices):
    nb, pixels, width = x.shape
    each = pixels // devices
    in_specs = [
        pl.BlockSpec((1, pixels, width), lambda i: (first + i, 0, 0)),
        whole_spec((1, width)),
        whole_spec(qkv.shape),
        whole_spec(w.shape),
    ]
    scratch = [pltpu.VMEM((pixels, 3 * width), BF16), pltpu.VMEM((pixels, width), BF16)]
    params = dict(
        grid=(count,),
        in_specs=in_specs,
        compiler_params=pltpu.CompilerParams(vmem_limit_bytes=VMEM_LIMIT),
        cost_estimate=pl.CostEstimate(
            flops=count * 5 * 10**9, bytes_accessed=10 * 2**20, transcendentals=0
        ),
        name="spatial",
    )
    if direct(pixels, devices, count):
        return pl.pallas_call(
            functools.partial(spatial_send_kernel, devices),
            out_shape=jax.ShapeDtypeStruct((devices, count * each, width), BF16),
            out_specs=whole_spec((devices, count * each, width)),
            scratch_shapes=scratch + [pltpu.VMEM((devices, count * each, width), F32)],
            **params,
        )(x, gain[None], qkv, w)
    return pl.pallas_call(
        spatial_kernel,
        out_shape=jax.ShapeDtypeStruct((count, pixels, width), BF16),
        out_specs=pl.BlockSpec((1, pixels, width), lambda i: (i, 0, 0)),
        scratch_shapes=scratch,
        **params,
    )(x, gain[None], qkv, w)


def direct(pixels, devices, count):
    each = pixels // devices
    return each % 8 == 0 and (each * count) % 16 == 0


def gelu(v):
    half = 0.5 * v
    inner = v * ((2 / math.pi) ** 0.5 + (2 / math.pi) ** 0.5 * 0.044715 * (v * v))
    return half + half * jnp.tanh(inner)


def mlp_kernel(run, earlier, orders, counts, place_ref, x_ref, gain_ref, bias_ref, *refs):
    n_weights = 4 + 2 * len(counts)
    weight_refs, refs = refs[:n_weights], refs[n_weights:]
    earlier_refs, refs = refs[:earlier], refs[earlier:]
    out_ref, normed, acc, buf, sems, *rest = refs
    band, depth = place_ref[1], place_ref[2]
    rows, width = normed.shape
    zsize, groups = bias_ref.shape[1], bias_ref.shape[2]
    half = bias_ref.shape[4]
    size = groups * half
    natural = [(i, None) for i in range(groups)]
    mixed = [(m, 0) for m in orders[0]] + [(m, 1) for m in orders[1]]

    blocks = []
    for c in range(2):
        up, down = weight_refs[2 * c], weight_refs[2 * c + 1]
        blocks.append(([(up, 0, size, 0), (down, 0, size, size)], c, 0, natural))
    k = 1
    for j, count in enumerate(counts):
        for i in range(count):
            for c in range(2):
                ref = weight_refs[4 + 2 * j + c]
                blocks.append(([(ref, i * 2 * size, 2 * size, 0)], c, k, mixed))
            k += 1

    def copies(n):
        slot = n % buf.shape[0]
        return [
            pltpu.make_async_copy(
                ref.at[pl.ds(first, count), :],
                buf.at[slot, pl.ds(to, count), :],
                sems.at[slot, i],
            )
            for i, (ref, first, count, to) in enumerate(blocks[n][0])
        ]

    ahead = buf.shape[0] - 1
    for n in range(ahead):
        for copy in copies(n):
            copy.start()

    x = x_ref[:rows, :].astype(F32)
    cent = x - jnp.mean(x, axis=1, keepdims=True)
    var = jnp.mean(cent * cent, axis=1, keepdims=True)
    normed[...] = (cent * lax.rsqrt(var + 1e-5) * gain_ref[...]).astype(BF16)
    acc[...] = x

    for n, (_, c, k, order) in enumerate(blocks):
        for copy in copies(n):
            copy.wait()
        if n + ahead < len(blocks):
            for copy in copies(n + ahead):
                copy.start()
        slot = n % buf.shape[0]
        kz = depth ^ lax.rem(depth - k + zsize, zsize)
        bias = []
        for m, h in order:
            at = m if h is None else (band ^ m) * 2 + h
            bias.append(bias_ref[c, kz, at])
        total = None
        hidden = []
        for part in range(2):
            ids = range(part * groups // 2, (part + 1) * groups // 2)
            if order is natural:
                up = buf[slot, ids[0] * half : ids[0] * half + size // 2, :]
            else:
                up = jnp.concatenate([buf[slot, 2 * g * half : (2 * g + 1) * half, :] for g in ids])
            v = mm_t(normed[...], up) + jnp.concatenate([bias[g] for g in ids], axis=1)
            hidden.append(gelu(v).astype(BF16))
        for part in range(2):
            ids = range(part * groups // 2, (part + 1) * groups // 2)
            if order is natural:
                down = buf[slot, size + ids[0] * half : size + ids[0] * half + size // 2, :]
            else:
                down = jnp.concatenate(
                    [buf[slot, (2 * g + 1) * half : (2 * g + 2) * half, :] for g in ids]
                )
            piece = mm(hidden[part], down)
            total = piece if total is None else total + piece
        acc[...] += total

    if len(out_ref.shape) == 2:
        out_ref[...] = acc[...].astype(BF16)
        return
    lay = rest[0]
    each, bands, _ = out_ref.shape
    whole = bands * each
    parts = earlier + 1
    for p in range(parts):
        part = earlier_refs[p] if p < earlier else acc
        for c in range(width // LANES):
            cols = slice(c * LANES, (c + 1) * LANES)
            if parts == 1:
                lay[c * whole : (c + 1) * whole, :] = part[:, cols]
                continue
            for i in range(rows // run):
                to = c * whole + (i * parts + p) * run
                lay[to : to + run, :] = part[i * run : (i + 1) * run, cols].astype(F32)
    for c in range(width // LANES):
        for px in range(each):
            out_ref[px, :, c * LANES : (c + 1) * LANES] = lay[
                pl.ds(c * whole + px, bands, stride=each), :
            ].astype(BF16)


def mlp(place, x, rows, gain, bias, own, gathered, orders, earlier, run, result):
    width = x.shape[1]
    size = own[0].shape[0]
    counts = tuple(g.shape[0] // (2 * size) for g in gathered[::2])
    scratch = [
        pltpu.VMEM((rows, width), BF16),
        pltpu.VMEM((rows, width), F32),
        pltpu.VMEM((3, 2 * size, width), BF16),
        pltpu.SemaphoreType.DMA((3, 2)),
    ]
    if result is None:
        shape = (rows, width)
    else:
        shape = result
        scratch.append(pltpu.VMEM((math.prod(result) // LANES, LANES), F32))
    vmem = pl.BlockSpec(memory_space=pltpu.VMEM)
    return pl.pallas_call(
        functools.partial(mlp_kernel, run, len(earlier), orders, counts),
        out_shape=jax.ShapeDtypeStruct(shape, BF16),
        in_specs=[pl.BlockSpec(memory_space=pltpu.SMEM), vmem, vmem, vmem]
        + [pl.BlockSpec(memory_space=pl.ANY)] * (4 + len(gathered))
        + [vmem] * len(earlier),
        out_specs=vmem,
        scratch_shapes=scratch,
        compiler_params=pltpu.CompilerParams(vmem_limit_bytes=48 * 2**20),
        cost_estimate=pl.CostEstimate(
            flops=4 * rows * width * 4096, bytes_accessed=20 * 2**20, transcendentals=0
        ),
        name="mlp",
    )(place, x, gain[None], bias, *own, *gathered, *earlier)


def swap(x, axis, mask):
    count = lax.axis_size(axis)
    return lax.ppermute(x, axis, [(i, i ^ mask) for i in range(count)])


def selectors():
    row = np.arange(GROUP * 2 * LANES)[:, None]
    col = np.arange(SPAN * LANES)[None]
    within = row % (2 * LANES)
    sel = (within == (col // LANES) * CH_TOK + col % WIN) & (
        row // (2 * LANES) == col % LANES // WIN
    )
    row = np.arange(2 * LANES)[:, None]
    col = np.arange(SPAN * WIN)[None]
    sel1 = row == (col // WIN) * CH_TOK + col % WIN
    group = row // WIN == np.arange(LANES)[None] % SPAN
    return sel.astype(BF16), sel1.astype(BF16), group.astype(BF16)


def whole_spec(shape):
    return pl.BlockSpec(shape, lambda *_: (0,) * len(shape))


def spectral(place, near, far, tables, own, spec_out, nb, bands):
    bsize, zsize, some, _ = near.shape
    pixels = 2 * zsize * some
    width = spec_out.shape[0]
    lanes = (bands // SPAN + 1) * LANES
    args = [near, far, *selectors(), *tables, own, spec_out]
    part_px = pixels // GROUP
    return pl.pallas_call(
        functools.partial(spectral_kernel, nb, bands),
        out_shape=jax.ShapeDtypeStruct((nb, pixels, width), F32),
        in_specs=[pl.BlockSpec(memory_space=pltpu.SMEM)]
        + [pl.BlockSpec(memory_space=pltpu.VMEM)] * len(args),
        out_specs=pl.BlockSpec(memory_space=pltpu.VMEM),
        scratch_shapes=[
            pltpu.VMEM((pixels, lanes), BF16),
            pltpu.VMEM((LANES * (part_px + GAP), LANES), F32),
            pltpu.VMEM((HEADS * nb * (pixels + GAP), LANES), F32),
            pltpu.VMEM((HEADS * nb * (pixels + GAP), LANES), F32),
            pltpu.VMEM((pixels, LANES), F32),
        ],
        compiler_params=pltpu.CompilerParams(vmem_limit_bytes=48 * 2**20),
        cost_estimate=pl.CostEstimate(
            flops=12 * 10**9, bytes_accessed=12 * 2**20, transcendentals=0
        ),
        name="spectral",
    )(place, *args)


def local(
    radiance,
    stem_weight,
    band_embed,
    norm_spectral,
    spec_qkv,
    spec_out,
    norm_spatial,
    spat_qkv,
    spat_out,
    norm_mlp,
    up_weight,
    up_bias,
    down_weight,
):
    bands, width = band_embed.shape
    bsize, psize = lax.axis_size("band"), lax.axis_size("pix")
    devices = bsize * psize
    nb = -(-bands // devices)
    band, pix = lax.axis_index("band"), lax.axis_index("pix")
    base = jnp.minimum((pix * bsize + band) * nb, bands - nb).astype(jnp.int32)

    rows, channels = radiance.shape
    message = jnp.concatenate([radiance.astype(BF16), up_bias.reshape(rows, -1)], axis=1)
    message, up_weight, down_weight = lax.optimization_barrier((message, up_weight, down_weight))
    own_weights = [up_weight, down_weight, swap(up_weight, "pix", 1), swap(down_weight, "pix", 1)]

    half = up_weight.shape[0] // bsize // 2
    bits = [1 << i for i in range(bsize.bit_length() - 1)]
    bit_orders = (bits, bits[::-1])
    orders = []
    for order in bit_orders:
        ids = [0]
        for bit in order:
            ids = ids + [i ^ bit for i in ids]
        orders.append(tuple(ids))
    share = []
    for h in range(2):
        at = (band * 2 + h) * half
        share.append(
            jnp.concatenate(
                [lax.dynamic_slice_in_dim(w, at, half, 0) for w in (up_weight, down_weight)]
            )
        )
    ring = [(i, (i + 2) % psize) for i in range(psize)]

    def step_ring(x):
        return lax.ppermute(x, "pix", ring)

    def halves(chunks, h):
        return jnp.concatenate([c[h * 2 * half : (h + 1) * 2 * half] for c in chunks])

    def first_bit(chunks):
        out = []
        for h, order in enumerate(bit_orders):
            mine = halves(chunks, h)
            out.append((mine, swap(mine, "band", order[0]) if order else None))
        return out

    def other_bits(pairs, count):
        done = []
        for (mine, other), order in zip(pairs, bit_orders):
            held = [x.reshape(count, 1, 2 * half, -1) for x in (mine, other) if x is not None]
            held = jnp.concatenate(held, axis=1)
            for bit in order[1:]:
                held = jnp.concatenate([held, swap(held, "band", bit)], axis=1)
            done.append(held)
        return jnp.concatenate(done, axis=1).reshape(count * bsize * 4 * half, -1)

    zs = jnp.stack([message] + [swap(message, "pix", 2 * k) for k in range(1, psize // 2)])
    ring_1 = step_ring(jnp.concatenate(share))
    zs, ring_1, stem_weight = lax.optimization_barrier((zs, ring_1, stem_weight))
    near = jnp.stack([zs] + [swap(zs, "band", k) for k in range(1, bsize)])
    ring_2 = step_ring(ring_1)
    pairs_1 = first_bit([ring_1])
    own = lax.dynamic_slice_in_dim(band_embed, base, nb, 0)
    tables = make_tables(stem_weight, band_embed, own, norm_spectral, spec_qkv)
    near, tables = lax.optimization_barrier((near, tables))
    far = swap(near, "pix", 1)
    place = jnp.stack([base, band, pix // 2, pix % 2]).astype(jnp.int32)
    far, ring_2, pairs_1 = lax.optimization_barrier((far, ring_2, pairs_1))
    rings = [ring_2]
    for _ in range(psize // 2 - 3):
        rings.append(step_ring(rings[-1]))
    whole_1 = other_bits(pairs_1, 1)
    after_spectral = spectral(place, near, far, tables, own, spec_out, nb, bands)
    after_spectral, rings, whole_1 = lax.optimization_barrier((after_spectral, rings, whole_1))
    gathered = [whole_1, swap(whole_1, "pix", 1)]
    pairs_2 = first_bit(rings)
    bias = jnp.stack([near[0, :, :, channels:], far[0, :, :, channels:]])
    bias = bias.reshape(2, psize // 2, 2 * bsize, 1, half).astype(F32)
    pixels = after_spectral.shape[1]
    each = pixels // devices
    count = nb // 2 if nb % 2 == 0 and direct(pixels, devices, nb // 2) else nb
    arrived, results = [], []
    for first in range(0, nb, count):
        part = spatial(after_spectral, norm_spatial, spat_qkv, spat_out, first, count, devices)
        if first == 0:
            part, pairs_2 = lax.optimization_barrier((part, pairs_2))
            whole_2 = other_bits(pairs_2, len(rings))
        if first + count == nb:
            part, whole_2 = lax.optimization_barrier((part, whole_2))
            gathered += [whole_2, swap(whole_2, "pix", 1)]
        if direct(pixels, devices, count):
            moved = lax.all_to_all(part, ("pix", "band"), split_axis=0, concat_axis=0, tiled=True)
        else:
            moved = lax.all_to_all(part, ("pix", "band"), split_axis=1, concat_axis=0, tiled=True)
        arrived.append(moved.reshape(-1, width))
    run = count * each
    for i, moved in enumerate(arrived):
        last = i == len(arrived) - 1
        results.append(
            mlp(
                place,
                moved,
                bands // nb * run,
                norm_mlp,
                bias,
                own_weights,
                gathered,
                tuple(orders),
                results if last else [],
                run,
                (each, bands, width) if last else None,
            )
        )
    return results[-1]


def solution(mesh):
    placed = (
        P("pix", "band"),
        P(),
        P(),
        P(),
        P(),
        P(),
        P(),
        P(),
        P(),
        P(),
        P("pix", None),
        P("pix"),
        P("pix", None),
    )
    return jax.shard_map(
        local, mesh=mesh, in_specs=placed, out_specs=P(("pix", "band"), None, None), check_vma=False
    )
```

```python
import functools
import math

import jax
import jax.numpy as jnp
import numpy as np
from jax import lax
from jax.experimental import pallas as pl
from jax.experimental.pallas import tpu as pltpu
from jax.sharding import PartitionSpec as P

HEADS = 16
CH_TOK = 16
WIN = 2 * CH_TOK
LANES = 128
GROUP = LANES // WIN
SPAN = LANES // CH_TOK
GAP = 8
F32 = jnp.float32
BF16 = jnp.bfloat16
HIGH = lax.Precision.HIGHEST
LOG2_E = math.log2(math.e)
VMEM_LIMIT = 60 * 2**20


def takes(us):
    return pl.CostEstimate(flops=us * 10**9, bytes_accessed=2**20, transcendentals=0)


def mm(a, b):
    return jnp.dot(a, b, preferred_element_type=F32)


def mm_t(a, b):
    return lax.dot_general(a, b, (((1,), (1,)), ((), ())), preferred_element_type=F32)


def split2(x):
    hi = x.astype(BF16)
    return hi, (x - hi.astype(F32)).astype(BF16)


def mm_exact(a, b):
    return lax.dot_general(
        a, b, (((1,), (1,)), ((), ())), precision=HIGH, preferred_element_type=F32
    )


def feature_kernel(
    stem_ref, embed_ref, own_ref, gain_ref, feats_ref, gram_ref, cross_ref, const_ref, pieces_ref
):
    def centred(x):
        return x - jnp.mean(x, axis=1, keepdims=True)

    gain = gain_ref[...]
    stem = centred(stem_ref[...])
    bands, width = embed_ref.shape
    blank = jnp.zeros((LANES - bands, width), F32)
    embed = jnp.concatenate([centred(embed_ref[...]), blank])
    stem_g = stem * gain
    tail = jnp.zeros((8, width), F32)
    feats_ref[...] = jnp.concatenate(
        [embed * gain] + [stem_g] * GROUP + [centred(own_ref[...]) * gain, tail]
    ).astype(BF16)

    wide = SPAN * WIN
    forms = mm_exact(jnp.concatenate([embed, stem]), stem) * (1.0 / width)
    forms = jnp.concatenate([forms] * SPAN, axis=1)
    gram = jnp.concatenate([forms[LANES:]] * SPAN)
    same = (
        lax.broadcasted_iota(jnp.int32, (wide, wide), 0) // WIN
        == lax.broadcasted_iota(jnp.int32, (wide, wide), 1) // WIN
    )
    gram_ref[0], gram_ref[1] = split2(jnp.where(same, gram, 0.0))
    same = (
        lax.broadcasted_iota(jnp.int32, (LANES, wide), 0) % SPAN
        == lax.broadcasted_iota(jnp.int32, (LANES, wide), 1) // WIN
    )
    cross = jnp.where(same, 2.0 * forms[:LANES], 0.0)
    cross_ref[...] = jnp.sum(cross.reshape(LANES // SPAN, SPAN, wide), axis=1)
    const_ref[...] = mm_exact(jnp.ones((8, width), F32), embed * embed) * (1.0 / width)

    rest = stem_ref[...]
    pieces = []
    for _ in range(3):
        hi = rest.astype(BF16).astype(F32)
        pieces.append(hi)
        rest = rest - hi
    pieces_ref[...] = jnp.concatenate(pieces + [jnp.zeros_like(rest)]).astype(BF16)


def make_features(stem_weight, band_embed, own, gain):
    width = band_embed.shape[1]
    own8 = jnp.pad(own, ((0, 8 - own.shape[0]), (0, 0)))
    wide = SPAN * WIN
    vmem = pl.BlockSpec(memory_space=pltpu.VMEM)
    return pl.pallas_call(
        feature_kernel,
        out_shape=[
            jax.ShapeDtypeStruct((2 * LANES + 16, width), BF16),
            jax.ShapeDtypeStruct((2, wide, wide), BF16),
            jax.ShapeDtypeStruct((LANES // SPAN, wide), F32),
            jax.ShapeDtypeStruct((8, LANES), F32),
            jax.ShapeDtypeStruct((LANES, width), BF16),
        ],
        in_specs=[vmem] * 4,
        out_specs=[vmem] * 5,
        compiler_params=pltpu.CompilerParams(vmem_limit_bytes=VMEM_LIMIT),
        cost_estimate=takes(4),
        name="features",
    )(stem_weight, band_embed, own8, gain[None])


def tables_kernel(bands, feats_ref, qkv_ref, mse_ref, mee_ref, av_ref):
    a = mm(feats_ref[...], qkv_ref[...]).astype(BF16)
    head = a.shape[1] // 6
    keys = 2 * LANES
    scale = head**-0.5 * LOG2_E
    beyond = lax.broadcasted_iota(jnp.int32, (8, keys), 1)
    beyond = (beyond >= bands) & (beyond < LANES)
    for i in range(2):
        c = 3 * i * head
        q = a[:, c : c + head]
        k = a[:keys, c + head : c + 2 * head]
        m = mm_t(q[LANES : LANES + WIN], k) * scale
        hi, lo = split2(m)
        mse_ref[:WIN, i * keys : (i + 1) * keys] = hi
        mse_ref[WIN:, i * keys : (i + 1) * keys] = lo
        m = mm_t(q[keys : keys + 16], k)[:8] * scale
        mee_ref[:, i * keys : (i + 1) * keys] = jnp.where(beyond, -1e30, m)
    av_ref[...] = a[:keys, 2 * head :]


def make_tables(bands, feats, qkv):
    steps = HEADS // 2
    width = qkv.shape[0]
    cols = qkv.shape[1] // steps
    return pl.pallas_call(
        functools.partial(tables_kernel, bands),
        grid=(steps,),
        out_shape=[
            jax.ShapeDtypeStruct((2 * WIN, HEADS * 2 * LANES), BF16),
            jax.ShapeDtypeStruct((8, HEADS * 2 * LANES), F32),
            jax.ShapeDtypeStruct((2 * LANES, steps * cols * 2 // 3), BF16),
        ],
        in_specs=[whole_spec(feats.shape), pl.BlockSpec((width, cols), lambda i: (0, i))],
        out_specs=[
            pl.BlockSpec((2 * WIN, 4 * LANES), lambda i: (0, i)),
            pl.BlockSpec((8, 4 * LANES), lambda i: (0, i)),
            pl.BlockSpec((2 * LANES, cols * 2 // 3), lambda i: (0, i)),
        ],
        compiler_params=pltpu.CompilerParams(vmem_limit_bytes=VMEM_LIMIT),
        cost_estimate=takes(8),
        name="tables",
    )(feats, qkv)


def spectral_kernel(
    nb,
    bands,
    place_ref,
    near_ref,
    far_ref,
    sel_ref,
    sel1_ref,
    group_ref,
    mse_ref,
    mee_ref,
    av_ref,
    gram_ref,
    cross_ref,
    const_ref,
    stem_ref,
    embed_ref,
    out_w_ref,
    out_ref,
    rad_ref,
    win,
    ue,
    uw,
    rstd,
):
    base, band, depth, core = (place_ref[k] for k in range(4))
    bsize, zsize, some, _ = near_ref.shape
    px, lanes = rad_ref.shape
    channels = bands * CH_TOK // bsize
    edge = CH_TOK // 2
    for k, ref in enumerate((near_ref, far_ref)):
        for kz in range(zsize):
            at = ((depth ^ kz) * 2 + (core ^ k)) * some
            pieces = [ref[b ^ band, kz, :, :channels].astype(F32) for b in range(bsize)]
            pieces = [jnp.zeros((some, edge), F32)] + pieces
            pieces.append(jnp.zeros((some, lanes - bands * CH_TOK - edge), F32))
            rad_ref[pl.ds(pl.multiple_of(at, some), some), :] = jnp.concatenate(
                pieces, axis=1
            ).astype(BF16)

    part_px = px // GROUP
    tiles = bands // SPAN
    wstep, ustep = part_px + GAP, px + GAP
    lane = lax.broadcasted_iota(jnp.int32, (px, LANES), 1)
    row = lax.broadcasted_iota(jnp.int32, (px, LANES), 0)
    blocks = [rad_ref[:, j * LANES : (j + 2) * LANES] for j in range(tiles)]

    packed = jnp.concatenate(
        [
            jnp.concatenate([b[i * part_px : (i + 1) * part_px] for i in range(GROUP)], axis=1)
            for b in blocks
        ]
    )
    for i in range(0, SPAN, 2):
        wide = mm(packed, sel_ref[:, i * LANES : (i + 2) * LANES])
        for j in range(tiles):
            for k in range(2):
                t = j * SPAN + i + k
                win[t * wstep : t * wstep + part_px, :] = wide[
                    j * part_px : (j + 1) * part_px, k * LANES : (k + 1) * LANES
                ]
    for t in range(bands, LANES):
        win[t * wstep : t * wstep + part_px, :] = jnp.zeros((part_px, LANES), F32)

    acc = jnp.zeros((px, LANES), F32)
    thin = mm(jnp.concatenate(blocks), sel1_ref[...])
    thin_b = thin.astype(BF16)
    form = mm(thin_b, gram_ref[0]) + mm(thin_b, gram_ref[1])
    for j in range(tiles):
        rows = slice(j * px, (j + 1) * px)
        hi, lo = split2(thin[rows] * (form[rows] + cross_ref[j : j + 1, :]))
        summed = mm(hi, group_ref[...]) + mm(lo, group_ref[...])
        acc = jnp.where(lane // SPAN == j, summed, acc)
    scale = lax.rsqrt(acc + const_ref[:1, :] + 1e-5)
    rstd[...] = scale

    own = []
    for i in range(nb):
        t = base + i
        tile = t // SPAN
        cols = pl.ds(pl.multiple_of(tile * LANES, LANES), 2 * LANES)
        shift = t % SPAN
        at = lax.broadcasted_iota(jnp.int32, (2 * LANES, LANES), 0)
        to = lax.broadcasted_iota(jnp.int32, (2 * LANES, LANES), 1)
        pick = (at == shift * CH_TOK + to % WIN).astype(F32).astype(BF16)
        mine = mm(rad_ref[:, cols], pick).astype(BF16)
        own.append(mine)
        rq = jnp.sum(jnp.where(lane == t, scale, 0.0), axis=1, keepdims=True)
        for h in range(0, HEADS, 2):
            both = slice(2 * h * LANES, 2 * (h + 2) * LANES)
            part = (mm(mine[:, : 2 * WIN], mse_ref[:, both]) + mee_ref[i : i + 1, both]) * rq
            for k in range(2):
                r = ((h + k) * nb + i) * ustep
                ue[r : r + px, :] = part[:, 2 * k * LANES : (2 * k + 1) * LANES]
                uw[r : r + px, :] = jnp.where(
                    lane // WIN == row // part_px,
                    part[:, (2 * k + 1) * LANES : (2 * k + 2) * LANES],
                    0.0,
                )

    rows = HEADS * nb
    step = 4

    def groups(g, _):
        ids = [g * step + k for k in range(step)]
        ws = [win[pl.ds(p, LANES, stride=wstep), :].astype(BF16) for p in ids]
        ls = [
            jnp.concatenate(
                [uw[pl.ds(i * part_px + p, rows, stride=ustep), :] for i in range(GROUP)]
            ).astype(BF16)
            for p in ids
        ]
        ss = [mm_t(a, w) for a, w in zip(ls, ws)]
        es = []
        for k, p in enumerate(ids):
            for i in range(GROUP):
                q = i * part_px + p
                rki = rstd[pl.ds(q, 1), :]
                s = (ss[k][i * rows : (i + 1) * rows] + ue[pl.ds(q, rows, stride=ustep), :]) * rki
                e = jnp.exp2(s - jnp.max(s, axis=1, keepdims=True))
                e = e * (1.0 / jnp.sum(e, axis=1, keepdims=True)) * rki
                ue[pl.ds(q, rows, stride=ustep), :] = e
                es.append(e)
        for k, p in enumerate(ids):
            z = mm(jnp.concatenate(es[k * GROUP : (k + 1) * GROUP]).astype(BF16), ws[k])
            for i in range(GROUP):
                uw[pl.ds(i * part_px + p, rows, stride=ustep), :] = z[i * rows : (i + 1) * rows]
        return 0

    lax.fori_loop(0, part_px // step, groups, 0)

    keep = lane // WIN == row // part_px
    half = lane < LANES // 2
    for i in range(nb):
        mixes = []
        for h in range(0, HEADS, 2):
            outs = []
            for k in range(2):
                r = ((h + k) * nb + i) * ustep
                both = jnp.concatenate(
                    [ue[r : r + px, :], jnp.where(keep, uw[r : r + px, :], 0.0)], axis=1
                ).astype(BF16)
                outs.append(mm(both, av_ref[:, (h + k) * LANES : (h + k + 1) * LANES]))
            mixes.append(jnp.where(half, outs[0], outs[1]).astype(BF16))
        update = mm(jnp.concatenate(mixes, axis=1), out_w_ref[...])
        token = (mm(own[i], stem_ref[...]) + embed_ref[i : i + 1, :]).astype(BF16)
        out_ref[i] = token.astype(F32) + update


def spatial_band(x, gain_ref, qkv_ref, w_ref, proj, mixed):
    pixels, width = x.shape
    cent = x - jnp.mean(x, axis=1, keepdims=True)
    var = jnp.mean(cent * cent, axis=1, keepdims=True)
    normed = (cent * lax.rsqrt(var + 1e-5) * gain_ref[...]).astype(BF16)
    chunk = 6 * width // HEADS
    for c in range(0, 3 * width, chunk):
        proj[:, c : c + chunk] = mm(normed, qkv_ref[:, c : c + chunk]).astype(BF16)
    head = width // HEADS
    low = lax.broadcasted_iota(jnp.int32, (pixels, 2 * head), 1) < head
    for pair in range(HEADS // 2):
        c = pair * 6 * head
        t0 = proj[:, c : c + 2 * head]
        t1 = proj[:, c + 2 * head : c + 4 * head]
        t2 = proj[:, c + 4 * head : c + 6 * head]
        zero = jnp.zeros_like(t0)
        r0 = jnp.concatenate([t0[:, head:], t0[:, :head]], axis=1)
        r2 = jnp.concatenate([t2[:, head:], t2[:, :head]], axis=1)
        outs = []
        for q, k, v in (
            (jnp.where(low, t0, zero), r0, t1),
            (jnp.where(low, zero, t1), r2, t2),
        ):
            s = mm_t(q, k)
            e = jnp.exp((s - jnp.max(s, axis=1, keepdims=True)) * (head**-0.5))
            total = jnp.sum(e, axis=1, keepdims=True)
            outs.append(mm(e.astype(BF16), v) * (1.0 / total))
        mixed[:, pair * 2 * head : (pair + 1) * 2 * head] = jnp.where(
            low, outs[0], outs[1]
        ).astype(BF16)
    return x + mm(mixed[...], w_ref[...])


def spatial_kernel(x_ref, gain_ref, qkv_ref, w_ref, out_ref, proj, mixed):
    out_ref[0] = spatial_band(x_ref[0], gain_ref, qkv_ref, w_ref, proj, mixed).astype(BF16)


def spatial_send_kernel(devices, x_ref, gain_ref, qkv_ref, w_ref, out_ref, proj, mixed, rows):
    b = pl.program_id(0)
    y = spatial_band(x_ref[0], gain_ref, qkv_ref, w_ref, proj, mixed)
    each = y.shape[0] // devices
    rows[:, pl.ds(pl.multiple_of(b * each, each), each), :] = y.reshape(devices, each, y.shape[1])

    @pl.when(b == pl.num_programs(0) - 1)
    def _():
        out_ref[...] = rows[...].astype(BF16)


def spatial(x, gain, qkv, w, first, count, devices):
    nb, pixels, width = x.shape
    each = pixels // devices
    in_specs = [
        pl.BlockSpec((1, pixels, width), lambda i: (first + i, 0, 0)),
        whole_spec((1, width)),
        whole_spec(qkv.shape),
        whole_spec(w.shape),
    ]
    scratch = [pltpu.VMEM((pixels, 3 * width), BF16), pltpu.VMEM((pixels, width), BF16)]
    params = dict(
        grid=(count,),
        in_specs=in_specs,
        compiler_params=pltpu.CompilerParams(vmem_limit_bytes=VMEM_LIMIT),
        cost_estimate=takes(15),
        name="spatial",
    )
    if direct(pixels, devices, count):
        return pl.pallas_call(
            functools.partial(spatial_send_kernel, devices),
            out_shape=jax.ShapeDtypeStruct((devices, count * each, width), BF16),
            out_specs=whole_spec((devices, count * each, width)),
            scratch_shapes=scratch + [pltpu.VMEM((devices, count * each, width), F32)],
            **params,
        )(x, gain[None], qkv, w)
    return pl.pallas_call(
        spatial_kernel,
        out_shape=jax.ShapeDtypeStruct((count, pixels, width), BF16),
        out_specs=pl.BlockSpec((1, pixels, width), lambda i: (i, 0, 0)),
        scratch_shapes=scratch,
        **params,
    )(x, gain[None], qkv, w)


def direct(pixels, devices, count):
    each = pixels // devices
    return each % 8 == 0 and (each * count) % 16 == 0


def gelu(v):
    half = 0.5 * v
    inner = v * ((2 / math.pi) ** 0.5 + (2 / math.pi) ** 0.5 * 0.044715 * (v * v))
    return half + half * jnp.tanh(inner)


def mlp_kernel(run, earlier, contents, place_ref, x_ref, gain_ref, bias_ref, *refs):
    n_weights = 4 + len(contents)
    weight_refs, refs = refs[:n_weights], refs[n_weights:]
    earlier_refs, refs = refs[:earlier], refs[earlier:]
    out_ref, normed, acc, buf, sems, *rest = refs
    band, depth = place_ref[1], place_ref[2]
    rows, width = normed.shape
    zsize, groups = bias_ref.shape[1], bias_ref.shape[2]
    half = bias_ref.shape[4]
    size = groups * half

    blocks = []
    for c in range(2):
        up, down = weight_refs[2 * c], weight_refs[2 * c + 1]
        bias = [bias_ref[c, 0, i] for i in range(groups)]
        blocks.append(([(up, 0, size, 0), (down, 0, size, size)], bias, False))
    pieces = []
    for ref, (c, h, sources) in zip(weight_refs[4:], contents):
        for i, (k, m) in enumerate(sources):
            pieces.append((ref, i, bias_ref[c, depth ^ lax.rem(depth - k + zsize, zsize), (band ^ m) * 2 + h]))
    for i in range(0, len(pieces), groups):
        some = pieces[i : i + groups]
        runs = []
        for j, (ref, at, _) in enumerate(some):
            if runs and runs[-1][0] is ref and runs[-1][1] + runs[-1][2] == at * 2 * half:
                runs[-1][2] += 2 * half
            else:
                runs.append([ref, at * 2 * half, 2 * half, j * 2 * half])
        blocks.append((runs, [p[2] for p in some], True))

    def copies(n):
        slot = n % buf.shape[0]
        return [
            pltpu.make_async_copy(
                ref.at[pl.ds(first, count), :],
                buf.at[slot, pl.ds(to, count), :],
                sems.at[slot, i],
            )
            for i, (ref, first, count, to) in enumerate(blocks[n][0])
        ]

    ahead = buf.shape[0] - 1
    for n in range(ahead):
        for copy in copies(n):
            copy.start()

    x = x_ref[:rows, :].astype(F32)
    cent = x - jnp.mean(x, axis=1, keepdims=True)
    var = jnp.mean(cent * cent, axis=1, keepdims=True)
    normed[...] = (cent * lax.rsqrt(var + 1e-5) * gain_ref[...]).astype(BF16)
    acc[...] = x

    for n, (_, bias, mixed) in enumerate(blocks):
        for copy in copies(n):
            copy.wait()
        if n + ahead < len(blocks):
            for copy in copies(n + ahead):
                copy.start()
        slot = n % buf.shape[0]
        total = None
        hidden = []
        for part in range(2):
            ids = range(part * groups // 2, (part + 1) * groups // 2)
            if not mixed:
                up = buf[slot, ids[0] * half : ids[0] * half + size // 2, :]
            else:
                up = jnp.concatenate([buf[slot, 2 * g * half : (2 * g + 1) * half, :] for g in ids])
            v = mm_t(normed[...], up) + jnp.concatenate([bias[g] for g in ids], axis=1)
            hidden.append(gelu(v).astype(BF16))
        for part in range(2):
            ids = range(part * groups // 2, (part + 1) * groups // 2)
            if not mixed:
                down = buf[slot, size + ids[0] * half : size + ids[0] * half + size // 2, :]
            else:
                down = jnp.concatenate(
                    [buf[slot, (2 * g + 1) * half : (2 * g + 2) * half, :] for g in ids]
                )
            piece = mm(hidden[part], down)
            total = piece if total is None else total + piece
        acc[...] += total

    if len(out_ref.shape) == 2:
        out_ref[...] = acc[...].astype(BF16)
        return
    lay = rest[0]
    each, bands, _ = out_ref.shape
    whole = bands * each
    parts = earlier + 1
    for p in range(parts):
        part = earlier_refs[p] if p < earlier else acc
        for c in range(width // LANES):
            cols = slice(c * LANES, (c + 1) * LANES)
            if parts == 1:
                lay[c * whole : (c + 1) * whole, :] = part[:, cols]
                continue
            for i in range(rows // run):
                to = c * whole + (i * parts + p) * run
                lay[to : to + run, :] = part[i * run : (i + 1) * run, cols].astype(F32)
    for c in range(width // LANES):
        for px in range(each):
            out_ref[px, :, c * LANES : (c + 1) * LANES] = lay[
                pl.ds(c * whole + px, bands, stride=each), :
            ].astype(BF16)


def mlp(place, x, rows, gain, bias, own, gathered, contents, earlier, run, result):
    width = x.shape[1]
    size = own[0].shape[0]
    scratch = [
        pltpu.VMEM((rows, width), BF16),
        pltpu.VMEM((rows, width), F32),
        pltpu.VMEM((3, 2 * size, width), BF16),
        pltpu.SemaphoreType.DMA((3, 2 * bias.shape[2])),
    ]
    if result is None:
        shape = (rows, width)
    else:
        shape = result
        scratch.append(pltpu.VMEM((math.prod(result) // LANES, LANES), F32))
    vmem = pl.BlockSpec(memory_space=pltpu.VMEM)
    return pl.pallas_call(
        functools.partial(mlp_kernel, run, len(earlier), contents),
        out_shape=jax.ShapeDtypeStruct(shape, BF16),
        in_specs=[pl.BlockSpec(memory_space=pltpu.SMEM), vmem, vmem, vmem]
        + [pl.BlockSpec(memory_space=pl.ANY)] * (4 + len(gathered))
        + [vmem] * len(earlier),
        out_specs=vmem,
        scratch_shapes=scratch,
        compiler_params=pltpu.CompilerParams(vmem_limit_bytes=VMEM_LIMIT),
        cost_estimate=takes(0),
        name="mlp",
    )(place, x, gain[None], bias, *own, *gathered, *earlier)


def swap(x, axis, mask):
    count = lax.axis_size(axis)
    return lax.ppermute(x, axis, [(i, i ^ mask) for i in range(count)])


def selectors():
    row = np.arange(GROUP * 2 * LANES)[:, None]
    col = np.arange(SPAN * LANES)[None]
    within = row % (2 * LANES)
    sel = (within == (col // LANES) * CH_TOK + col % WIN) & (
        row // (2 * LANES) == col % LANES // WIN
    )
    row = np.arange(2 * LANES)[:, None]
    col = np.arange(SPAN * WIN)[None]
    sel1 = row == (col // WIN) * CH_TOK + col % WIN
    group = row // WIN == np.arange(LANES)[None] % SPAN
    return sel.astype(BF16), sel1.astype(BF16), group.astype(BF16)


def whole_spec(shape):
    return pl.BlockSpec(shape, lambda *_: (0,) * len(shape))


def spectral(place, near, far, tables, own, spec_out, nb, bands):
    bsize, zsize, some, _ = near.shape
    pixels = 2 * zsize * some
    width = spec_out.shape[0]
    lanes = (bands // SPAN + 1) * LANES
    args = [near, far, *selectors(), *tables, own, spec_out]
    part_px = pixels // GROUP
    return pl.pallas_call(
        functools.partial(spectral_kernel, nb, bands),
        out_shape=jax.ShapeDtypeStruct((nb, pixels, width), F32),
        in_specs=[pl.BlockSpec(memory_space=pltpu.SMEM)]
        + [pl.BlockSpec(memory_space=pltpu.VMEM)] * len(args),
        out_specs=pl.BlockSpec(memory_space=pltpu.VMEM),
        scratch_shapes=[
            pltpu.VMEM((pixels, lanes), BF16),
            pltpu.VMEM((LANES * (part_px + GAP), LANES), F32),
            pltpu.VMEM((HEADS * nb * (pixels + GAP), LANES), F32),
            pltpu.VMEM((HEADS * nb * (pixels + GAP), LANES), F32),
            pltpu.VMEM((pixels, LANES), F32),
        ],
        compiler_params=pltpu.CompilerParams(vmem_limit_bytes=VMEM_LIMIT),
        cost_estimate=takes(26),
        name="spectral",
    )(place, *args)


def local(
    radiance,
    stem_weight,
    band_embed,
    norm_spectral,
    spec_qkv,
    spec_out,
    norm_spatial,
    spat_qkv,
    spat_out,
    norm_mlp,
    up_weight,
    up_bias,
    down_weight,
):
    bands, width = band_embed.shape
    bsize, psize = lax.axis_size("band"), lax.axis_size("pix")
    devices = bsize * psize
    nb = -(-bands // devices)
    band, pix = lax.axis_index("band"), lax.axis_index("pix")
    base = jnp.minimum((pix * bsize + band) * nb, bands - nb).astype(jnp.int32)

    rows, channels = radiance.shape
    message = jnp.concatenate([radiance.astype(BF16), up_bias.reshape(rows, -1)], axis=1)
    own = lax.dynamic_slice_in_dim(band_embed, base, nb, 0)
    features = make_features(stem_weight, band_embed, own, norm_spectral)

    half = up_weight.shape[0] // bsize // 2
    bits = [1 << i for i in range(bsize.bit_length() - 1)]
    bit_orders = (bits, bits[::-1])
    share = []
    for h in range(2):
        at = (band * 2 + h) * half
        share.append(
            jnp.concatenate(
                [lax.dynamic_slice_in_dim(w, at, half, 0) for w in (up_weight, down_weight)]
            )
        )
    share = jnp.concatenate(share)

    def ring(x, step):
        return lax.ppermute(x, "pix", [(i, (i + 2 * step) % psize) for i in range(psize)])


    def first_bit(chunks):
        out = []
        for h, order in enumerate(bit_orders):
            mine = jnp.concatenate([c[h * 2 * half : (h + 1) * 2 * half] for c in chunks])
            out.append((mine, swap(mine, "band", order[0])))
        return out

    def joined(pair):
        return jnp.concatenate(pair)

    def other_bits(held):
        done = []
        for mine, order in zip(held, bit_orders):
            got = []
            for bit in order[1:]:
                got.append(swap(joined([mine] + got) if got else mine, "band", bit))
            done += got
        return done

    zs = jnp.stack([message] + [swap(message, "pix", 2 * k) for k in range(1, psize // 2)])
    zs, share, features = lax.optimization_barrier((zs, share, features))
    near = jnp.stack([zs] + [swap(zs, "band", k) for k in range(1, bsize)])
    tables = make_tables(bands, features[0], spec_qkv) + features[1:]
    shares = [ring(share, 1)]
    near, tables, shares, share, up_weight, down_weight = lax.optimization_barrier(
        (near, tables, shares, share, up_weight, down_weight)
    )
    far = swap(near, "pix", 1)
    own_weights = [up_weight, down_weight, swap(up_weight, "pix", 1), swap(down_weight, "pix", 1)]
    pairs_1 = first_bit(shares)
    while len(shares) < psize // 2 - 2:
        shares.append(ring(shares[-1], 1))
    shares.append(ring(share, -1))
    place = jnp.stack([base, band, pix // 2, pix % 2]).astype(jnp.int32)
    after_spectral = spectral(place, near, far, tables, own, spec_out, nb, bands)
    after_spectral, shares, own_weights, pairs_1 = lax.optimization_barrier(
        (after_spectral, shares, own_weights, pairs_1)
    )
    held_1 = [joined(pair) for pair in pairs_1]
    got_1 = other_bits(held_1)
    pairs = first_bit(shares[1:])
    bias = jnp.stack([near[0, :, :, channels:], far[0, :, :, channels:]])
    bias = bias.reshape(2, psize // 2, 2 * bsize, 1, half).astype(F32)
    pixels = after_spectral.shape[1]
    each = pixels // devices
    count = nb // 2 if nb % 2 == 0 and direct(pixels, devices, nb // 2) else nb
    arrived, results = [], []
    for first in range(0, nb, count):
        part = spatial(after_spectral, norm_spatial, spat_qkv, spat_out, first, count, devices)
        if first == 0:
            part, after_spectral, pairs, got_1 = lax.optimization_barrier(
                (part, after_spectral, pairs, got_1)
            )
            held = [joined(pair) for pair in pairs]
            got = other_bits(held)
            early = held_1 + got_1
            early_far, held_far = [[swap(x, "pix", 1) for x in xs] for xs in (early, held)]
        else:
            part, arrived, early_far, held_far = lax.optimization_barrier(
                (part, arrived, early_far, held_far)
            )
        last_part = part
        if direct(pixels, devices, count):
            moved = lax.all_to_all(part, ("pix", "band"), split_axis=0, concat_axis=0, tiled=True)
        else:
            moved = lax.all_to_all(part, ("pix", "band"), split_axis=1, concat_axis=0, tiled=True)
        arrived.append(moved.reshape(-1, width))
    got, _ = lax.optimization_barrier((got, last_part))
    got_far = [swap(x, "pix", 1) for x in got]
    gathered = [*early, *early_far, *held, *held_far, *got, *got_far]
    groups = []
    for some in (range(1, 2), range(2, psize // 2)):
        held_ids, got_ids = [], []
        for h, order in enumerate(bit_orders):
            ids = [(k, m) for m in (0, order[0]) for k in some]
            held_ids.append((h, tuple(ids)))
            for bit in order[1:]:
                new = [(k, m ^ bit) for k, m in ids]
                got_ids.append((h, tuple(new)))
                ids = ids + new
        groups += [held_ids, got_ids]
    groups = [groups[0] + groups[1], groups[2], groups[3]]
    contents = tuple((c, *x) for part in groups for c in range(2) for x in part)
    run = count * each
    for i, moved in enumerate(arrived):
        last = i == len(arrived) - 1
        results.append(
            mlp(
                place,
                moved,
                bands // nb * run,
                norm_mlp,
                bias,
                own_weights,
                gathered,
                contents,
                results if last else [],
                run,
                (each, bands, width) if last else None,
            )
        )
    return results[-1]


def solution(mesh):
    placed = (
        P("pix", "band"),
        P(),
        P(),
        P(),
        P(),
        P(),
        P(),
        P(),
        P(),
        P(),
        P("pix", None),
        P("pix"),
        P("pix", None),
    )
    return jax.shard_map(
        local, mesh=mesh, in_specs=placed, out_specs=P(("pix", "band"), None, None), check_vma=False
    )
```

```python
import functools
import math

import jax
import jax.numpy as jnp
import numpy as np
from jax import lax
from jax.experimental import pallas as pl
from jax.experimental.pallas import tpu as pltpu
from jax.sharding import PartitionSpec as P

HEADS = 16
CH_TOK = 16
WIN = 2 * CH_TOK
LANES = 128
GROUP = LANES // WIN
SPAN = LANES // CH_TOK
GAP = 8
F32 = jnp.float32
BF16 = jnp.bfloat16
HIGH = lax.Precision.HIGHEST
LOG2_E = math.log2(math.e)
VMEM_LIMIT = 60 * 2**20


def takes(us):
    return pl.CostEstimate(flops=us * 10**9, bytes_accessed=2**20, transcendentals=0)


def mm(a, b):
    return jnp.dot(a, b, preferred_element_type=F32)


def mm_t(a, b):
    return lax.dot_general(a, b, (((1,), (1,)), ((), ())), preferred_element_type=F32)


def split2(x):
    hi = x.astype(BF16)
    return hi, (x - hi.astype(F32)).astype(BF16)


def mm_exact(a, b):
    return lax.dot_general(
        a, b, (((1,), (1,)), ((), ())), precision=HIGH, preferred_element_type=F32
    )


def feature_kernel(
    stem_ref, embed_ref, own_ref, gain_ref, feats_ref, gram_ref, cross_ref, const_ref, pieces_ref
):
    def centred(x):
        return x - jnp.mean(x, axis=1, keepdims=True)

    gain = gain_ref[...]
    stem = centred(stem_ref[...])
    bands, width = embed_ref.shape
    blank = jnp.zeros((LANES - bands, width), F32)
    embed = jnp.concatenate([centred(embed_ref[...]), blank])
    stem_g = stem * gain
    tail = jnp.zeros((8, width), F32)
    feats_ref[...] = jnp.concatenate(
        [embed * gain] + [stem_g] * GROUP + [centred(own_ref[...]) * gain, tail]
    ).astype(BF16)

    wide = SPAN * WIN
    forms = mm_exact(jnp.concatenate([embed, stem]), stem) * (1.0 / width)
    forms = jnp.concatenate([forms] * SPAN, axis=1)
    gram = jnp.concatenate([forms[LANES:]] * SPAN)
    same = (
        lax.broadcasted_iota(jnp.int32, (wide, wide), 0) // WIN
        == lax.broadcasted_iota(jnp.int32, (wide, wide), 1) // WIN
    )
    gram_ref[0], gram_ref[1] = split2(jnp.where(same, gram, 0.0))
    same = (
        lax.broadcasted_iota(jnp.int32, (LANES, wide), 0) % SPAN
        == lax.broadcasted_iota(jnp.int32, (LANES, wide), 1) // WIN
    )
    cross = jnp.where(same, 2.0 * forms[:LANES], 0.0)
    cross_ref[...] = jnp.sum(cross.reshape(LANES // SPAN, SPAN, wide), axis=1)
    const_ref[...] = mm_exact(jnp.ones((8, width), F32), embed * embed) * (1.0 / width)

    rest = stem_ref[...]
    pieces = []
    for _ in range(3):
        hi = rest.astype(BF16).astype(F32)
        pieces.append(hi)
        rest = rest - hi
    pieces_ref[...] = jnp.concatenate(pieces + [jnp.zeros_like(rest)]).astype(BF16)


def make_features(stem_weight, band_embed, own, gain):
    width = band_embed.shape[1]
    own8 = jnp.pad(own, ((0, 8 - own.shape[0]), (0, 0)))
    wide = SPAN * WIN
    vmem = pl.BlockSpec(memory_space=pltpu.VMEM)
    return pl.pallas_call(
        feature_kernel,
        out_shape=[
            jax.ShapeDtypeStruct((2 * LANES + 16, width), BF16),
            jax.ShapeDtypeStruct((2, wide, wide), BF16),
            jax.ShapeDtypeStruct((LANES // SPAN, wide), F32),
            jax.ShapeDtypeStruct((8, LANES), F32),
            jax.ShapeDtypeStruct((LANES, width), BF16),
        ],
        in_specs=[vmem] * 4,
        out_specs=[vmem] * 5,
        compiler_params=pltpu.CompilerParams(vmem_limit_bytes=VMEM_LIMIT),
        cost_estimate=takes(4),
        name="features",
    )(stem_weight, band_embed, own8, gain[None])


def tables_kernel(bands, feats_ref, qkv_ref, mse_ref, mee_ref, av_ref):
    a = mm(feats_ref[...], qkv_ref[...]).astype(BF16)
    head = a.shape[1] // 6
    keys = 2 * LANES
    scale = head**-0.5 * LOG2_E
    beyond = lax.broadcasted_iota(jnp.int32, (8, keys), 1)
    beyond = (beyond >= bands) & (beyond < LANES)
    for i in range(2):
        c = 3 * i * head
        q = a[:, c : c + head]
        k = a[:keys, c + head : c + 2 * head]
        m = mm_t(q[LANES : LANES + WIN], k) * scale
        hi, lo = split2(m)
        mse_ref[:WIN, i * keys : (i + 1) * keys] = hi
        mse_ref[WIN:, i * keys : (i + 1) * keys] = lo
        m = mm_t(q[keys : keys + 16], k)[:8] * scale
        mee_ref[:, i * keys : (i + 1) * keys] = jnp.where(beyond, -1e30, m)
    av_ref[...] = a[:keys, 2 * head :]


def make_tables(bands, feats, qkv):
    steps = HEADS // 2
    width = qkv.shape[0]
    cols = qkv.shape[1] // steps
    return pl.pallas_call(
        functools.partial(tables_kernel, bands),
        grid=(steps,),
        out_shape=[
            jax.ShapeDtypeStruct((2 * WIN, HEADS * 2 * LANES), BF16),
            jax.ShapeDtypeStruct((8, HEADS * 2 * LANES), F32),
            jax.ShapeDtypeStruct((2 * LANES, steps * cols * 2 // 3), BF16),
        ],
        in_specs=[whole_spec(feats.shape), pl.BlockSpec((width, cols), lambda i: (0, i))],
        out_specs=[
            pl.BlockSpec((2 * WIN, 4 * LANES), lambda i: (0, i)),
            pl.BlockSpec((8, 4 * LANES), lambda i: (0, i)),
            pl.BlockSpec((2 * LANES, cols * 2 // 3), lambda i: (0, i)),
        ],
        compiler_params=pltpu.CompilerParams(vmem_limit_bytes=VMEM_LIMIT),
        cost_estimate=takes(8),
        name="tables",
    )(feats, qkv)


def spectral_kernel(
    nb,
    bands,
    place_ref,
    near_ref,
    far_ref,
    sel_ref,
    sel1_ref,
    group_ref,
    mse_ref,
    mee_ref,
    av_ref,
    gram_ref,
    cross_ref,
    const_ref,
    stem_ref,
    embed_ref,
    out_w_ref,
    out_ref,
    rad_ref,
    win,
    ue,
    uw,
    rstd,
):
    base, band, depth, core = (place_ref[k] for k in range(4))
    bsize, zsize, some, _ = near_ref.shape
    px, lanes = rad_ref.shape
    channels = bands * CH_TOK // bsize
    edge = CH_TOK // 2
    for k, ref in enumerate((near_ref, far_ref)):
        for kz in range(zsize):
            at = ((depth ^ kz) * 2 + (core ^ k)) * some
            pieces = [ref[b ^ band, kz, :, :channels].astype(F32) for b in range(bsize)]
            pieces = [jnp.zeros((some, edge), F32)] + pieces
            pieces.append(jnp.zeros((some, lanes - bands * CH_TOK - edge), F32))
            rad_ref[pl.ds(pl.multiple_of(at, some), some), :] = jnp.concatenate(
                pieces, axis=1
            ).astype(BF16)

    part_px = px // GROUP
    tiles = bands // SPAN
    wstep, ustep = part_px + GAP, px + GAP
    lane = lax.broadcasted_iota(jnp.int32, (px, LANES), 1)
    row = lax.broadcasted_iota(jnp.int32, (px, LANES), 0)
    blocks = [rad_ref[:, j * LANES : (j + 2) * LANES] for j in range(tiles)]

    packed = jnp.concatenate(
        [
            jnp.concatenate([b[i * part_px : (i + 1) * part_px] for i in range(GROUP)], axis=1)
            for b in blocks
        ]
    )
    for i in range(0, SPAN, 2):
        wide = mm(packed, sel_ref[:, i * LANES : (i + 2) * LANES])
        for j in range(tiles):
            for k in range(2):
                t = j * SPAN + i + k
                win[t * wstep : t * wstep + part_px, :] = wide[
                    j * part_px : (j + 1) * part_px, k * LANES : (k + 1) * LANES
                ]
    for t in range(bands, LANES):
        win[t * wstep : t * wstep + part_px, :] = jnp.zeros((part_px, LANES), F32)

    acc = jnp.zeros((px, LANES), F32)
    thin = mm(jnp.concatenate(blocks), sel1_ref[...])
    thin_b = thin.astype(BF16)
    form = mm(thin_b, gram_ref[0]) + mm(thin_b, gram_ref[1])
    for j in range(tiles):
        rows = slice(j * px, (j + 1) * px)
        hi, lo = split2(thin[rows] * (form[rows] + cross_ref[j : j + 1, :]))
        summed = mm(hi, group_ref[...]) + mm(lo, group_ref[...])
        acc = jnp.where(lane // SPAN == j, summed, acc)
    scale = lax.rsqrt(acc + const_ref[:1, :] + 1e-5)
    rstd[...] = scale

    own = []
    for i in range(nb):
        t = base + i
        tile = t // SPAN
        cols = pl.ds(pl.multiple_of(tile * LANES, LANES), 2 * LANES)
        shift = t % SPAN
        at = lax.broadcasted_iota(jnp.int32, (2 * LANES, LANES), 0)
        to = lax.broadcasted_iota(jnp.int32, (2 * LANES, LANES), 1)
        pick = (at == shift * CH_TOK + to % WIN).astype(F32).astype(BF16)
        mine = mm(rad_ref[:, cols], pick).astype(BF16)
        own.append(mine)
        rq = jnp.sum(jnp.where(lane == t, scale, 0.0), axis=1, keepdims=True)
        for h in range(0, HEADS, 2):
            both = slice(2 * h * LANES, 2 * (h + 2) * LANES)
            part = (mm(mine[:, : 2 * WIN], mse_ref[:, both]) + mee_ref[i : i + 1, both]) * rq
            for k in range(2):
                r = ((h + k) * nb + i) * ustep
                ue[r : r + px, :] = part[:, 2 * k * LANES : (2 * k + 1) * LANES]
                uw[r : r + px, :] = jnp.where(
                    lane // WIN == row // part_px,
                    part[:, (2 * k + 1) * LANES : (2 * k + 2) * LANES],
                    0.0,
                )

    rows = HEADS * nb
    step = 4

    def groups(g, _):
        ids = [g * step + k for k in range(step)]
        ws = [win[pl.ds(p, LANES, stride=wstep), :].astype(BF16) for p in ids]
        ls = [
            jnp.concatenate(
                [uw[pl.ds(i * part_px + p, rows, stride=ustep), :] for i in range(GROUP)]
            ).astype(BF16)
            for p in ids
        ]
        ss = [mm_t(a, w) for a, w in zip(ls, ws)]
        es = []
        for k, p in enumerate(ids):
            for i in range(GROUP):
                q = i * part_px + p
                rki = rstd[pl.ds(q, 1), :]
                s = (ss[k][i * rows : (i + 1) * rows] + ue[pl.ds(q, rows, stride=ustep), :]) * rki
                e = jnp.exp2(s - jnp.max(s, axis=1, keepdims=True))
                e = e * (1.0 / jnp.sum(e, axis=1, keepdims=True)) * rki
                ue[pl.ds(q, rows, stride=ustep), :] = e
                es.append(e)
        for k, p in enumerate(ids):
            z = mm(jnp.concatenate(es[k * GROUP : (k + 1) * GROUP]).astype(BF16), ws[k])
            for i in range(GROUP):
                uw[pl.ds(i * part_px + p, rows, stride=ustep), :] = z[i * rows : (i + 1) * rows]
        return 0

    lax.fori_loop(0, part_px // step, groups, 0)

    keep = lane // WIN == row // part_px
    half = lane < LANES // 2
    for i in range(nb):
        mixes = []
        for h in range(0, HEADS, 2):
            outs = []
            for k in range(2):
                r = ((h + k) * nb + i) * ustep
                both = jnp.concatenate(
                    [ue[r : r + px, :], jnp.where(keep, uw[r : r + px, :], 0.0)], axis=1
                ).astype(BF16)
                outs.append(mm(both, av_ref[:, (h + k) * LANES : (h + k + 1) * LANES]))
            mixes.append(jnp.where(half, outs[0], outs[1]).astype(BF16))
        update = mm(jnp.concatenate(mixes, axis=1), out_w_ref[...])
        token = (mm(own[i], stem_ref[...]) + embed_ref[i : i + 1, :]).astype(BF16)
        out_ref[i] = token.astype(F32) + update


def spatial_band(x, gain_ref, qkv_ref, w_ref, proj, mixed):
    pixels, width = x.shape
    cent = x - jnp.mean(x, axis=1, keepdims=True)
    var = jnp.mean(cent * cent, axis=1, keepdims=True)
    normed = (cent * lax.rsqrt(var + 1e-5) * gain_ref[...]).astype(BF16)
    chunk = 6 * width // HEADS
    for c in range(0, 3 * width, chunk):
        proj[:, c : c + chunk] = mm(normed, qkv_ref[:, c : c + chunk]).astype(BF16)
    head = width // HEADS
    low = lax.broadcasted_iota(jnp.int32, (pixels, 2 * head), 1) < head
    for pair in range(HEADS // 2):
        c = pair * 6 * head
        t0 = proj[:, c : c + 2 * head]
        t1 = proj[:, c + 2 * head : c + 4 * head]
        t2 = proj[:, c + 4 * head : c + 6 * head]
        zero = jnp.zeros_like(t0)
        r0 = jnp.concatenate([t0[:, head:], t0[:, :head]], axis=1)
        r2 = jnp.concatenate([t2[:, head:], t2[:, :head]], axis=1)
        outs = []
        for q, k, v in (
            (jnp.where(low, t0, zero), r0, t1),
            (jnp.where(low, zero, t1), r2, t2),
        ):
            s = mm_t(q, k)
            e = jnp.exp((s - jnp.max(s, axis=1, keepdims=True)) * (head**-0.5))
            total = jnp.sum(e, axis=1, keepdims=True)
            outs.append(mm(e.astype(BF16), v) * (1.0 / total))
        mixed[:, pair * 2 * head : (pair + 1) * 2 * head] = jnp.where(
            low, outs[0], outs[1]
        ).astype(BF16)
    return x + mm(mixed[...], w_ref[...])


def spatial_kernel(x_ref, gain_ref, qkv_ref, w_ref, out_ref, proj, mixed):
    out_ref[0] = spatial_band(x_ref[0], gain_ref, qkv_ref, w_ref, proj, mixed).astype(BF16)


def spatial_send_kernel(devices, x_ref, gain_ref, qkv_ref, w_ref, out_ref, proj, mixed, rows):
    b = pl.program_id(0)
    y = spatial_band(x_ref[0], gain_ref, qkv_ref, w_ref, proj, mixed)
    each = y.shape[0] // devices
    rows[:, pl.ds(pl.multiple_of(b * each, each), each), :] = y.reshape(devices, each, y.shape[1])

    @pl.when(b == pl.num_programs(0) - 1)
    def _():
        out_ref[...] = rows[...].astype(BF16)


def spatial(x, gain, qkv, w, first, count, devices):
    nb, pixels, width = x.shape
    each = pixels // devices
    in_specs = [
        pl.BlockSpec((1, pixels, width), lambda i: (first + i, 0, 0)),
        whole_spec((1, width)),
        whole_spec(qkv.shape),
        whole_spec(w.shape),
    ]
    scratch = [pltpu.VMEM((pixels, 3 * width), BF16), pltpu.VMEM((pixels, width), BF16)]
    params = dict(
        grid=(count,),
        in_specs=in_specs,
        compiler_params=pltpu.CompilerParams(vmem_limit_bytes=VMEM_LIMIT),
        cost_estimate=takes(15),
        name="spatial",
    )
    if direct(pixels, devices, count):
        return pl.pallas_call(
            functools.partial(spatial_send_kernel, devices),
            out_shape=jax.ShapeDtypeStruct((devices, count * each, width), BF16),
            out_specs=whole_spec((devices, count * each, width)),
            scratch_shapes=scratch + [pltpu.VMEM((devices, count * each, width), F32)],
            **params,
        )(x, gain[None], qkv, w)
    return pl.pallas_call(
        spatial_kernel,
        out_shape=jax.ShapeDtypeStruct((count, pixels, width), BF16),
        out_specs=pl.BlockSpec((1, pixels, width), lambda i: (i, 0, 0)),
        scratch_shapes=scratch,
        **params,
    )(x, gain[None], qkv, w)


def direct(pixels, devices, count):
    each = pixels // devices
    return each % 8 == 0 and (each * count) % 16 == 0


def gelu(v):
    half = 0.5 * v
    inner = v * ((2 / math.pi) ** 0.5 + (2 / math.pi) ** 0.5 * 0.044715 * (v * v))
    return half + half * jnp.tanh(inner)


def mlp_kernel(run, earlier, contents, place_ref, x_ref, gain_ref, bias_ref, *refs):
    n_weights = 4 + len(contents)
    weight_refs, refs = refs[:n_weights], refs[n_weights:]
    earlier_refs, refs = refs[:earlier], refs[earlier:]
    out_ref, normed, acc, buf, sems, *rest = refs
    band, depth = place_ref[1], place_ref[2]
    rows, width = normed.shape
    zsize, groups = bias_ref.shape[1], bias_ref.shape[2]
    half = bias_ref.shape[4]
    size = groups * half

    blocks = []
    for c in range(2):
        up, down = weight_refs[2 * c], weight_refs[2 * c + 1]
        bias = [bias_ref[c, 0, i] for i in range(groups)]
        blocks.append(([(up, 0, size, 0), (down, 0, size, size)], bias, False))
    pieces = []
    for ref, (c, sources) in zip(weight_refs[4:], contents):
        for i, (k, m, h) in enumerate(sources):
            pieces.append((ref, i, bias_ref[c, depth ^ lax.rem(depth - k + zsize, zsize), (band ^ m) * 2 + h]))
    for i in range(0, len(pieces), groups):
        some = pieces[i : i + groups]
        runs = []
        for j, (ref, at, _) in enumerate(some):
            if runs and runs[-1][0] is ref and runs[-1][1] + runs[-1][2] == at * 2 * half:
                runs[-1][2] += 2 * half
            else:
                runs.append([ref, at * 2 * half, 2 * half, j * 2 * half])
        blocks.append((runs, [p[2] for p in some], True))

    def copies(n):
        slot = n % buf.shape[0]
        return [
            pltpu.make_async_copy(
                ref.at[pl.ds(first, count), :],
                buf.at[slot, pl.ds(to, count), :],
                sems.at[slot, i],
            )
            for i, (ref, first, count, to) in enumerate(blocks[n][0])
        ]

    ahead = buf.shape[0] - 1
    for n in range(ahead):
        for copy in copies(n):
            copy.start()

    x = x_ref[:rows, :].astype(F32)
    cent = x - jnp.mean(x, axis=1, keepdims=True)
    var = jnp.mean(cent * cent, axis=1, keepdims=True)
    normed[...] = (cent * lax.rsqrt(var + 1e-5) * gain_ref[...]).astype(BF16)
    acc[...] = x

    for n, (_, bias, mixed) in enumerate(blocks):
        for copy in copies(n):
            copy.wait()
        if n + ahead < len(blocks):
            for copy in copies(n + ahead):
                copy.start()
        slot = n % buf.shape[0]
        total = None
        hidden = []
        for part in range(2):
            ids = range(part * groups // 2, (part + 1) * groups // 2)
            if not mixed:
                up = buf[slot, ids[0] * half : ids[0] * half + size // 2, :]
            else:
                up = jnp.concatenate([buf[slot, 2 * g * half : (2 * g + 1) * half, :] for g in ids])
            v = mm_t(normed[...], up) + jnp.concatenate([bias[g] for g in ids], axis=1)
            hidden.append(gelu(v).astype(BF16))
        for part in range(2):
            ids = range(part * groups // 2, (part + 1) * groups // 2)
            if not mixed:
                down = buf[slot, size + ids[0] * half : size + ids[0] * half + size // 2, :]
            else:
                down = jnp.concatenate(
                    [buf[slot, (2 * g + 1) * half : (2 * g + 2) * half, :] for g in ids]
                )
            piece = mm(hidden[part], down)
            total = piece if total is None else total + piece
        acc[...] += total

    if len(out_ref.shape) == 2:
        out_ref[...] = acc[...].astype(BF16)
        return
    lay = rest[0]
    each, bands, _ = out_ref.shape
    whole = bands * each
    parts = earlier + 1
    for p in range(parts):
        part = earlier_refs[p] if p < earlier else acc
        for c in range(width // LANES):
            cols = slice(c * LANES, (c + 1) * LANES)
            if parts == 1:
                lay[c * whole : (c + 1) * whole, :] = part[:, cols]
                continue
            for i in range(rows // run):
                to = c * whole + (i * parts + p) * run
                lay[to : to + run, :] = part[i * run : (i + 1) * run, cols].astype(F32)
    for c in range(width // LANES):
        for px in range(each):
            out_ref[px, :, c * LANES : (c + 1) * LANES] = lay[
                pl.ds(c * whole + px, bands, stride=each), :
            ].astype(BF16)


def mlp(place, x, rows, gain, bias, own, gathered, contents, earlier, run, result):
    width = x.shape[1]
    size = own[0].shape[0]
    scratch = [
        pltpu.VMEM((rows, width), BF16),
        pltpu.VMEM((rows, width), F32),
        pltpu.VMEM((3, 2 * size, width), BF16),
        pltpu.SemaphoreType.DMA((3, 2 * bias.shape[2])),
    ]
    if result is None:
        shape = (rows, width)
    else:
        shape = result
        scratch.append(pltpu.VMEM((math.prod(result) // LANES, LANES), F32))
    vmem = pl.BlockSpec(memory_space=pltpu.VMEM)
    return pl.pallas_call(
        functools.partial(mlp_kernel, run, len(earlier), contents),
        out_shape=jax.ShapeDtypeStruct(shape, BF16),
        in_specs=[pl.BlockSpec(memory_space=pltpu.SMEM), vmem, vmem, vmem]
        + [pl.BlockSpec(memory_space=pl.ANY)] * (4 + len(gathered))
        + [vmem] * len(earlier),
        out_specs=vmem,
        scratch_shapes=scratch,
        compiler_params=pltpu.CompilerParams(vmem_limit_bytes=VMEM_LIMIT),
        cost_estimate=takes(0),
        name="mlp",
    )(place, x, gain[None], bias, *own, *gathered, *earlier)


def swap(x, axis, mask):
    count = lax.axis_size(axis)
    return lax.ppermute(x, axis, [(i, i ^ mask) for i in range(count)])


def selectors():
    row = np.arange(GROUP * 2 * LANES)[:, None]
    col = np.arange(SPAN * LANES)[None]
    within = row % (2 * LANES)
    sel = (within == (col // LANES) * CH_TOK + col % WIN) & (
        row // (2 * LANES) == col % LANES // WIN
    )
    row = np.arange(2 * LANES)[:, None]
    col = np.arange(SPAN * WIN)[None]
    sel1 = row == (col // WIN) * CH_TOK + col % WIN
    group = row // WIN == np.arange(LANES)[None] % SPAN
    return sel.astype(BF16), sel1.astype(BF16), group.astype(BF16)


def whole_spec(shape):
    return pl.BlockSpec(shape, lambda *_: (0,) * len(shape))


def spectral(place, near, far, tables, own, spec_out, nb, bands):
    bsize, zsize, some, _ = near.shape
    pixels = 2 * zsize * some
    width = spec_out.shape[0]
    lanes = (bands // SPAN + 1) * LANES
    args = [near, far, *selectors(), *tables, own, spec_out]
    part_px = pixels // GROUP
    return pl.pallas_call(
        functools.partial(spectral_kernel, nb, bands),
        out_shape=jax.ShapeDtypeStruct((nb, pixels, width), F32),
        in_specs=[pl.BlockSpec(memory_space=pltpu.SMEM)]
        + [pl.BlockSpec(memory_space=pltpu.VMEM)] * len(args),
        out_specs=pl.BlockSpec(memory_space=pltpu.VMEM),
        scratch_shapes=[
            pltpu.VMEM((pixels, lanes), BF16),
            pltpu.VMEM((LANES * (part_px + GAP), LANES), F32),
            pltpu.VMEM((HEADS * nb * (pixels + GAP), LANES), F32),
            pltpu.VMEM((HEADS * nb * (pixels + GAP), LANES), F32),
            pltpu.VMEM((pixels, LANES), F32),
        ],
        compiler_params=pltpu.CompilerParams(vmem_limit_bytes=VMEM_LIMIT),
        cost_estimate=takes(26),
        name="spectral",
    )(place, *args)


def local(
    radiance,
    stem_weight,
    band_embed,
    norm_spectral,
    spec_qkv,
    spec_out,
    norm_spatial,
    spat_qkv,
    spat_out,
    norm_mlp,
    up_weight,
    up_bias,
    down_weight,
):
    bands, width = band_embed.shape
    bsize, psize = lax.axis_size("band"), lax.axis_size("pix")
    devices = bsize * psize
    nb = -(-bands // devices)
    band, pix = lax.axis_index("band"), lax.axis_index("pix")
    base = jnp.minimum((pix * bsize + band) * nb, bands - nb).astype(jnp.int32)

    rows, channels = radiance.shape
    message = jnp.concatenate([radiance.astype(BF16), up_bias.reshape(rows, -1)], axis=1)
    own = lax.dynamic_slice_in_dim(band_embed, base, nb, 0)
    features = make_features(stem_weight, band_embed, own, norm_spectral)

    half = up_weight.shape[0] // bsize // 2
    share = []
    for h in range(2):
        at = (band * 2 + h) * half
        share.append(
            jnp.concatenate(
                [lax.dynamic_slice_in_dim(w, at, half, 0) for w in (up_weight, down_weight)]
            )
        )
    share = jnp.concatenate(share)

    def ring(x, step):
        return lax.ppermute(x, "pix", [(i, (i + 2 * step) % psize) for i in range(psize)])


    relayed = bsize == 4
    straight = (1, 2) if relayed else tuple(range(1, bsize))

    def relay(got, count):
        out = []
        for h, m in enumerate((2, 1)):
            part = [x.reshape(-1, 2, 2 * half, width)[:, h] for x in got[m]]
            part = jnp.concatenate(part).reshape(count * 2 * half, width)
            out.append(swap(part, "band", 3 - m))
        return out

    zs = jnp.stack([message] + [swap(message, "pix", 2 * k) for k in range(1, psize // 2)])
    zs, share, features = lax.optimization_barrier((zs, share, features))
    near = jnp.stack([zs] + [swap(zs, "band", k) for k in range(1, bsize)])
    tables = make_tables(bands, features[0], spec_qkv) + features[1:]
    shares = [ring(share, 1)]
    near, tables, shares, share, up_weight, down_weight = lax.optimization_barrier(
        (near, tables, shares, share, up_weight, down_weight)
    )
    far = swap(near, "pix", 1)
    first = {m: swap(shares[0], "band", m) for m in straight}
    while len(shares) < psize // 2 - 2:
        shares.append(ring(shares[-1], 1))
    shares.append(ring(share, -1))
    place = jnp.stack([base, band, pix // 2, pix % 2]).astype(jnp.int32)
    after_spectral = spectral(place, near, far, tables, own, spec_out, nb, bands)
    after_spectral, shares, first, up_weight, down_weight = lax.optimization_barrier(
        (after_spectral, shares, first, up_weight, down_weight)
    )
    own_weights = [up_weight, down_weight, swap(up_weight, "pix", 1), swap(down_weight, "pix", 1)]
    later = jnp.concatenate(shares[1:])
    rest = {m: swap(later, "band", m) for m in straight}
    bias = jnp.stack([near[0, :, :, channels:], far[0, :, :, channels:]])
    bias = bias.reshape(2, psize // 2, 2 * bsize, 1, half).astype(F32)
    pixels = after_spectral.shape[1]
    each = pixels // devices
    count = nb // 2 if nb % 2 == 0 and direct(pixels, devices, nb // 2) else nb
    arrived, results = [], []
    for start in range(0, nb, count):
        part = spatial(after_spectral, norm_spatial, spat_qkv, spat_out, start, count, devices)
        if start == 0:
            part, after_spectral, own_weights = lax.optimization_barrier(
                (part, after_spectral, own_weights)
            )
            held = [shares[0], later] + [x[m] for m in straight for x in (first, rest)]
            last_hop = []
            if relayed:
                last_hop = relay({m: (first[m], rest[m]) for m in straight}, psize // 2 - 1)
            held_far = [swap(x, "pix", 1) for x in held]
        else:
            part, arrived, held_far, last_hop = lax.optimization_barrier(
                (part, arrived, held_far, last_hop)
            )
        if direct(pixels, devices, count):
            moved = lax.all_to_all(part, ("pix", "band"), split_axis=0, concat_axis=0, tiled=True)
        else:
            moved = lax.all_to_all(part, ("pix", "band"), split_axis=1, concat_axis=0, tiled=True)
        arrived.append(moved.reshape(-1, width))
    last_hop, _ = lax.optimization_barrier((last_hop, part))
    gathered = [*held, *held_far, *last_hop, *[swap(x, "pix", 1) for x in last_hop]]
    one, more = ((1,), tuple(range(2, psize // 2)))
    ids = [
        tuple((k, m, h) for k in some for h in range(2)) for m in (0, *straight) for some in (one, more)
    ]
    hop_ids = [tuple((k, 3, h) for k in one + more) for h in range(len(last_hop))]
    contents = tuple((c, x) for part in (ids, hop_ids) for c in range(2) for x in part)
    run = count * each
    for i, moved in enumerate(arrived):
        last = i == len(arrived) - 1
        results.append(
            mlp(
                place,
                moved,
                bands // nb * run,
                norm_mlp,
                bias,
                own_weights,
                gathered,
                contents,
                results if last else [],
                run,
                (each, bands, width) if last else None,
            )
        )
    return results[-1]


def solution(mesh):
    placed = (
        P("pix", "band"),
        P(),
        P(),
        P(),
        P(),
        P(),
        P(),
        P(),
        P(),
        P(),
        P("pix", None),
        P("pix"),
        P("pix", None),
    )
    return jax.shard_map(
        local, mesh=mesh, in_specs=placed, out_specs=P(("pix", "band"), None, None), check_vma=False
    )
```

```python
import functools
import math

import jax
import jax.numpy as jnp
import numpy as np
from jax import lax
from jax.experimental import pallas as pl
from jax.experimental.pallas import tpu as pltpu
from jax.sharding import PartitionSpec as P

HEADS = 16
CH_TOK = 16
WIN = 2 * CH_TOK
LANES = 128
GROUP = LANES // WIN
SPAN = LANES // CH_TOK
GAP = 8
F32 = jnp.float32
BF16 = jnp.bfloat16
HIGH = lax.Precision.HIGHEST
LOG2_E = math.log2(math.e)
VMEM_LIMIT = 60 * 2**20


def takes(us):
    return pl.CostEstimate(flops=us * 10**9, bytes_accessed=2**20, transcendentals=0)


def mm(a, b):
    return jnp.dot(a, b, preferred_element_type=F32)


def mm_t(a, b):
    return lax.dot_general(a, b, (((1,), (1,)), ((), ())), preferred_element_type=F32)


def split2(x):
    hi = x.astype(BF16)
    return hi, (x - hi.astype(F32)).astype(BF16)


def mm_exact(a, b):
    return lax.dot_general(
        a, b, (((1,), (1,)), ((), ())), precision=HIGH, preferred_element_type=F32
    )


def feature_kernel(
    stem_ref, embed_ref, own_ref, gain_ref, feats_ref, gram_ref, cross_ref, const_ref, pieces_ref
):
    def centred(x):
        return x - jnp.mean(x, axis=1, keepdims=True)

    gain = gain_ref[...]
    stem = centred(stem_ref[...])
    bands, width = embed_ref.shape
    blank = jnp.zeros((LANES - bands, width), F32)
    embed = jnp.concatenate([centred(embed_ref[...]), blank])
    stem_g = stem * gain
    tail = jnp.zeros((8, width), F32)
    feats_ref[...] = jnp.concatenate(
        [embed * gain] + [stem_g] * GROUP + [centred(own_ref[...]) * gain, tail]
    ).astype(BF16)

    wide = SPAN * WIN
    forms = mm_exact(jnp.concatenate([embed, stem]), stem) * (1.0 / width)
    forms = jnp.concatenate([forms] * SPAN, axis=1)
    gram = jnp.concatenate([forms[LANES:]] * SPAN)
    same = (
        lax.broadcasted_iota(jnp.int32, (wide, wide), 0) // WIN
        == lax.broadcasted_iota(jnp.int32, (wide, wide), 1) // WIN
    )
    gram_ref[0], gram_ref[1] = split2(jnp.where(same, gram, 0.0))
    same = (
        lax.broadcasted_iota(jnp.int32, (LANES, wide), 0) % SPAN
        == lax.broadcasted_iota(jnp.int32, (LANES, wide), 1) // WIN
    )
    cross = jnp.where(same, 2.0 * forms[:LANES], 0.0)
    cross_ref[...] = jnp.sum(cross.reshape(LANES // SPAN, SPAN, wide), axis=1)
    const_ref[...] = mm_exact(jnp.ones((8, width), F32), embed * embed) * (1.0 / width)

    rest = stem_ref[...]
    pieces = []
    for _ in range(3):
        hi = rest.astype(BF16).astype(F32)
        pieces.append(hi)
        rest = rest - hi
    pieces_ref[...] = jnp.concatenate(pieces + [jnp.zeros_like(rest)]).astype(BF16)


def make_features(stem_weight, band_embed, own, gain):
    width = band_embed.shape[1]
    own8 = jnp.pad(own, ((0, 8 - own.shape[0]), (0, 0)))
    wide = SPAN * WIN
    vmem = pl.BlockSpec(memory_space=pltpu.VMEM)
    return pl.pallas_call(
        feature_kernel,
        out_shape=[
            jax.ShapeDtypeStruct((2 * LANES + 16, width), BF16),
            jax.ShapeDtypeStruct((2, wide, wide), BF16),
            jax.ShapeDtypeStruct((LANES // SPAN, wide), F32),
            jax.ShapeDtypeStruct((8, LANES), F32),
            jax.ShapeDtypeStruct((LANES, width), BF16),
        ],
        in_specs=[vmem] * 4,
        out_specs=[vmem] * 5,
        compiler_params=pltpu.CompilerParams(vmem_limit_bytes=VMEM_LIMIT),
        cost_estimate=takes(4),
        name="features",
    )(stem_weight, band_embed, own8, gain[None])


def tables_kernel(bands, feats_ref, qkv_ref, mse_ref, mee_ref, av_ref):
    a = mm(feats_ref[...], qkv_ref[...]).astype(BF16)
    heads = mse_ref.shape[1] // (2 * LANES)
    head = a.shape[1] // (3 * heads)
    keys = 2 * LANES
    scale = head**-0.5 * LOG2_E
    beyond = lax.broadcasted_iota(jnp.int32, (8, keys), 1)
    beyond = (beyond >= bands) & (beyond < LANES)
    for i in range(heads):
        c = 3 * i * head
        q = a[:, c : c + head]
        k = a[:keys, c + head : c + 2 * head]
        m = mm_t(q[LANES : LANES + WIN], k) * scale
        hi, lo = split2(m)
        mse_ref[:WIN, i * keys : (i + 1) * keys] = hi
        mse_ref[WIN:, i * keys : (i + 1) * keys] = lo
        m = mm_t(q[keys : keys + 16], k)[:8] * scale
        mee_ref[:, i * keys : (i + 1) * keys] = jnp.where(beyond, -1e30, m)
        if i % 2 == 0:
            av_ref[:, 2 * i * head : 2 * (i + 2) * head] = a[:keys, c + 2 * head : c + 6 * head]


def make_tables(bands, feats, qkv):
    steps = HEADS // 4
    width = qkv.shape[0]
    cols = qkv.shape[1] // steps
    return pl.pallas_call(
        functools.partial(tables_kernel, bands),
        grid=(steps,),
        out_shape=[
            jax.ShapeDtypeStruct((2 * WIN, HEADS * 2 * LANES), BF16),
            jax.ShapeDtypeStruct((8, HEADS * 2 * LANES), F32),
            jax.ShapeDtypeStruct((2 * LANES, HEADS * LANES), BF16),
        ],
        in_specs=[whole_spec(feats.shape), pl.BlockSpec((width, cols), lambda i: (0, i))],
        out_specs=[
            pl.BlockSpec((2 * WIN, 8 * LANES), lambda i: (0, i)),
            pl.BlockSpec((8, 8 * LANES), lambda i: (0, i)),
            pl.BlockSpec((2 * LANES, HEADS * LANES // steps), lambda i: (0, i)),
        ],
        compiler_params=pltpu.CompilerParams(vmem_limit_bytes=VMEM_LIMIT),
        cost_estimate=takes(8),
        name="tables",
    )(feats, qkv)


def spectral_kernel(
    nb,
    bands,
    place_ref,
    near_ref,
    far_ref,
    sel_ref,
    sel1_ref,
    group_ref,
    mse_ref,
    mee_ref,
    av_ref,
    gram_ref,
    cross_ref,
    const_ref,
    stem_ref,
    embed_ref,
    out_w_ref,
    out_ref,
    rad_ref,
    win,
    ue,
    uw,
    rstd,
):
    base, band, depth, core = (place_ref[k] for k in range(4))
    bsize, zsize, some, _ = near_ref.shape
    px, lanes = rad_ref.shape
    channels = bands * CH_TOK // bsize
    edge = CH_TOK // 2
    for k, ref in enumerate((near_ref, far_ref)):
        for kz in range(zsize):
            at = ((depth ^ kz) * 2 + (core ^ k)) * some
            pieces = [ref[b ^ band, kz, :, :channels].astype(F32) for b in range(bsize)]
            pieces = [jnp.zeros((some, edge), F32)] + pieces
            pieces.append(jnp.zeros((some, lanes - bands * CH_TOK - edge), F32))
            rad_ref[pl.ds(pl.multiple_of(at, some), some), :] = jnp.concatenate(
                pieces, axis=1
            ).astype(BF16)

    part_px = px // GROUP
    tiles = bands // SPAN
    wstep, ustep = part_px + GAP, px + GAP
    lane = lax.broadcasted_iota(jnp.int32, (px, LANES), 1)
    row = lax.broadcasted_iota(jnp.int32, (px, LANES), 0)
    blocks = [rad_ref[:, j * LANES : (j + 2) * LANES] for j in range(tiles)]

    packed = jnp.concatenate(
        [
            jnp.concatenate([b[i * part_px : (i + 1) * part_px] for i in range(GROUP)], axis=1)
            for b in blocks
        ]
    )
    for i in range(0, SPAN, 2):
        wide = mm(packed, sel_ref[:, i * LANES : (i + 2) * LANES])
        for j in range(tiles):
            for k in range(2):
                t = j * SPAN + i + k
                win[t * wstep : t * wstep + part_px, :] = wide[
                    j * part_px : (j + 1) * part_px, k * LANES : (k + 1) * LANES
                ]
    for t in range(bands, LANES):
        win[t * wstep : t * wstep + part_px, :] = jnp.zeros((part_px, LANES), F32)

    acc = jnp.zeros((px, LANES), F32)
    thin = mm(jnp.concatenate(blocks), sel1_ref[...])
    thin_b = thin.astype(BF16)
    form = mm(thin_b, gram_ref[0]) + mm(thin_b, gram_ref[1])
    for j in range(tiles):
        rows = slice(j * px, (j + 1) * px)
        hi, lo = split2(thin[rows] * (form[rows] + cross_ref[j : j + 1, :]))
        summed = mm(hi, group_ref[...]) + mm(lo, group_ref[...])
        acc = jnp.where(lane // SPAN == j, summed, acc)
    scale = lax.rsqrt(acc + const_ref[:1, :] + 1e-5)
    rstd[...] = scale

    own, rq = [], []
    at = lax.broadcasted_iota(jnp.int32, (2 * LANES, LANES), 0)
    to = lax.broadcasted_iota(jnp.int32, (2 * LANES, LANES), 1)
    for i in range(nb):
        t = base + i
        cols = pl.ds(pl.multiple_of(t // SPAN * LANES, LANES), 2 * LANES)
        pick = (at == t % SPAN * CH_TOK + to % WIN).astype(F32).astype(BF16)
        own.append(mm(rad_ref[:, cols], pick).astype(BF16))
        rq.append(jnp.sum(jnp.where(lane == t, scale, 0.0), axis=1, keepdims=True))
    own = jnp.concatenate(own)
    keep = lane // WIN == row // part_px
    for h in range(0, HEADS, 2):
        both = slice(2 * h * LANES, 2 * (h + 2) * LANES)
        parts = mm(own[:, : 2 * WIN], mse_ref[:, both])
        for i in range(nb):
            part = (parts[i * px : (i + 1) * px] + mee_ref[i : i + 1, both]) * rq[i]
            for k in range(2):
                r = ((h + k) * nb + i) * ustep
                ue[r : r + px, :] = part[:, 2 * k * LANES : (2 * k + 1) * LANES]
                uw[r : r + px, :] = jnp.where(
                    keep, part[:, (2 * k + 1) * LANES : (2 * k + 2) * LANES], 0.0
                )

    rows = HEADS * nb
    step = math.gcd(8, part_px)

    def groups(g, _):
        ids = [g * step + k for k in range(step)]
        ws = [win[pl.ds(p, LANES, stride=wstep), :].astype(BF16) for p in ids]
        ls = [
            jnp.concatenate(
                [uw[pl.ds(i * part_px + p, rows, stride=ustep), :] for i in range(GROUP)]
            ).astype(BF16)
            for p in ids
        ]
        ss = [mm_t(a, w) for a, w in zip(ls, ws)]
        es = []
        for k, p in enumerate(ids):
            for i in range(GROUP):
                q = i * part_px + p
                rki = rstd[pl.ds(q, 1), :]
                s = (ss[k][i * rows : (i + 1) * rows] + ue[pl.ds(q, rows, stride=ustep), :]) * rki
                e = jnp.exp2(s - jnp.max(s, axis=1, keepdims=True))
                e = e * (1.0 / jnp.sum(e, axis=1, keepdims=True)) * rki
                ue[pl.ds(q, rows, stride=ustep), :] = e
                es.append(e)
        for k, p in enumerate(ids):
            z = mm(jnp.concatenate(es[k * GROUP : (k + 1) * GROUP]).astype(BF16), ws[k])
            for i in range(GROUP):
                uw[pl.ds(i * part_px + p, rows, stride=ustep), :] = z[i * rows : (i + 1) * rows]
        return 0

    lax.fori_loop(0, part_px // step, groups, 0)

    half = lax.broadcasted_iota(jnp.int32, (nb * px, LANES), 1) < LANES // 2
    mixes = []
    for h in range(0, HEADS, 2):
        outs = []
        for k in range(2):
            both = []
            for i in range(nb):
                r = ((h + k) * nb + i) * ustep
                z = jnp.where(keep, uw[r : r + px, :], 0.0)
                both.append(jnp.concatenate([ue[r : r + px, :], z], axis=1).astype(BF16))
            weights = av_ref[:, (h + k) * LANES : (h + k + 1) * LANES]
            outs.append(mm(jnp.concatenate(both), weights))
        mixes.append(jnp.where(half, outs[0], outs[1]).astype(BF16))
    mixes = jnp.concatenate(mixes, axis=1)
    chunk = 2 * LANES
    for c in range(0, out_w_ref.shape[1], chunk):
        cols = slice(c, c + chunk)
        update = mm(mixes, out_w_ref[:, cols])
        token = mm(own, stem_ref[:, cols])
        for i in range(nb):
            rows = slice(i * px, (i + 1) * px)
            rounded = (token[rows] + embed_ref[i : i + 1, cols]).astype(BF16)
            out_ref[i, :, cols] = rounded.astype(F32) + update[rows]


def spatial_kernel(
    devices, x_ref, gain_ref, qkv_ref, w_ref, out_ref, normed, proj, mixed, qkv_buf, w_buf, sems
):
    count, pixels, width = x_ref.shape
    pairs = HEADS // 2
    chunk = 3 * width // pairs
    copies = [
        pltpu.make_async_copy(qkv_ref, qkv_buf, sems.at[0]),
        pltpu.make_async_copy(w_ref, w_buf, sems.at[1]),
    ]
    for copy in copies:
        copy.start()

    for b in range(count):
        x = x_ref[b]
        cent = x - jnp.mean(x, axis=1, keepdims=True)
        var = jnp.mean(cent * cent, axis=1, keepdims=True)
        value = cent * lax.rsqrt(var + 1e-5) * gain_ref[...]
        normed[b * pixels : (b + 1) * pixels, :] = value.astype(BF16)

    head = width // HEADS
    low = lax.broadcasted_iota(jnp.int32, (pixels, 2 * head), 1) < head
    copies[0].wait()
    for c in range(0, 3 * width, width):
        proj[:, c : c + width] = mm(normed[...], qkv_buf[:, c : c + width]).astype(BF16)
    for b in range(count):
        rows = slice(b * pixels, (b + 1) * pixels)
        for pair in range(pairs):
            c = pair * chunk
            t0 = proj[rows, c : c + 2 * head]
            t1 = proj[rows, c + 2 * head : c + 4 * head]
            t2 = proj[rows, c + 4 * head : c + 6 * head]
            zero = jnp.zeros_like(t0)
            r0 = jnp.concatenate([t0[:, head:], t0[:, :head]], axis=1)
            r2 = jnp.concatenate([t2[:, head:], t2[:, :head]], axis=1)
            outs = []
            for q, k, v in (
                (jnp.where(low, t0, zero), r0, t1),
                (jnp.where(low, zero, t1), r2, t2),
            ):
                s = mm_t(q, k)
                e = jnp.exp((s - jnp.max(s, axis=1, keepdims=True)) * (head**-0.5))
                total = jnp.sum(e, axis=1, keepdims=True)
                outs.append(mm(e.astype(BF16), v) * (1.0 / total))
            mixed[rows, pair * 2 * head : (pair + 1) * 2 * head] = jnp.where(
                low, outs[0], outs[1]
            ).astype(BF16)

    copies[1].wait()
    chunk = 2 * LANES
    for c in range(0, width, chunk):
        cols = slice(c, c + chunk)
        update = mm(mixed[...], w_buf[:, cols])
        ys = [x_ref[b, :, cols] + update[b * pixels : (b + 1) * pixels] for b in range(count)]
        if devices:
            ys = [y.reshape(devices, pixels // devices, chunk) for y in ys]
            out_ref[:, :, cols] = jnp.concatenate(ys, axis=1).astype(BF16)
        else:
            for b in range(count):
                out_ref[b, :, cols] = ys[b].astype(BF16)


def spatial(x, gain, qkv, w, first, count, devices):
    nb, pixels, width = x.shape
    if direct(pixels, devices, count):
        shape = (devices, count * pixels // devices, width)
    else:
        devices, shape = 0, (count, pixels, width)
    return pl.pallas_call(
        functools.partial(spatial_kernel, devices),
        grid=(1,),
        out_shape=jax.ShapeDtypeStruct(shape, BF16),
        in_specs=[
            pl.BlockSpec((count, pixels, width), lambda i: (first // count, 0, 0)),
            whole_spec((1, width)),
            pl.BlockSpec(memory_space=pl.ANY),
            pl.BlockSpec(memory_space=pl.ANY),
        ],
        out_specs=whole_spec(shape),
        scratch_shapes=[
            pltpu.VMEM((count * pixels, width), BF16),
            pltpu.VMEM((count * pixels, 3 * width), BF16),
            pltpu.VMEM((count * pixels, width), BF16),
            pltpu.VMEM(qkv.shape, BF16),
            pltpu.VMEM((width, width), BF16),
            pltpu.SemaphoreType.DMA((2,)),
        ],
        compiler_params=pltpu.CompilerParams(vmem_limit_bytes=VMEM_LIMIT),
        cost_estimate=takes(15),
        name="spatial",
    )(x, gain[None], qkv, w)


def direct(pixels, devices, count):
    each = pixels // devices
    return each % 8 == 0 and (each * count) % 16 == 0


def gelu(v):
    half = 0.5 * v
    inner = v * ((2 / math.pi) ** 0.5 + (2 / math.pi) ** 0.5 * 0.044715 * (v * v))
    return half + half * jnp.tanh(inner)


def mlp_kernel(run, earlier, contents, place_ref, x_ref, gain_ref, bias_ref, *refs):
    n_weights = 4 + len(contents)
    weight_refs, refs = refs[:n_weights], refs[n_weights:]
    earlier_refs, refs = refs[:earlier], refs[earlier:]
    out_ref, normed, acc, buf, sems, *rest = refs
    band, depth = place_ref[1], place_ref[2]
    rows, width = normed.shape
    zsize, groups = bias_ref.shape[1], bias_ref.shape[2]
    half = bias_ref.shape[4]
    size = groups * half

    blocks = []
    for c in range(2):
        up, down = weight_refs[2 * c], weight_refs[2 * c + 1]
        bias = [bias_ref[c, 0, i] for i in range(groups)]
        blocks.append(([(up, 0, size, 0), (down, 0, size, size)], bias, False))
    pieces = []
    for ref, (c, sources) in zip(weight_refs[4:], contents):
        for i, (k, m, h) in enumerate(sources):
            pieces.append((ref, i, bias_ref[c, depth ^ lax.rem(depth - k + zsize, zsize), (band ^ m) * 2 + h]))
    for i in range(0, len(pieces), groups):
        some = pieces[i : i + groups]
        runs = []
        for j, (ref, at, _) in enumerate(some):
            if runs and runs[-1][0] is ref and runs[-1][1] + runs[-1][2] == at * 2 * half:
                runs[-1][2] += 2 * half
            else:
                runs.append([ref, at * 2 * half, 2 * half, j * 2 * half])
        blocks.append((runs, [p[2] for p in some], True))

    def copies(n):
        slot = n % buf.shape[0]
        return [
            pltpu.make_async_copy(
                ref.at[pl.ds(first, count), :],
                buf.at[slot, pl.ds(to, count), :],
                sems.at[slot, i],
            )
            for i, (ref, first, count, to) in enumerate(blocks[n][0])
        ]

    ahead = buf.shape[0] - 1
    for n in range(ahead):
        for copy in copies(n):
            copy.start()

    x = x_ref[:rows, :].astype(F32)
    cent = x - jnp.mean(x, axis=1, keepdims=True)
    var = jnp.mean(cent * cent, axis=1, keepdims=True)
    normed[...] = (cent * lax.rsqrt(var + 1e-5) * gain_ref[...]).astype(BF16)
    acc[...] = x

    for n, (_, bias, mixed) in enumerate(blocks):
        for copy in copies(n):
            copy.wait()
        if n + ahead < len(blocks):
            for copy in copies(n + ahead):
                copy.start()
        slot = n % buf.shape[0]
        total = None
        hidden = []
        for part in range(2):
            ids = range(part * groups // 2, (part + 1) * groups // 2)
            if not mixed:
                up = buf[slot, ids[0] * half : ids[0] * half + size // 2, :]
            else:
                up = jnp.concatenate([buf[slot, 2 * g * half : (2 * g + 1) * half, :] for g in ids])
            v = mm_t(normed[...], up) + jnp.concatenate([bias[g] for g in ids], axis=1)
            hidden.append(gelu(v).astype(BF16))
        for part in range(2):
            ids = range(part * groups // 2, (part + 1) * groups // 2)
            if not mixed:
                down = buf[slot, size + ids[0] * half : size + ids[0] * half + size // 2, :]
            else:
                down = jnp.concatenate(
                    [buf[slot, (2 * g + 1) * half : (2 * g + 2) * half, :] for g in ids]
                )
            piece = mm(hidden[part], down)
            total = piece if total is None else total + piece
        acc[...] += total

    if len(out_ref.shape) == 2:
        out_ref[...] = acc[...].astype(BF16)
        return
    lay = rest[0]
    each, bands, _ = out_ref.shape
    whole = bands * each
    parts = earlier + 1
    for p in range(parts):
        part = earlier_refs[p] if p < earlier else acc
        for c in range(width // LANES):
            cols = slice(c * LANES, (c + 1) * LANES)
            if parts == 1:
                lay[c * whole : (c + 1) * whole, :] = part[:, cols]
                continue
            for i in range(rows // run):
                to = c * whole + (i * parts + p) * run
                lay[to : to + run, :] = part[i * run : (i + 1) * run, cols].astype(F32)
    for c in range(width // LANES):
        for px in range(each):
            out_ref[px, :, c * LANES : (c + 1) * LANES] = lay[
                pl.ds(c * whole + px, bands, stride=each), :
            ].astype(BF16)


def mlp(place, x, rows, gain, bias, own, gathered, contents, earlier, run, result):
    width = x.shape[1]
    size = own[0].shape[0]
    scratch = [
        pltpu.VMEM((rows, width), BF16),
        pltpu.VMEM((rows, width), F32),
        pltpu.VMEM((3, 2 * size, width), BF16),
        pltpu.SemaphoreType.DMA((3, 2 * bias.shape[2])),
    ]
    if result is None:
        shape = (rows, width)
    else:
        shape = result
        scratch.append(pltpu.VMEM((math.prod(result) // LANES, LANES), F32))
    vmem = pl.BlockSpec(memory_space=pltpu.VMEM)
    return pl.pallas_call(
        functools.partial(mlp_kernel, run, len(earlier), contents),
        grid=(1,),
        out_shape=jax.ShapeDtypeStruct(shape, BF16),
        in_specs=[pl.BlockSpec(memory_space=pltpu.SMEM), vmem, vmem, vmem]
        + [pl.BlockSpec(memory_space=pl.ANY)] * (4 + len(gathered))
        + [vmem] * len(earlier),
        out_specs=whole_spec(shape),
        scratch_shapes=scratch,
        compiler_params=pltpu.CompilerParams(vmem_limit_bytes=VMEM_LIMIT),
        cost_estimate=takes(0),
        name="mlp",
    )(place, x, gain[None], bias, *own, *gathered, *earlier)


def swap(x, axis, mask):
    count = lax.axis_size(axis)
    return lax.ppermute(x, axis, [(i, i ^ mask) for i in range(count)])


def selectors():
    row = np.arange(GROUP * 2 * LANES)[:, None]
    col = np.arange(SPAN * LANES)[None]
    within = row % (2 * LANES)
    sel = (within == (col // LANES) * CH_TOK + col % WIN) & (
        row // (2 * LANES) == col % LANES // WIN
    )
    row = np.arange(2 * LANES)[:, None]
    col = np.arange(SPAN * WIN)[None]
    sel1 = row == (col // WIN) * CH_TOK + col % WIN
    group = row // WIN == np.arange(LANES)[None] % SPAN
    return sel.astype(BF16), sel1.astype(BF16), group.astype(BF16)


def whole_spec(shape):
    return pl.BlockSpec(shape, lambda *_: (0,) * len(shape))


def spectral(place, near, far, tables, own, spec_out, nb, bands):
    bsize, zsize, some, _ = near.shape
    pixels = 2 * zsize * some
    width = spec_out.shape[0]
    lanes = (bands // SPAN + 1) * LANES
    args = [near, far, *selectors(), *tables, own, spec_out]
    part_px = pixels // GROUP
    return pl.pallas_call(
        functools.partial(spectral_kernel, nb, bands),
        out_shape=jax.ShapeDtypeStruct((nb, pixels, width), F32),
        in_specs=[pl.BlockSpec(memory_space=pltpu.SMEM)]
        + [pl.BlockSpec(memory_space=pltpu.VMEM)] * len(args),
        out_specs=pl.BlockSpec(memory_space=pltpu.VMEM),
        scratch_shapes=[
            pltpu.VMEM((pixels, lanes), BF16),
            pltpu.VMEM((LANES * (part_px + GAP), LANES), F32),
            pltpu.VMEM((HEADS * nb * (pixels + GAP), LANES), F32),
            pltpu.VMEM((HEADS * nb * (pixels + GAP), LANES), F32),
            pltpu.VMEM((pixels, LANES), F32),
        ],
        compiler_params=pltpu.CompilerParams(vmem_limit_bytes=VMEM_LIMIT),
        cost_estimate=takes(26),
        name="spectral",
    )(place, *args)


def local(
    radiance,
    stem_weight,
    band_embed,
    norm_spectral,
    spec_qkv,
    spec_out,
    norm_spatial,
    spat_qkv,
    spat_out,
    norm_mlp,
    up_weight,
    up_bias,
    down_weight,
):
    bands, width = band_embed.shape
    bsize, psize = lax.axis_size("band"), lax.axis_size("pix")
    devices = bsize * psize
    nb = -(-bands // devices)
    band, pix = lax.axis_index("band"), lax.axis_index("pix")
    base = jnp.minimum((pix * bsize + band) * nb, bands - nb).astype(jnp.int32)

    rows, channels = radiance.shape
    message = jnp.concatenate([radiance.astype(BF16), up_bias.reshape(rows, -1)], axis=1)
    own = lax.dynamic_slice_in_dim(band_embed, base, nb, 0)
    features = make_features(stem_weight, band_embed, own, norm_spectral)

    half = up_weight.shape[0] // bsize // 2
    share = []
    for h in range(2):
        at = (band * 2 + h) * half
        share.append(
            jnp.concatenate(
                [lax.dynamic_slice_in_dim(w, at, half, 0) for w in (up_weight, down_weight)]
            )
        )
    share = jnp.concatenate(share)

    def ring(x, step):
        return lax.ppermute(x, "pix", [(i, (i + 2 * step) % psize) for i in range(psize)])


    relayed = bsize == 4
    straight = (1, 2) if relayed else tuple(range(1, bsize))

    def relay(got, count):
        out = []
        for h, m in enumerate((2, 1)):
            part = [x.reshape(-1, 2, 2 * half, width)[:, h] for x in got[m]]
            part = jnp.concatenate(part).reshape(count * 2 * half, width)
            out.append(swap(part, "band", 3 - m))
        return out

    zs = jnp.stack([message] + [swap(message, "pix", 2 * k) for k in range(1, psize // 2)])
    share, features = lax.optimization_barrier((share, features))
    shares = [ring(share, 1)]
    zs, features = lax.optimization_barrier((zs, features))
    near = jnp.stack([zs] + [swap(zs, "band", k) for k in range(1, bsize)])
    tables = make_tables(bands, features[0], spec_qkv) + features[1:]
    near, tables, shares, share, up_weight, down_weight = lax.optimization_barrier(
        (near, tables, shares, share, up_weight, down_weight)
    )
    far = swap(near, "pix", 1)
    first = {m: swap(shares[0], "band", m) for m in straight}
    while len(shares) < psize // 2 - 2:
        shares.append(ring(shares[-1], 1))
    shares.append(ring(share, -1))
    place = jnp.stack([base, band, pix // 2, pix % 2]).astype(jnp.int32)
    after_spectral = spectral(place, near, far, tables, own, spec_out, nb, bands)
    after_spectral, shares, first, up_weight, down_weight = lax.optimization_barrier(
        (after_spectral, shares, first, up_weight, down_weight)
    )
    own_weights = [up_weight, down_weight, swap(up_weight, "pix", 1), swap(down_weight, "pix", 1)]
    later = jnp.concatenate(shares[1:])
    rest = {m: swap(later, "band", m) for m in straight}
    bias = jnp.stack([near[0, :, :, channels:], far[0, :, :, channels:]])
    bias = bias.reshape(2, psize // 2, 2 * bsize, 1, half).astype(F32)
    pixels = after_spectral.shape[1]
    each = pixels // devices
    count = nb // 2 if nb % 2 == 0 and direct(pixels, devices, nb // 2) else nb
    arrived, results = [], []
    for start in range(0, nb, count):
        part = spatial(after_spectral, norm_spatial, spat_qkv, spat_out, start, count, devices)
        if start == 0:
            part, after_spectral, own_weights = lax.optimization_barrier(
                (part, after_spectral, own_weights)
            )
            held = [shares[0], later] + [x[m] for m in straight for x in (first, rest)]
            last_hop = []
            if relayed:
                last_hop = relay({m: (first[m], rest[m]) for m in straight}, psize // 2 - 1)
            held_far = [swap(x, "pix", 1) for x in held]
        else:
            part, arrived, held_far, last_hop = lax.optimization_barrier(
                (part, arrived, held_far, last_hop)
            )
        if direct(pixels, devices, count):
            moved = lax.all_to_all(part, ("pix", "band"), split_axis=0, concat_axis=0, tiled=True)
        else:
            moved = lax.all_to_all(part, ("pix", "band"), split_axis=1, concat_axis=0, tiled=True)
        arrived.append(moved.reshape(-1, width))
    last_hop, _ = lax.optimization_barrier((last_hop, part))
    gathered = [*held, *held_far, *last_hop, *[swap(x, "pix", 1) for x in last_hop]]
    one, more = ((1,), tuple(range(2, psize // 2)))
    ids = [
        tuple((k, m, h) for k in some for h in range(2)) for m in (0, *straight) for some in (one, more)
    ]
    hop_ids = [tuple((k, 3, h) for k in one + more) for h in range(len(last_hop))]
    contents = tuple((c, x) for part in (ids, hop_ids) for c in range(2) for x in part)
    run = count * each
    for i, moved in enumerate(arrived):
        last = i == len(arrived) - 1
        results.append(
            mlp(
                place,
                moved,
                bands // nb * run,
                norm_mlp,
                bias,
                own_weights,
                gathered,
                contents,
                results if last else [],
                run,
                (each, bands, width) if last else None,
            )
        )
    return results[-1]


def solution(mesh):
    placed = (
        P("pix", "band"),
        P(),
        P(),
        P(),
        P(),
        P(),
        P(),
        P(),
        P(),
        P(),
        P("pix", None),
        P("pix"),
        P("pix", None),
    )
    return jax.shard_map(
        local, mesh=mesh, in_specs=placed, out_specs=P(("pix", "band"), None, None), check_vma=False
    )
```

```python
import functools
import math

import jax
import jax.numpy as jnp
import numpy as np
from jax import lax
from jax.experimental import pallas as pl
from jax.experimental.pallas import tpu as pltpu
from jax.sharding import PartitionSpec as P

HEADS = 16
CH_TOK = 16
WIN = 2 * CH_TOK
LANES = 128
GROUP = LANES // WIN
SPAN = LANES // CH_TOK
GAP = 8
F32 = jnp.float32
BF16 = jnp.bfloat16
HIGH = lax.Precision.HIGHEST
LOG2_E = math.log2(math.e)
VMEM_LIMIT = 60 * 2**20


def takes(us):
    return pl.CostEstimate(flops=us * 10**9, bytes_accessed=2**20, transcendentals=0)


def mm(a, b):
    return jnp.dot(a, b, preferred_element_type=F32)


def mm_t(a, b):
    return lax.dot_general(a, b, (((1,), (1,)), ((), ())), preferred_element_type=F32)


def split2(x):
    hi = x.astype(BF16)
    return hi, (x - hi.astype(F32)).astype(BF16)


def mm_exact(a, b):
    return lax.dot_general(
        a, b, (((1,), (1,)), ((), ())), precision=HIGH, preferred_element_type=F32
    )


def feature_kernel(
    stem_ref, embed_ref, own_ref, gain_ref, feats_ref, gram_ref, cross_ref, const_ref, pieces_ref
):
    def centred(x):
        return x - jnp.mean(x, axis=1, keepdims=True)

    gain = gain_ref[...]
    stem = centred(stem_ref[...])
    bands, width = embed_ref.shape
    blank = jnp.zeros((LANES - bands, width), F32)
    embed = jnp.concatenate([centred(embed_ref[...]), blank])
    stem_g = stem * gain
    tail = jnp.zeros((8, width), F32)
    feats_ref[...] = jnp.concatenate(
        [embed * gain] + [stem_g] * GROUP + [centred(own_ref[...]) * gain, tail]
    ).astype(BF16)

    wide = SPAN * WIN
    forms = mm_exact(jnp.concatenate([embed, stem]), stem) * (1.0 / width)
    forms = jnp.concatenate([forms] * SPAN, axis=1)
    gram = jnp.concatenate([forms[LANES:]] * SPAN)
    same = (
        lax.broadcasted_iota(jnp.int32, (wide, wide), 0) // WIN
        == lax.broadcasted_iota(jnp.int32, (wide, wide), 1) // WIN
    )
    gram_ref[0], gram_ref[1] = split2(jnp.where(same, gram, 0.0))
    same = (
        lax.broadcasted_iota(jnp.int32, (LANES, wide), 0) % SPAN
        == lax.broadcasted_iota(jnp.int32, (LANES, wide), 1) // WIN
    )
    cross = jnp.where(same, 2.0 * forms[:LANES], 0.0)
    cross_ref[...] = jnp.sum(cross.reshape(LANES // SPAN, SPAN, wide), axis=1)
    const_ref[...] = mm_exact(jnp.ones((8, width), F32), embed * embed) * (1.0 / width)

    rest = stem_ref[...]
    pieces = []
    for _ in range(3):
        hi = rest.astype(BF16).astype(F32)
        pieces.append(hi)
        rest = rest - hi
    pieces_ref[...] = jnp.concatenate(pieces + [jnp.zeros_like(rest)]).astype(BF16)


def make_features(stem_weight, band_embed, own, gain):
    width = band_embed.shape[1]
    own8 = jnp.pad(own, ((0, 8 - own.shape[0]), (0, 0)))
    wide = SPAN * WIN
    vmem = pl.BlockSpec(memory_space=pltpu.VMEM)
    return pl.pallas_call(
        feature_kernel,
        out_shape=[
            jax.ShapeDtypeStruct((2 * LANES + 16, width), BF16),
            jax.ShapeDtypeStruct((2, wide, wide), BF16),
            jax.ShapeDtypeStruct((LANES // SPAN, wide), F32),
            jax.ShapeDtypeStruct((8, LANES), F32),
            jax.ShapeDtypeStruct((LANES, width), BF16),
        ],
        in_specs=[vmem] * 4,
        out_specs=[vmem] * 5,
        compiler_params=pltpu.CompilerParams(vmem_limit_bytes=VMEM_LIMIT),
        cost_estimate=takes(4),
        name="features",
    )(stem_weight, band_embed, own8, gain[None])


def tables_kernel(bands, feats_ref, qkv_ref, mse_ref, mee_ref, av_ref):
    a = mm(feats_ref[...], qkv_ref[...]).astype(BF16)
    heads = mse_ref.shape[1] // (2 * LANES)
    head = a.shape[1] // (3 * heads)
    keys = 2 * LANES
    scale = head**-0.5 * LOG2_E
    beyond = lax.broadcasted_iota(jnp.int32, (8, keys), 1)
    beyond = (beyond >= bands) & (beyond < LANES)
    for i in range(heads):
        c = 3 * i * head
        q = a[:, c : c + head]
        k = a[:keys, c + head : c + 2 * head]
        m = mm_t(q[LANES : LANES + WIN], k) * scale
        hi, lo = split2(m)
        mse_ref[:WIN, i * keys : (i + 1) * keys] = hi
        mse_ref[WIN:, i * keys : (i + 1) * keys] = lo
        m = mm_t(q[keys : keys + 16], k)[:8] * scale
        mee_ref[:, i * keys : (i + 1) * keys] = jnp.where(beyond, -1e30, m)
        if i % 2 == 0:
            av_ref[:, 2 * i * head : 2 * (i + 2) * head] = a[:keys, c + 2 * head : c + 6 * head]


def make_tables(bands, feats, qkv):
    steps = HEADS // 4
    width = qkv.shape[0]
    cols = qkv.shape[1] // steps
    return pl.pallas_call(
        functools.partial(tables_kernel, bands),
        grid=(steps,),
        out_shape=[
            jax.ShapeDtypeStruct((2 * WIN, HEADS * 2 * LANES), BF16),
            jax.ShapeDtypeStruct((8, HEADS * 2 * LANES), F32),
            jax.ShapeDtypeStruct((2 * LANES, HEADS * LANES), BF16),
        ],
        in_specs=[whole_spec(feats.shape), pl.BlockSpec((width, cols), lambda i: (0, i))],
        out_specs=[
            pl.BlockSpec((2 * WIN, 8 * LANES), lambda i: (0, i)),
            pl.BlockSpec((8, 8 * LANES), lambda i: (0, i)),
            pl.BlockSpec((2 * LANES, HEADS * LANES // steps), lambda i: (0, i)),
        ],
        compiler_params=pltpu.CompilerParams(vmem_limit_bytes=VMEM_LIMIT),
        cost_estimate=takes(8),
        name="tables",
    )(feats, qkv)


def spectral_kernel(
    nb,
    bands,
    place_ref,
    near_ref,
    far_ref,
    sel_ref,
    sel1_ref,
    group_ref,
    mse_ref,
    mee_ref,
    av_ref,
    gram_ref,
    cross_ref,
    const_ref,
    stem_ref,
    embed_ref,
    out_w_ref,
    out_ref,
    rad_ref,
    win,
    ue,
    uw,
    rstd,
):
    base, band, depth, core = (place_ref[k] for k in range(4))
    bsize, zsize, some, _ = near_ref.shape
    px, lanes = rad_ref.shape
    channels = bands * CH_TOK // bsize
    edge = CH_TOK // 2
    for k, ref in enumerate((near_ref, far_ref)):
        for kz in range(zsize):
            at = ((depth ^ kz) * 2 + (core ^ k)) * some
            pieces = [ref[b ^ band, kz, :, :channels].astype(F32) for b in range(bsize)]
            pieces = [jnp.zeros((some, edge), F32)] + pieces
            pieces.append(jnp.zeros((some, lanes - bands * CH_TOK - edge), F32))
            rad_ref[pl.ds(pl.multiple_of(at, some), some), :] = jnp.concatenate(
                pieces, axis=1
            ).astype(BF16)

    part_px = px // GROUP
    tiles = bands // SPAN
    wstep, ustep = part_px + GAP, px + GAP
    lane = lax.broadcasted_iota(jnp.int32, (px, LANES), 1)
    row = lax.broadcasted_iota(jnp.int32, (px, LANES), 0)
    blocks = [rad_ref[:, j * LANES : (j + 2) * LANES] for j in range(tiles)]

    packed = jnp.concatenate(
        [
            jnp.concatenate([b[i * part_px : (i + 1) * part_px] for i in range(GROUP)], axis=1)
            for b in blocks
        ]
    )
    for i in range(0, SPAN, 2):
        wide = mm(packed, sel_ref[:, i * LANES : (i + 2) * LANES])
        for j in range(tiles):
            for k in range(2):
                t = j * SPAN + i + k
                win[t * wstep : t * wstep + part_px, :] = wide[
                    j * part_px : (j + 1) * part_px, k * LANES : (k + 1) * LANES
                ]
    for t in range(bands, LANES):
        win[t * wstep : t * wstep + part_px, :] = jnp.zeros((part_px, LANES), F32)

    acc = jnp.zeros((px, LANES), F32)
    thin = mm(jnp.concatenate(blocks), sel1_ref[...])
    thin_b = thin.astype(BF16)
    form = mm(thin_b, gram_ref[0]) + mm(thin_b, gram_ref[1])
    for j in range(tiles):
        rows = slice(j * px, (j + 1) * px)
        hi, lo = split2(thin[rows] * (form[rows] + cross_ref[j : j + 1, :]))
        summed = mm(hi, group_ref[...]) + mm(lo, group_ref[...])
        acc = jnp.where(lane // SPAN == j, summed, acc)
    scale = lax.rsqrt(acc + const_ref[:1, :] + 1e-5)
    rstd[...] = scale

    own, rq = [], []
    at = lax.broadcasted_iota(jnp.int32, (2 * LANES, LANES), 0)
    to = lax.broadcasted_iota(jnp.int32, (2 * LANES, LANES), 1)
    for i in range(nb):
        t = base + i
        cols = pl.ds(pl.multiple_of(t // SPAN * LANES, LANES), 2 * LANES)
        pick = (at == t % SPAN * CH_TOK + to % WIN).astype(F32).astype(BF16)
        own.append(mm(rad_ref[:, cols], pick).astype(BF16))
        rq.append(jnp.sum(jnp.where(lane == t, scale, 0.0), axis=1, keepdims=True))
    own = jnp.concatenate(own)
    keep = lane // WIN == row // part_px
    for h in range(0, HEADS, 2):
        both = slice(2 * h * LANES, 2 * (h + 2) * LANES)
        parts = mm(own[:, : 2 * WIN], mse_ref[:, both])
        for i in range(nb):
            part = (parts[i * px : (i + 1) * px] + mee_ref[i : i + 1, both]) * rq[i]
            for k in range(2):
                r = ((h + k) * nb + i) * ustep
                ue[r : r + px, :] = part[:, 2 * k * LANES : (2 * k + 1) * LANES]
                uw[r : r + px, :] = jnp.where(
                    keep, part[:, (2 * k + 1) * LANES : (2 * k + 2) * LANES], 0.0
                )

    rows = HEADS * nb
    step = math.gcd(8, part_px)

    def groups(g, _):
        ids = [g * step + k for k in range(step)]
        ws = [win[pl.ds(p, LANES, stride=wstep), :].astype(BF16) for p in ids]
        ls = [
            jnp.concatenate(
                [uw[pl.ds(i * part_px + p, rows, stride=ustep), :] for i in range(GROUP)]
            ).astype(BF16)
            for p in ids
        ]
        ss = [mm_t(a, w) for a, w in zip(ls, ws)]
        es = []
        for k, p in enumerate(ids):
            for i in range(GROUP):
                q = i * part_px + p
                rki = rstd[pl.ds(q, 1), :]
                s = (ss[k][i * rows : (i + 1) * rows] + ue[pl.ds(q, rows, stride=ustep), :]) * rki
                e = jnp.exp2(s - jnp.max(s, axis=1, keepdims=True))
                e = e * (1.0 / jnp.sum(e, axis=1, keepdims=True)) * rki
                ue[pl.ds(q, rows, stride=ustep), :] = e
                es.append(e)
        for k, p in enumerate(ids):
            z = mm(jnp.concatenate(es[k * GROUP : (k + 1) * GROUP]).astype(BF16), ws[k])
            for i in range(GROUP):
                uw[pl.ds(i * part_px + p, rows, stride=ustep), :] = z[i * rows : (i + 1) * rows]
        return 0

    lax.fori_loop(0, part_px // step, groups, 0)

    half = lax.broadcasted_iota(jnp.int32, (nb * px, LANES), 1) < LANES // 2
    mixes = []
    for h in range(0, HEADS, 2):
        outs = []
        for k in range(2):
            both = []
            for i in range(nb):
                r = ((h + k) * nb + i) * ustep
                z = jnp.where(keep, uw[r : r + px, :], 0.0)
                both.append(jnp.concatenate([ue[r : r + px, :], z], axis=1).astype(BF16))
            weights = av_ref[:, (h + k) * LANES : (h + k + 1) * LANES]
            outs.append(mm(jnp.concatenate(both), weights))
        mixes.append(jnp.where(half, outs[0], outs[1]).astype(BF16))
    mixes = jnp.concatenate(mixes, axis=1)
    chunk = 2 * LANES
    for c in range(0, out_w_ref.shape[1], chunk):
        cols = slice(c, c + chunk)
        update = mm(mixes, out_w_ref[:, cols])
        token = mm(own, stem_ref[:, cols])
        for i in range(nb):
            rows = slice(i * px, (i + 1) * px)
            rounded = (token[rows] + embed_ref[i : i + 1, cols]).astype(BF16)
            out_ref[i, :, cols] = rounded.astype(F32) + update[rows]


def spatial_kernel(
    devices, x_ref, gain_ref, qkv_ref, w_ref, out_ref, normed, proj, mixed, qkv_buf, w_buf, sems
):
    count, pixels, width = x_ref.shape
    pairs = HEADS // 2
    chunk = 3 * width // pairs
    copies = [
        pltpu.make_async_copy(qkv_ref, qkv_buf, sems.at[0]),
        pltpu.make_async_copy(w_ref, w_buf, sems.at[1]),
    ]
    for copy in copies:
        copy.start()

    for b in range(count):
        x = x_ref[b]
        cent = x - jnp.mean(x, axis=1, keepdims=True)
        var = jnp.mean(cent * cent, axis=1, keepdims=True)
        value = cent * lax.rsqrt(var + 1e-5) * gain_ref[...]
        normed[b * pixels : (b + 1) * pixels, :] = value.astype(BF16)

    head = width // HEADS
    low = lax.broadcasted_iota(jnp.int32, (pixels, 2 * head), 1) < head
    copies[0].wait()
    for c in range(0, 3 * width, width):
        proj[:, c : c + width] = mm(normed[...], qkv_buf[:, c : c + width]).astype(BF16)
    for b in range(count):
        rows = slice(b * pixels, (b + 1) * pixels)
        for pair in range(pairs):
            c = pair * chunk
            t0 = proj[rows, c : c + 2 * head]
            t1 = proj[rows, c + 2 * head : c + 4 * head]
            t2 = proj[rows, c + 4 * head : c + 6 * head]
            zero = jnp.zeros_like(t0)
            r0 = jnp.concatenate([t0[:, head:], t0[:, :head]], axis=1)
            r2 = jnp.concatenate([t2[:, head:], t2[:, :head]], axis=1)
            outs = []
            for q, k, v in (
                (jnp.where(low, t0, zero), r0, t1),
                (jnp.where(low, zero, t1), r2, t2),
            ):
                s = mm_t(q, k)
                e = jnp.exp((s - jnp.max(s, axis=1, keepdims=True)) * (head**-0.5))
                total = jnp.sum(e, axis=1, keepdims=True)
                outs.append(mm(e.astype(BF16), v) * (1.0 / total))
            mixed[rows, pair * 2 * head : (pair + 1) * 2 * head] = jnp.where(
                low, outs[0], outs[1]
            ).astype(BF16)

    copies[1].wait()
    chunk = 2 * LANES
    for c in range(0, width, chunk):
        cols = slice(c, c + chunk)
        update = mm(mixed[...], w_buf[:, cols])
        ys = [x_ref[b, :, cols] + update[b * pixels : (b + 1) * pixels] for b in range(count)]
        if devices:
            ys = [y.reshape(devices, pixels // devices, chunk) for y in ys]
            out_ref[:, :, cols] = jnp.concatenate(ys, axis=1).astype(BF16)
        else:
            for b in range(count):
                out_ref[b, :, cols] = ys[b].astype(BF16)


def spatial(x, gain, qkv, w, first, count, devices):
    nb, pixels, width = x.shape
    if direct(pixels, devices, count):
        shape = (devices, count * pixels // devices, width)
    else:
        devices, shape = 0, (count, pixels, width)
    return pl.pallas_call(
        functools.partial(spatial_kernel, devices),
        grid=(1,),
        out_shape=jax.ShapeDtypeStruct(shape, BF16),
        in_specs=[
            pl.BlockSpec((count, pixels, width), lambda i: (first // count, 0, 0)),
            whole_spec((1, width)),
            pl.BlockSpec(memory_space=pl.ANY),
            pl.BlockSpec(memory_space=pl.ANY),
        ],
        out_specs=whole_spec(shape),
        scratch_shapes=[
            pltpu.VMEM((count * pixels, width), BF16),
            pltpu.VMEM((count * pixels, 3 * width), BF16),
            pltpu.VMEM((count * pixels, width), BF16),
            pltpu.VMEM(qkv.shape, BF16),
            pltpu.VMEM((width, width), BF16),
            pltpu.SemaphoreType.DMA((2,)),
        ],
        compiler_params=pltpu.CompilerParams(vmem_limit_bytes=VMEM_LIMIT),
        cost_estimate=takes(15),
        name="spatial",
    )(x, gain[None], qkv, w)


def direct(pixels, devices, count):
    each = pixels // devices
    return each % 8 == 0 and (each * count) % 16 == 0


def gelu(v):
    half = 0.5 * v
    inner = v * ((2 / math.pi) ** 0.5 + (2 / math.pi) ** 0.5 * 0.044715 * (v * v))
    return half + half * jnp.tanh(inner)


def mlp_kernel(run, earlier, contents, place_ref, x_ref, gain_ref, bias_ref, *refs):
    n_weights = 4 + len(contents)
    weight_refs, refs = refs[:n_weights], refs[n_weights:]
    earlier_refs, refs = refs[:earlier], refs[earlier:]
    out_ref, normed, acc, buf, sems, *rest = refs
    band, depth = place_ref[1], place_ref[2]
    rows, width = normed.shape
    zsize, groups = bias_ref.shape[1], bias_ref.shape[2]
    half = bias_ref.shape[4]
    size = groups * half

    blocks = []
    for c in range(2):
        up, down = weight_refs[2 * c], weight_refs[2 * c + 1]
        bias = [bias_ref[c, 0, i] for i in range(groups)]
        blocks.append(([(up, 0, size, 0), (down, 0, size, size)], bias, False))
    pieces = []
    for ref, (c, sources) in zip(weight_refs[4:], contents):
        for i, (k, m, h) in enumerate(sources):
            pieces.append((ref, i, bias_ref[c, depth ^ lax.rem(depth - k + zsize, zsize), (band ^ m) * 2 + h]))
    for i in range(0, len(pieces), groups):
        some = pieces[i : i + groups]
        runs = []
        for j, (ref, at, _) in enumerate(some):
            if runs and runs[-1][0] is ref and runs[-1][1] + runs[-1][2] == at * 2 * half:
                runs[-1][2] += 2 * half
            else:
                runs.append([ref, at * 2 * half, 2 * half, j * 2 * half])
        blocks.append((runs, [p[2] for p in some], True))

    def copies(n):
        slot = n % buf.shape[0]
        return [
            pltpu.make_async_copy(
                ref.at[pl.ds(first, count), :],
                buf.at[slot, pl.ds(to, count), :],
                sems.at[slot, i],
            )
            for i, (ref, first, count, to) in enumerate(blocks[n][0])
        ]

    ahead = buf.shape[0] - 1
    for n in range(ahead):
        for copy in copies(n):
            copy.start()

    x = x_ref[:rows, :].astype(F32)
    cent = x - jnp.mean(x, axis=1, keepdims=True)
    var = jnp.mean(cent * cent, axis=1, keepdims=True)
    normed[...] = (cent * lax.rsqrt(var + 1e-5) * gain_ref[...]).astype(BF16)
    acc[...] = x

    for n, (_, bias, mixed) in enumerate(blocks):
        for copy in copies(n):
            copy.wait()
        if n + ahead < len(blocks):
            for copy in copies(n + ahead):
                copy.start()
        slot = n % buf.shape[0]
        total = None
        hidden = []
        for part in range(2):
            ids = range(part * groups // 2, (part + 1) * groups // 2)
            if not mixed:
                up = buf[slot, ids[0] * half : ids[0] * half + size // 2, :]
            else:
                up = jnp.concatenate([buf[slot, 2 * g * half : (2 * g + 1) * half, :] for g in ids])
            v = mm_t(normed[...], up) + jnp.concatenate([bias[g] for g in ids], axis=1)
            hidden.append(gelu(v).astype(BF16))
        for part in range(2):
            ids = range(part * groups // 2, (part + 1) * groups // 2)
            if not mixed:
                down = buf[slot, size + ids[0] * half : size + ids[0] * half + size // 2, :]
            else:
                down = jnp.concatenate(
                    [buf[slot, (2 * g + 1) * half : (2 * g + 2) * half, :] for g in ids]
                )
            piece = mm(hidden[part], down)
            total = piece if total is None else total + piece
        acc[...] += total

    if len(out_ref.shape) == 2:
        out_ref[...] = acc[...].astype(BF16)
        return
    lay = rest[0]
    each, bands, _ = out_ref.shape
    whole = bands * each
    parts = earlier + 1
    for p in range(parts):
        part = earlier_refs[p] if p < earlier else acc
        for c in range(width // LANES):
            cols = slice(c * LANES, (c + 1) * LANES)
            if parts == 1:
                lay[c * whole : (c + 1) * whole, :] = part[:, cols]
                continue
            for i in range(rows // run):
                to = c * whole + (i * parts + p) * run
                lay[to : to + run, :] = part[i * run : (i + 1) * run, cols].astype(F32)
    for c in range(width // LANES):
        for px in range(each):
            out_ref[px, :, c * LANES : (c + 1) * LANES] = lay[
                pl.ds(c * whole + px, bands, stride=each), :
            ].astype(BF16)


def mlp(place, x, rows, gain, bias, own, gathered, contents, earlier, run, result):
    width = x.shape[1]
    size = own[0].shape[0]
    scratch = [
        pltpu.VMEM((rows, width), BF16),
        pltpu.VMEM((rows, width), F32),
        pltpu.VMEM((3, 2 * size, width), BF16),
        pltpu.SemaphoreType.DMA((3, 2 * bias.shape[2])),
    ]
    if result is None:
        shape = (rows, width)
    else:
        shape = result
        scratch.append(pltpu.VMEM((math.prod(result) // LANES, LANES), F32))
    vmem = pl.BlockSpec(memory_space=pltpu.VMEM)
    return pl.pallas_call(
        functools.partial(mlp_kernel, run, len(earlier), contents),
        grid=(1,),
        out_shape=jax.ShapeDtypeStruct(shape, BF16),
        in_specs=[pl.BlockSpec(memory_space=pltpu.SMEM), vmem, vmem, vmem]
        + [pl.BlockSpec(memory_space=pl.ANY)] * (4 + len(gathered))
        + [vmem] * len(earlier),
        out_specs=whole_spec(shape),
        scratch_shapes=scratch,
        compiler_params=pltpu.CompilerParams(vmem_limit_bytes=VMEM_LIMIT),
        cost_estimate=takes(0),
        name="mlp",
    )(place, x, gain[None], bias, *own, *gathered, *earlier)


def swap(x, axis, mask):
    count = lax.axis_size(axis)
    return lax.ppermute(x, axis, [(i, i ^ mask) for i in range(count)])


def selectors():
    row = np.arange(GROUP * 2 * LANES)[:, None]
    col = np.arange(SPAN * LANES)[None]
    within = row % (2 * LANES)
    sel = (within == (col // LANES) * CH_TOK + col % WIN) & (
        row // (2 * LANES) == col % LANES // WIN
    )
    row = np.arange(2 * LANES)[:, None]
    col = np.arange(SPAN * WIN)[None]
    sel1 = row == (col // WIN) * CH_TOK + col % WIN
    group = row // WIN == np.arange(LANES)[None] % SPAN
    return sel.astype(BF16), sel1.astype(BF16), group.astype(BF16)


def whole_spec(shape):
    return pl.BlockSpec(shape, lambda *_: (0,) * len(shape))


def spectral(place, near, far, tables, own, spec_out, nb, bands):
    bsize, zsize, some, _ = near.shape
    pixels = 2 * zsize * some
    width = spec_out.shape[0]
    lanes = (bands // SPAN + 1) * LANES
    args = [near, far, *selectors(), *tables, own, spec_out]
    part_px = pixels // GROUP
    return pl.pallas_call(
        functools.partial(spectral_kernel, nb, bands),
        out_shape=jax.ShapeDtypeStruct((nb, pixels, width), F32),
        in_specs=[pl.BlockSpec(memory_space=pltpu.SMEM)]
        + [pl.BlockSpec(memory_space=pltpu.VMEM)] * len(args),
        out_specs=pl.BlockSpec(memory_space=pltpu.VMEM),
        scratch_shapes=[
            pltpu.VMEM((pixels, lanes), BF16),
            pltpu.VMEM((LANES * (part_px + GAP), LANES), F32),
            pltpu.VMEM((HEADS * nb * (pixels + GAP), LANES), F32),
            pltpu.VMEM((HEADS * nb * (pixels + GAP), LANES), F32),
            pltpu.VMEM((pixels, LANES), F32),
        ],
        compiler_params=pltpu.CompilerParams(vmem_limit_bytes=VMEM_LIMIT),
        cost_estimate=takes(26),
        name="spectral",
    )(place, *args)


def local(
    radiance,
    stem_weight,
    band_embed,
    norm_spectral,
    spec_qkv,
    spec_out,
    norm_spatial,
    spat_qkv,
    spat_out,
    norm_mlp,
    up_weight,
    up_bias,
    down_weight,
):
    bands, width = band_embed.shape
    bsize, psize = lax.axis_size("band"), lax.axis_size("pix")
    devices = bsize * psize
    nb = -(-bands // devices)
    band, pix = lax.axis_index("band"), lax.axis_index("pix")
    base = jnp.minimum((pix * bsize + band) * nb, bands - nb).astype(jnp.int32)

    rows, channels = radiance.shape
    message = jnp.concatenate([radiance.astype(BF16), up_bias.reshape(rows, -1)], axis=1)
    own = lax.dynamic_slice_in_dim(band_embed, base, nb, 0)
    features = make_features(stem_weight, band_embed, own, norm_spectral)

    half = up_weight.shape[0] // bsize // 2
    share = []
    for h in range(2):
        at = (band * 2 + h) * half
        share.append(
            jnp.concatenate(
                [lax.dynamic_slice_in_dim(w, at, half, 0) for w in (up_weight, down_weight)]
            )
        )
    share = jnp.concatenate(share)

    def ring(x, step):
        return lax.ppermute(x, "pix", [(i, (i + 2 * step) % psize) for i in range(psize)])


    relayed = bsize == 4
    straight = (1, 2) if relayed else tuple(range(1, bsize))

    def relay(got, count):
        out = []
        for h, m in enumerate((2, 1)):
            part = [x.reshape(-1, 2, 2 * half, width)[:, h] for x in got[m]]
            part = jnp.concatenate(part).reshape(count * 2 * half, width)
            out.append(swap(part, "band", 3 - m))
        return out

    zs = jnp.stack([message] + [swap(message, "pix", 2 * k) for k in range(1, psize // 2)])
    share, features = lax.optimization_barrier((share, features))
    shares = [ring(share, 1)]
    place = jnp.stack([base, band, pix // 2, pix % 2]).astype(jnp.int32)
    zs, features, place = lax.optimization_barrier((zs, features, place))
    near = jnp.stack([zs] + [swap(zs, "band", k) for k in range(1, bsize)])
    tables = make_tables(bands, features[0], spec_qkv) + features[1:]
    near, tables, shares, share, up_weight, down_weight = lax.optimization_barrier(
        (near, tables, shares, share, up_weight, down_weight)
    )
    far = swap(near, "pix", 1)
    first = {m: swap(shares[0], "band", m) for m in straight}
    while len(shares) < psize // 2 - 2:
        shares.append(ring(shares[-1], 1))
    shares.append(ring(share, -1))
    after_spectral = spectral(place, near, far, tables, own, spec_out, nb, bands)
    after_spectral, shares, first, up_weight, down_weight = lax.optimization_barrier(
        (after_spectral, shares, first, up_weight, down_weight)
    )
    own_weights = [up_weight, down_weight, swap(up_weight, "pix", 1), swap(down_weight, "pix", 1)]
    later = jnp.concatenate(shares[1:])
    rest = {m: swap(later, "band", m) for m in straight}
    bias = jnp.stack([near[0, :, :, channels:], far[0, :, :, channels:]])
    bias = bias.reshape(2, psize // 2, 2 * bsize, 1, half).astype(F32)
    pixels = after_spectral.shape[1]
    each = pixels // devices
    count = nb // 2 if nb % 2 == 0 and direct(pixels, devices, nb // 2) else nb
    arrived, results = [], []
    for start in range(0, nb, count):
        part = spatial(after_spectral, norm_spatial, spat_qkv, spat_out, start, count, devices)
        if start == 0:
            part, after_spectral, own_weights = lax.optimization_barrier(
                (part, after_spectral, own_weights)
            )
            held = [shares[0], later] + [x[m] for m in straight for x in (first, rest)]
            last_hop = []
            first, rest = lax.optimization_barrier((first, rest))
            if relayed:
                last_hop = relay({m: (first[m], rest[m]) for m in straight}, psize // 2 - 1)
            held_far = [swap(x, "pix", 1) for x in held]
        else:
            part, arrived, held_far, last_hop = lax.optimization_barrier(
                (part, arrived, held_far, last_hop)
            )
        if direct(pixels, devices, count):
            moved = lax.all_to_all(part, ("pix", "band"), split_axis=0, concat_axis=0, tiled=True)
        else:
            moved = lax.all_to_all(part, ("pix", "band"), split_axis=1, concat_axis=0, tiled=True)
        arrived.append(moved.reshape(-1, width))
    last_hop, _ = lax.optimization_barrier((last_hop, part))
    gathered = [*held, *held_far, *last_hop, *[swap(x, "pix", 1) for x in last_hop]]
    one, more = ((1,), tuple(range(2, psize // 2)))
    ids = [
        tuple((k, m, h) for k in some for h in range(2)) for m in (0, *straight) for some in (one, more)
    ]
    hop_ids = [tuple((k, 3, h) for k in one + more) for h in range(len(last_hop))]
    contents = tuple((c, x) for part in (ids, hop_ids) for c in range(2) for x in part)
    run = count * each
    for i, moved in enumerate(arrived):
        last = i == len(arrived) - 1
        results.append(
            mlp(
                place,
                moved,
                bands // nb * run,
                norm_mlp,
                bias,
                own_weights,
                gathered,
                contents,
                results if last else [],
                run,
                (each, bands, width) if last else None,
            )
        )
    return results[-1]


def solution(mesh):
    placed = (
        P("pix", "band"),
        P(),
        P(),
        P(),
        P(),
        P(),
        P(),
        P(),
        P(),
        P(),
        P("pix", None),
        P("pix"),
        P("pix", None),
    )
    return jax.shard_map(
        local, mesh=mesh, in_specs=placed, out_specs=P(("pix", "band"), None, None), check_vma=False
    )
```

```python
import functools
import math

import jax
import jax.numpy as jnp
import numpy as np
from jax import lax
from jax.experimental import pallas as pl
from jax.experimental.pallas import tpu as pltpu
from jax.sharding import PartitionSpec as P

HEADS = 16
CH_TOK = 16
WIN = 2 * CH_TOK
LANES = 128
GROUP = LANES // WIN
SPAN = LANES // CH_TOK
GAP = 8
F32 = jnp.float32
BF16 = jnp.bfloat16
HIGH = lax.Precision.HIGHEST
LOG2_E = math.log2(math.e)
VMEM_LIMIT = 60 * 2**20


def takes(us):
    return pl.CostEstimate(flops=us * 10**9, bytes_accessed=2**20, transcendentals=0)


def mm(a, b):
    return jnp.dot(a, b, preferred_element_type=F32)


def mm_t(a, b):
    return lax.dot_general(a, b, (((1,), (1,)), ((), ())), preferred_element_type=F32)


def split2(x):
    hi = x.astype(BF16)
    return hi, (x - hi.astype(F32)).astype(BF16)


def mm_exact(a, b):
    return lax.dot_general(
        a, b, (((1,), (1,)), ((), ())), precision=HIGH, preferred_element_type=F32
    )


def feature_kernel(
    stem_ref, embed_ref, own_ref, gain_ref, feats_ref, gram_ref, cross_ref, const_ref, pieces_ref
):
    def centred(x):
        return x - jnp.mean(x, axis=1, keepdims=True)

    gain = gain_ref[...]
    stem = centred(stem_ref[...])
    bands, width = embed_ref.shape
    blank = jnp.zeros((LANES - bands, width), F32)
    embed = jnp.concatenate([centred(embed_ref[...]), blank])
    stem_g = stem * gain
    tail = jnp.zeros((8, width), F32)
    feats_ref[...] = jnp.concatenate(
        [embed * gain] + [stem_g] * GROUP + [centred(own_ref[...]) * gain, tail]
    ).astype(BF16)

    wide = SPAN * WIN
    forms = mm_exact(jnp.concatenate([embed, stem]), stem) * (1.0 / width)
    forms = jnp.concatenate([forms] * SPAN, axis=1)
    gram = jnp.concatenate([forms[LANES:]] * SPAN)
    same = (
        lax.broadcasted_iota(jnp.int32, (wide, wide), 0) // WIN
        == lax.broadcasted_iota(jnp.int32, (wide, wide), 1) // WIN
    )
    gram_ref[0], gram_ref[1] = split2(jnp.where(same, gram, 0.0))
    same = (
        lax.broadcasted_iota(jnp.int32, (LANES, wide), 0) % SPAN
        == lax.broadcasted_iota(jnp.int32, (LANES, wide), 1) // WIN
    )
    cross = jnp.where(same, 2.0 * forms[:LANES], 0.0)
    cross_ref[...] = jnp.sum(cross.reshape(LANES // SPAN, SPAN, wide), axis=1)
    const_ref[...] = mm_exact(jnp.ones((8, width), F32), embed * embed) * (1.0 / width)

    rest = stem_ref[...]
    pieces = []
    for _ in range(3):
        hi = rest.astype(BF16).astype(F32)
        pieces.append(hi)
        rest = rest - hi
    pieces_ref[...] = jnp.concatenate(pieces + [jnp.zeros_like(rest)]).astype(BF16)


def make_features(stem_weight, band_embed, own, gain):
    width = band_embed.shape[1]
    own8 = jnp.pad(own, ((0, 8 - own.shape[0]), (0, 0)))
    wide = SPAN * WIN
    vmem = pl.BlockSpec(memory_space=pltpu.VMEM)
    return pl.pallas_call(
        feature_kernel,
        out_shape=[
            jax.ShapeDtypeStruct((2 * LANES + 16, width), BF16),
            jax.ShapeDtypeStruct((2, wide, wide), BF16),
            jax.ShapeDtypeStruct((LANES // SPAN, wide), F32),
            jax.ShapeDtypeStruct((8, LANES), F32),
            jax.ShapeDtypeStruct((LANES, width), BF16),
        ],
        in_specs=[vmem] * 4,
        out_specs=[vmem] * 5,
        compiler_params=pltpu.CompilerParams(vmem_limit_bytes=VMEM_LIMIT),
        cost_estimate=takes(4),
        name="features",
    )(stem_weight, band_embed, own8, gain[None])


def tables_kernel(bands, feats_ref, qkv_ref, mse_ref, mee_ref, av_ref):
    a = mm(feats_ref[...], qkv_ref[...]).astype(BF16)
    heads = mse_ref.shape[1] // (2 * LANES)
    head = a.shape[1] // (3 * heads)
    keys = 2 * LANES
    scale = head**-0.5 * LOG2_E
    beyond = lax.broadcasted_iota(jnp.int32, (8, keys), 1)
    beyond = (beyond >= bands) & (beyond < LANES)
    for i in range(heads):
        c = 3 * i * head
        q = a[:, c : c + head]
        k = a[:keys, c + head : c + 2 * head]
        m = mm_t(q[LANES : LANES + WIN], k) * scale
        hi, lo = split2(m)
        mse_ref[:WIN, i * keys : (i + 1) * keys] = hi
        mse_ref[WIN:, i * keys : (i + 1) * keys] = lo
        m = mm_t(q[keys : keys + 16], k)[:8] * scale
        mee_ref[:, i * keys : (i + 1) * keys] = jnp.where(beyond, -1e30, m)
        if i % 2 == 0:
            av_ref[:, 2 * i * head : 2 * (i + 2) * head] = a[:keys, c + 2 * head : c + 6 * head]


def make_tables(bands, feats, qkv):
    steps = HEADS // 4
    width = qkv.shape[0]
    cols = qkv.shape[1] // steps
    return pl.pallas_call(
        functools.partial(tables_kernel, bands),
        grid=(steps,),
        out_shape=[
            jax.ShapeDtypeStruct((2 * WIN, HEADS * 2 * LANES), BF16),
            jax.ShapeDtypeStruct((8, HEADS * 2 * LANES), F32),
            jax.ShapeDtypeStruct((2 * LANES, HEADS * LANES), BF16),
        ],
        in_specs=[whole_spec(feats.shape), pl.BlockSpec((width, cols), lambda i: (0, i))],
        out_specs=[
            pl.BlockSpec((2 * WIN, 8 * LANES), lambda i: (0, i)),
            pl.BlockSpec((8, 8 * LANES), lambda i: (0, i)),
            pl.BlockSpec((2 * LANES, HEADS * LANES // steps), lambda i: (0, i)),
        ],
        compiler_params=pltpu.CompilerParams(vmem_limit_bytes=VMEM_LIMIT),
        cost_estimate=takes(8),
        name="tables",
    )(feats, qkv)


def spectral_kernel(
    nb,
    bands,
    place_ref,
    near_ref,
    far_ref,
    sel_ref,
    sel1_ref,
    group_ref,
    mse_ref,
    mee_ref,
    av_ref,
    gram_ref,
    cross_ref,
    const_ref,
    stem_ref,
    embed_ref,
    out_w_hbm,
    out_ref,
    rad_ref,
    win,
    ue,
    uw,
    rstd,
    out_w_ref,
    out_w_sem,
):
    base, band, depth, core = (place_ref[k] for k in range(4))
    fetch = pltpu.make_async_copy(out_w_hbm, out_w_ref, out_w_sem)
    fetch.start()
    bsize, zsize, some, _ = near_ref.shape
    px, lanes = rad_ref.shape
    channels = bands * CH_TOK // bsize
    edge = CH_TOK // 2
    for k, ref in enumerate((near_ref, far_ref)):
        for kz in range(zsize):
            at = ((depth ^ kz) * 2 + (core ^ k)) * some
            pieces = [ref[b ^ band, kz, :, :channels].astype(F32) for b in range(bsize)]
            pieces = [jnp.zeros((some, edge), F32)] + pieces
            pieces.append(jnp.zeros((some, lanes - bands * CH_TOK - edge), F32))
            rad_ref[pl.ds(pl.multiple_of(at, some), some), :] = jnp.concatenate(
                pieces, axis=1
            ).astype(BF16)

    part_px = px // GROUP
    tiles = bands // SPAN
    wstep, ustep = part_px + GAP, px + GAP
    lane = lax.broadcasted_iota(jnp.int32, (px, LANES), 1)
    row = lax.broadcasted_iota(jnp.int32, (px, LANES), 0)
    blocks = [rad_ref[:, j * LANES : (j + 2) * LANES] for j in range(tiles)]

    packed = jnp.concatenate(
        [
            jnp.concatenate([b[i * part_px : (i + 1) * part_px] for i in range(GROUP)], axis=1)
            for b in blocks
        ]
    )
    for i in range(0, SPAN, 2):
        wide = mm(packed, sel_ref[:, i * LANES : (i + 2) * LANES])
        for j in range(tiles):
            for k in range(2):
                t = j * SPAN + i + k
                win[t * wstep : t * wstep + part_px, :] = wide[
                    j * part_px : (j + 1) * part_px, k * LANES : (k + 1) * LANES
                ]
    for t in range(bands, LANES):
        win[t * wstep : t * wstep + part_px, :] = jnp.zeros((part_px, LANES), F32)

    acc = jnp.zeros((px, LANES), F32)
    thin = mm(jnp.concatenate(blocks), sel1_ref[...])
    thin_b = thin.astype(BF16)
    form = mm(thin_b, gram_ref[0]) + mm(thin_b, gram_ref[1])
    for j in range(tiles):
        rows = slice(j * px, (j + 1) * px)
        hi, lo = split2(thin[rows] * (form[rows] + cross_ref[j : j + 1, :]))
        summed = mm(hi, group_ref[...]) + mm(lo, group_ref[...])
        acc = jnp.where(lane // SPAN == j, summed, acc)
    scale = lax.rsqrt(acc + const_ref[:1, :] + 1e-5)
    rstd[...] = scale

    own, rq = [], []
    at = lax.broadcasted_iota(jnp.int32, (2 * LANES, LANES), 0)
    to = lax.broadcasted_iota(jnp.int32, (2 * LANES, LANES), 1)
    for i in range(nb):
        t = base + i
        cols = pl.ds(pl.multiple_of(t // SPAN * LANES, LANES), 2 * LANES)
        pick = (at == t % SPAN * CH_TOK + to % WIN).astype(F32).astype(BF16)
        own.append(mm(rad_ref[:, cols], pick).astype(BF16))
        rq.append(jnp.sum(jnp.where(lane == t, scale, 0.0), axis=1, keepdims=True))
    own = jnp.concatenate(own)
    keep = lane // WIN == row // part_px
    for h in range(0, HEADS, 2):
        both = slice(2 * h * LANES, 2 * (h + 2) * LANES)
        parts = mm(own[:, : 2 * WIN], mse_ref[:, both])
        for i in range(nb):
            part = (parts[i * px : (i + 1) * px] + mee_ref[i : i + 1, both]) * rq[i]
            for k in range(2):
                r = ((h + k) * nb + i) * ustep
                ue[r : r + px, :] = part[:, 2 * k * LANES : (2 * k + 1) * LANES]
                uw[r : r + px, :] = jnp.where(
                    keep, part[:, (2 * k + 1) * LANES : (2 * k + 2) * LANES], 0.0
                )

    rows = HEADS * nb
    step = math.gcd(8, part_px)

    def groups(g, _):
        ids = [g * step + k for k in range(step)]
        ws = [win[pl.ds(p, LANES, stride=wstep), :].astype(BF16) for p in ids]
        ls = [
            jnp.concatenate(
                [uw[pl.ds(i * part_px + p, rows, stride=ustep), :] for i in range(GROUP)]
            ).astype(BF16)
            for p in ids
        ]
        ss = [mm_t(a, w) for a, w in zip(ls, ws)]
        es = []
        for k, p in enumerate(ids):
            for i in range(GROUP):
                q = i * part_px + p
                rki = rstd[pl.ds(q, 1), :]
                s = (ss[k][i * rows : (i + 1) * rows] + ue[pl.ds(q, rows, stride=ustep), :]) * rki
                e = jnp.exp2(s - jnp.max(s, axis=1, keepdims=True))
                e = e * (1.0 / jnp.sum(e, axis=1, keepdims=True)) * rki
                ue[pl.ds(q, rows, stride=ustep), :] = e
                es.append(e)
        for k, p in enumerate(ids):
            z = mm(jnp.concatenate(es[k * GROUP : (k + 1) * GROUP]).astype(BF16), ws[k])
            for i in range(GROUP):
                uw[pl.ds(i * part_px + p, rows, stride=ustep), :] = z[i * rows : (i + 1) * rows]
        return 0

    lax.fori_loop(0, part_px // step, groups, 0)

    half = lax.broadcasted_iota(jnp.int32, (nb * px, LANES), 1) < LANES // 2
    mixes = []
    for h in range(0, HEADS, 2):
        outs = []
        for k in range(2):
            both = []
            for i in range(nb):
                r = ((h + k) * nb + i) * ustep
                z = jnp.where(keep, uw[r : r + px, :], 0.0)
                both.append(jnp.concatenate([ue[r : r + px, :], z], axis=1).astype(BF16))
            weights = av_ref[:, (h + k) * LANES : (h + k + 1) * LANES]
            outs.append(mm(jnp.concatenate(both), weights))
        mixes.append(jnp.where(half, outs[0], outs[1]).astype(BF16))
    mixes = jnp.concatenate(mixes, axis=1)
    fetch.wait()
    chunk = 2 * LANES
    for c in range(0, out_w_ref.shape[1], chunk):
        cols = slice(c, c + chunk)
        update = mm(mixes, out_w_ref[:, cols])
        token = mm(own, stem_ref[:, cols])
        for i in range(nb):
            rows = slice(i * px, (i + 1) * px)
            rounded = (token[rows] + embed_ref[i : i + 1, cols]).astype(BF16)
            out_ref[i, :, cols] = rounded.astype(F32) + update[rows]


def spatial_kernel(
    devices, x_ref, gain_ref, qkv_ref, w_ref, out_ref, normed, proj, mixed, qkv_buf, w_buf, sems
):
    count, pixels, width = x_ref.shape
    pairs = HEADS // 2
    chunk = 3 * width // pairs
    copies = [
        pltpu.make_async_copy(qkv_ref, qkv_buf, sems.at[0]),
        pltpu.make_async_copy(w_ref, w_buf, sems.at[1]),
    ]
    for copy in copies:
        copy.start()

    for b in range(count):
        x = x_ref[b]
        cent = x - jnp.mean(x, axis=1, keepdims=True)
        var = jnp.mean(cent * cent, axis=1, keepdims=True)
        value = cent * lax.rsqrt(var + 1e-5) * gain_ref[...]
        normed[b * pixels : (b + 1) * pixels, :] = value.astype(BF16)

    head = width // HEADS
    low = lax.broadcasted_iota(jnp.int32, (pixels, 2 * head), 1) < head
    copies[0].wait()
    for c in range(0, 3 * width, width):
        proj[:, c : c + width] = mm(normed[...], qkv_buf[:, c : c + width]).astype(BF16)
    for b in range(count):
        rows = slice(b * pixels, (b + 1) * pixels)
        for pair in range(pairs):
            c = pair * chunk
            t0 = proj[rows, c : c + 2 * head]
            t1 = proj[rows, c + 2 * head : c + 4 * head]
            t2 = proj[rows, c + 4 * head : c + 6 * head]
            zero = jnp.zeros_like(t0)
            r0 = jnp.concatenate([t0[:, head:], t0[:, :head]], axis=1)
            r2 = jnp.concatenate([t2[:, head:], t2[:, :head]], axis=1)
            outs = []
            for q, k, v in (
                (jnp.where(low, t0, zero), r0, t1),
                (jnp.where(low, zero, t1), r2, t2),
            ):
                s = mm_t(q, k)
                e = jnp.exp2((s - jnp.max(s, axis=1, keepdims=True)) * (head**-0.5 * LOG2_E))
                total = jnp.sum(e, axis=1, keepdims=True)
                outs.append(mm(e.astype(BF16), v) * (1.0 / total))
            mixed[rows, pair * 2 * head : (pair + 1) * 2 * head] = jnp.where(
                low, outs[0], outs[1]
            ).astype(BF16)

    copies[1].wait()
    chunk = 2 * LANES
    for c in range(0, width, chunk):
        cols = slice(c, c + chunk)
        update = mm(mixed[...], w_buf[:, cols])
        ys = [x_ref[b, :, cols] + update[b * pixels : (b + 1) * pixels] for b in range(count)]
        if devices:
            ys = [y.reshape(devices, pixels // devices, chunk) for y in ys]
            out_ref[:, :, cols] = jnp.concatenate(ys, axis=1).astype(BF16)
        else:
            for b in range(count):
                out_ref[b, :, cols] = ys[b].astype(BF16)


def spatial(x, gain, qkv, w, first, count, devices):
    nb, pixels, width = x.shape
    if direct(pixels, devices, count):
        shape = (devices, count * pixels // devices, width)
    else:
        devices, shape = 0, (count, pixels, width)
    return pl.pallas_call(
        functools.partial(spatial_kernel, devices),
        grid=(1,),
        out_shape=jax.ShapeDtypeStruct(shape, BF16),
        in_specs=[
            pl.BlockSpec((count, pixels, width), lambda i: (first // count, 0, 0)),
            whole_spec((1, width)),
            pl.BlockSpec(memory_space=pl.ANY),
            pl.BlockSpec(memory_space=pl.ANY),
        ],
        out_specs=whole_spec(shape),
        scratch_shapes=[
            pltpu.VMEM((count * pixels, width), BF16),
            pltpu.VMEM((count * pixels, 3 * width), BF16),
            pltpu.VMEM((count * pixels, width), BF16),
            pltpu.VMEM(qkv.shape, BF16),
            pltpu.VMEM((width, width), BF16),
            pltpu.SemaphoreType.DMA((2,)),
        ],
        compiler_params=pltpu.CompilerParams(vmem_limit_bytes=VMEM_LIMIT),
        cost_estimate=takes(15),
        name="spatial",
    )(x, gain[None], qkv, w)


def direct(pixels, devices, count):
    each = pixels // devices
    return each % 8 == 0 and (each * count) % 16 == 0


def gelu(v):
    half = 0.5 * v
    inner = v * ((2 / math.pi) ** 0.5 + (2 / math.pi) ** 0.5 * 0.044715 * (v * v))
    return half + half * jnp.tanh(inner)


def mlp_kernel(run, earlier, contents, place_ref, x_ref, gain_ref, bias_ref, *refs):
    n_weights = 4 + len(contents)
    weight_refs, refs = refs[:n_weights], refs[n_weights:]
    earlier_refs, refs = refs[:earlier], refs[earlier:]
    out_ref, normed, acc, buf, sems, *rest = refs
    band, depth = place_ref[1], place_ref[2]
    rows, width = normed.shape
    zsize, groups = bias_ref.shape[1], bias_ref.shape[2]
    half = bias_ref.shape[4]
    size = groups * half

    blocks = []
    for c in range(2):
        up, down = weight_refs[2 * c], weight_refs[2 * c + 1]
        bias = [bias_ref[c, 0, i] for i in range(groups)]
        blocks.append(([(up, 0, size, 0), (down, 0, size, size)], bias, False))
    pieces = []
    for ref, (c, sources) in zip(weight_refs[4:], contents):
        for i, (k, m, h) in enumerate(sources):
            pieces.append((ref, i, bias_ref[c, depth ^ lax.rem(depth - k + zsize, zsize), (band ^ m) * 2 + h]))
    for i in range(0, len(pieces), groups):
        some = pieces[i : i + groups]
        runs = []
        for j, (ref, at, _) in enumerate(some):
            if runs and runs[-1][0] is ref and runs[-1][1] + runs[-1][2] == at * 2 * half:
                runs[-1][2] += 2 * half
            else:
                runs.append([ref, at * 2 * half, 2 * half, j * 2 * half])
        blocks.append((runs, [p[2] for p in some], True))

    def copies(n):
        slot = n % buf.shape[0]
        return [
            pltpu.make_async_copy(
                ref.at[pl.ds(first, count), :],
                buf.at[slot, pl.ds(to, count), :],
                sems.at[slot, i],
            )
            for i, (ref, first, count, to) in enumerate(blocks[n][0])
        ]

    ahead = buf.shape[0] - 1
    for n in range(ahead):
        for copy in copies(n):
            copy.start()

    x = x_ref[:rows, :].astype(F32)
    cent = x - jnp.mean(x, axis=1, keepdims=True)
    var = jnp.mean(cent * cent, axis=1, keepdims=True)
    normed[...] = (cent * lax.rsqrt(var + 1e-5) * gain_ref[...]).astype(BF16)
    acc[...] = x

    for n, (_, bias, mixed) in enumerate(blocks):
        for copy in copies(n):
            copy.wait()
        if n + ahead < len(blocks):
            for copy in copies(n + ahead):
                copy.start()
        slot = n % buf.shape[0]
        total = None
        hidden = []
        for part in range(2):
            ids = range(part * groups // 2, (part + 1) * groups // 2)
            if not mixed:
                up = buf[slot, ids[0] * half : ids[0] * half + size // 2, :]
            else:
                up = jnp.concatenate([buf[slot, 2 * g * half : (2 * g + 1) * half, :] for g in ids])
            v = mm_t(normed[...], up) + jnp.concatenate([bias[g] for g in ids], axis=1)
            hidden.append(gelu(v).astype(BF16))
        for part in range(2):
            ids = range(part * groups // 2, (part + 1) * groups // 2)
            if not mixed:
                down = buf[slot, size + ids[0] * half : size + ids[0] * half + size // 2, :]
            else:
                down = jnp.concatenate(
                    [buf[slot, (2 * g + 1) * half : (2 * g + 2) * half, :] for g in ids]
                )
            piece = mm(hidden[part], down)
            total = piece if total is None else total + piece
        acc[...] += total

    if len(out_ref.shape) == 2:
        out_ref[...] = acc[...].astype(BF16)
        return
    lay = rest[0]
    each, bands, _ = out_ref.shape
    whole = bands * each
    parts = earlier + 1
    for p in range(parts):
        part = earlier_refs[p] if p < earlier else acc
        for c in range(width // LANES):
            cols = slice(c * LANES, (c + 1) * LANES)
            if parts == 1:
                lay[c * whole : (c + 1) * whole, :] = part[:, cols]
                continue
            for i in range(rows // run):
                to = c * whole + (i * parts + p) * run
                lay[to : to + run, :] = part[i * run : (i + 1) * run, cols].astype(F32)
    for c in range(width // LANES):
        for px in range(each):
            out_ref[px, :, c * LANES : (c + 1) * LANES] = lay[
                pl.ds(c * whole + px, bands, stride=each), :
            ].astype(BF16)


def mlp(place, x, rows, gain, bias, own, gathered, contents, earlier, run, result):
    width = x.shape[1]
    size = own[0].shape[0]
    scratch = [
        pltpu.VMEM((rows, width), BF16),
        pltpu.VMEM((rows, width), F32),
        pltpu.VMEM((3, 2 * size, width), BF16),
        pltpu.SemaphoreType.DMA((3, 2 * bias.shape[2])),
    ]
    if result is None:
        shape = (rows, width)
    else:
        shape = result
        scratch.append(pltpu.VMEM((math.prod(result) // LANES, LANES), F32))
    vmem = pl.BlockSpec(memory_space=pltpu.VMEM)
    return pl.pallas_call(
        functools.partial(mlp_kernel, run, len(earlier), contents),
        grid=(1,),
        out_shape=jax.ShapeDtypeStruct(shape, BF16),
        in_specs=[pl.BlockSpec(memory_space=pltpu.SMEM), vmem, vmem, vmem]
        + [pl.BlockSpec(memory_space=pl.ANY)] * (4 + len(gathered))
        + [vmem] * len(earlier),
        out_specs=whole_spec(shape),
        scratch_shapes=scratch,
        compiler_params=pltpu.CompilerParams(vmem_limit_bytes=VMEM_LIMIT),
        cost_estimate=takes(0),
        name="mlp",
    )(place, x, gain[None], bias, *own, *gathered, *earlier)


def swap(x, axis, mask):
    count = lax.axis_size(axis)
    return lax.ppermute(x, axis, [(i, i ^ mask) for i in range(count)])


def selectors():
    row = np.arange(GROUP * 2 * LANES)[:, None]
    col = np.arange(SPAN * LANES)[None]
    within = row % (2 * LANES)
    sel = (within == (col // LANES) * CH_TOK + col % WIN) & (
        row // (2 * LANES) == col % LANES // WIN
    )
    row = np.arange(2 * LANES)[:, None]
    col = np.arange(SPAN * WIN)[None]
    sel1 = row == (col // WIN) * CH_TOK + col % WIN
    group = row // WIN == np.arange(LANES)[None] % SPAN
    return sel.astype(BF16), sel1.astype(BF16), group.astype(BF16)


def whole_spec(shape):
    return pl.BlockSpec(shape, lambda *_: (0,) * len(shape))


def spectral(place, near, far, tables, own, spec_out, nb, bands):
    bsize, zsize, some, _ = near.shape
    pixels = 2 * zsize * some
    width = spec_out.shape[0]
    lanes = (bands // SPAN + 1) * LANES
    args = [near, far, *selectors(), *tables, own, spec_out]
    part_px = pixels // GROUP
    return pl.pallas_call(
        functools.partial(spectral_kernel, nb, bands),
        out_shape=jax.ShapeDtypeStruct((nb, pixels, width), F32),
        in_specs=[pl.BlockSpec(memory_space=pltpu.SMEM)]
        + [pl.BlockSpec(memory_space=pltpu.VMEM)] * (len(args) - 1)
        + [pl.BlockSpec(memory_space=pl.ANY)],
        out_specs=pl.BlockSpec(memory_space=pltpu.VMEM),
        scratch_shapes=[
            pltpu.VMEM((pixels, lanes), BF16),
            pltpu.VMEM((LANES * (part_px + GAP), LANES), F32),
            pltpu.VMEM((HEADS * nb * (pixels + GAP), LANES), F32),
            pltpu.VMEM((HEADS * nb * (pixels + GAP), LANES), F32),
            pltpu.VMEM((pixels, LANES), F32),
            pltpu.VMEM(spec_out.shape, BF16),
            pltpu.SemaphoreType.DMA,
        ],
        compiler_params=pltpu.CompilerParams(vmem_limit_bytes=VMEM_LIMIT),
        cost_estimate=takes(26),
        name="spectral",
    )(place, *args)


def local(
    radiance,
    stem_weight,
    band_embed,
    norm_spectral,
    spec_qkv,
    spec_out,
    norm_spatial,
    spat_qkv,
    spat_out,
    norm_mlp,
    up_weight,
    up_bias,
    down_weight,
):
    bands, width = band_embed.shape
    bsize, psize = lax.axis_size("band"), lax.axis_size("pix")
    devices = bsize * psize
    nb = -(-bands // devices)
    band, pix = lax.axis_index("band"), lax.axis_index("pix")
    base = jnp.minimum((pix * bsize + band) * nb, bands - nb).astype(jnp.int32)

    rows, channels = radiance.shape
    message = jnp.concatenate([radiance.astype(BF16), up_bias.reshape(rows, -1)], axis=1)
    own = lax.dynamic_slice_in_dim(band_embed, base, nb, 0)
    features = make_features(stem_weight, band_embed, own, norm_spectral)

    half = up_weight.shape[0] // bsize // 2
    share = []
    for h in range(2):
        at = (band * 2 + h) * half
        share.append(
            jnp.concatenate(
                [lax.dynamic_slice_in_dim(w, at, half, 0) for w in (up_weight, down_weight)]
            )
        )
    share = jnp.concatenate(share)

    def ring(x, step):
        return lax.ppermute(x, "pix", [(i, (i + 2 * step) % psize) for i in range(psize)])


    relayed = bsize == 4
    straight = (1, 2) if relayed else tuple(range(1, bsize))

    def relay(got, count):
        out = []
        for h, m in enumerate((2, 1)):
            part = [x.reshape(-1, 2, 2 * half, width)[:, h] for x in got[m]]
            part = jnp.concatenate(part).reshape(count * 2 * half, width)
            out.append(swap(part, "band", 3 - m))
        return out

    zs = jnp.stack([message] + [swap(message, "pix", 2 * k) for k in range(1, psize // 2)])
    share, features = lax.optimization_barrier((share, features))
    shares = [ring(share, 1)]
    place = jnp.stack([base, band, pix // 2, pix % 2]).astype(jnp.int32)
    zs, features, place = lax.optimization_barrier((zs, features, place))
    near = jnp.stack([zs] + [swap(zs, "band", k) for k in range(1, bsize)])
    tables = make_tables(bands, features[0], spec_qkv) + features[1:]
    near, tables, shares, share, up_weight, down_weight = lax.optimization_barrier(
        (near, tables, shares, share, up_weight, down_weight)
    )
    far = swap(near, "pix", 1)
    first = {m: swap(shares[0], "band", m) for m in straight}
    while len(shares) < psize // 2 - 2:
        shares.append(ring(shares[-1], 1))
    shares.append(ring(share, -1))
    after_spectral = spectral(place, near, far, tables, own, spec_out, nb, bands)
    after_spectral, shares, first, up_weight, down_weight = lax.optimization_barrier(
        (after_spectral, shares, first, up_weight, down_weight)
    )
    own_weights = [up_weight, down_weight, swap(up_weight, "pix", 1), swap(down_weight, "pix", 1)]
    later = jnp.concatenate(shares[1:])
    rest = {m: swap(later, "band", m) for m in straight}
    bias = jnp.stack([near[0, :, :, channels:], far[0, :, :, channels:]])
    bias = bias.reshape(2, psize // 2, 2 * bsize, 1, half).astype(F32)
    pixels = after_spectral.shape[1]
    each = pixels // devices
    count = nb // 2 if nb % 2 == 0 and direct(pixels, devices, nb // 2) else nb
    arrived, results = [], []
    for start in range(0, nb, count):
        part = spatial(after_spectral, norm_spatial, spat_qkv, spat_out, start, count, devices)
        if start == 0:
            part, after_spectral, own_weights = lax.optimization_barrier(
                (part, after_spectral, own_weights)
            )
            held = [shares[0], later] + [x[m] for m in straight for x in (first, rest)]
            last_hop = []
            first, rest = lax.optimization_barrier((first, rest))
            if relayed:
                last_hop = relay({m: (first[m], rest[m]) for m in straight}, psize // 2 - 1)
            held_far = [swap(x, "pix", 1) for x in held]
        else:
            part, arrived, held_far, last_hop = lax.optimization_barrier(
                (part, arrived, held_far, last_hop)
            )
        if direct(pixels, devices, count):
            moved = lax.all_to_all(part, ("pix", "band"), split_axis=0, concat_axis=0, tiled=True)
        else:
            moved = lax.all_to_all(part, ("pix", "band"), split_axis=1, concat_axis=0, tiled=True)
        arrived.append(moved.reshape(-1, width))
    last_hop, _ = lax.optimization_barrier((last_hop, part))
    gathered = [*held, *held_far, *last_hop, *[swap(x, "pix", 1) for x in last_hop]]
    one, more = ((1,), tuple(range(2, psize // 2)))
    ids = [
        tuple((k, m, h) for k in some for h in range(2)) for m in (0, *straight) for some in (one, more)
    ]
    hop_ids = [tuple((k, 3, h) for k in one + more) for h in range(len(last_hop))]
    contents = tuple((c, x) for part in (ids, hop_ids) for c in range(2) for x in part)
    run = count * each
    for i, moved in enumerate(arrived):
        last = i == len(arrived) - 1
        results.append(
            mlp(
                place,
                moved,
                bands // nb * run,
                norm_mlp,
                bias,
                own_weights,
                gathered,
                contents,
                results if last else [],
                run,
                (each, bands, width) if last else None,
            )
        )
    return results[-1]


def solution(mesh):
    placed = (
        P("pix", "band"),
        P(),
        P(),
        P(),
        P(),
        P(),
        P(),
        P(),
        P(),
        P(),
        P("pix", None),
        P("pix"),
        P("pix", None),
    )
    return jax.shard_map(
        local, mesh=mesh, in_specs=placed, out_specs=P(("pix", "band"), None, None), check_vma=False
    )
```
